32 devices in a mesh: head: 4 (over y, core), inner: 4 (over z), outer: 2 (over x).
Axes of the slice: x: 2, y: 2, z: 4, core: 2. Of those that a mesh axis runs over, the one named last changes fastest.
Arguments:
- queries: bfloat16 [4096, 8192], P(('inner', 'outer', 'head')), may hold values from -12.816310409006173 to 12.816310409006173
- keys: bfloat16 [4096, 1024], P(('inner', 'outer', 'head')), may hold values from -4 to 4
- values: bfloat16 [4096, 1024], P(('inner', 'outer', 'head')), may hold values from -6 to 6
- dout: bfloat16 [4096, 8192], P(('inner', 'outer', 'head')), may hold values from -6 to 6
- doc_lengths: int32 [32], replicated, may hold values from 1 to 256, 4096 in all
- span_order: int32 [16], replicated, may hold values from 0 to 15, as said below
Outputs:
- attended: bfloat16 [4096, 8192], P(('inner', 'outer', 'head'))
- entropy: float32 [4096, 64], P(('inner', 'outer'), 'head')
- grad_query: bfloat16 [4096, 8192], P(('inner', 'outer', 'head'))
- grad_key: bfloat16 [4096, 1024], P(('inner', 'outer', 'head'))
- grad_value: bfloat16 [4096, 1024], P(('inner', 'outer', 'head'))
The draws below stay inside these ranges and needn't reach their ends.
Inputs may be any that keep to these rules, and one draw needn't show every extreme that they name: `doc_lengths`: the 32 documents lie one after another over the 4096 positions of the sequence; the lengths sum to 4096 and the longest is exactly 256. Stored rows b * 256 to (b + 1) * 256 - 1 hold the sequence positions span_order[b] * 256 onward, in order; stored blocks 2 i and 2 i + 1 hold the spans i and 15 - i, in either order.
All inputs are finite; a program needn't handle non-finite values.
Results may differ from the reference program's by a relative error of at most 0.03.
Values may be sent and summed in bfloat16 or wider, within the bound.
No kernel may reach another device: no remote copies, remote signals or barrier semaphores. Data moves between devices by JAX's collectives and lax.ppermute only.
A program may use at most 128 MiB of HBM per device.

```python
import math
import jax
import jax.numpy as jnp
import numpy as np
from jax import lax

QUERY_HEADS = 64
KEY_VALUE_HEADS = 8
HEAD_WIDTH = 128
SPAN_TOKENS = 256
NCHUNK = 16
SEQUENCE_TOKENS = 4096
DOC_MAX = 256
NDOC = 32


def draw_keys(key, part):
    sampled_values = jnp.clip(jax.random.normal(jax.random.fold_in(key, 11), (SEQUENCE_TOKENS, KEY_VALUE_HEADS * HEAD_WIDTH), jnp.float32), -4.0, 4.0)
    return sampled_values.astype(jnp.bfloat16)


def draw_queries(key, part):
    sampled_values = jnp.clip(jax.random.normal(jax.random.fold_in(key, 12), (SEQUENCE_TOKENS, QUERY_HEADS * HEAD_WIDTH), jnp.float32), -4.0, 4.0)
    return sampled_values.astype(jnp.bfloat16)


def draw_span_order(key, part):
    half_count = NCHUNK // 2
    swaps = jax.random.randint(jax.random.fold_in(key, 21), (half_count,), 0, 2)
    device_ids = jnp.arange(half_count, dtype=jnp.int32)
    lower_ids = device_ids
    upper_ids = NCHUNK - 1 - device_ids
    first_ids = jnp.where(swaps == 0, lower_ids, upper_ids)
    second_ids = jnp.where(swaps == 0, upper_ids, lower_ids)
    return jnp.stack([first_ids, second_ids], axis=1).reshape(NCHUNK).astype(jnp.int32)


def block_scale(stream_key, shape, shards, smallest, high):
    def one(dim, blocks):
        draws = jax.random.uniform(jax.random.fold_in(jax.random.fold_in(stream_key, 6), dim), (blocks,), jnp.float32, smallest / len(shards), high / len(shards))
        return jnp.repeat(jnp.exp(draws), shape[dim] // blocks).reshape((-1,) + (1,) * (len(shape) - dim - 1))

    factor_of = one(*shards[0])
    for cut in shards[1:]:
        factor_of = factor_of * one(*cut)
    return factor_of


def profile(count, total, most, skew):
    portions = [(1 << 20) // math.isqrt(standing ** skew) + 1 for standing in range(2, count + 1)]
    spare, given = total - most - (count - 1), [1] * (count - 1)
    while spare > 0:
        movable = [i for i in range(count - 1) if given[i] < most]
        whole, budget = sum([portions[i] for i in movable]), spare
        for i in movable:
            more = min(most - given[i], max(1, budget * portions[i] // whole), spare)
            given[i] = given[i] + more
            spare = spare - more
    return np.array([most] + given)


def uneven_parts(own_key, amount, total, limit, lean):
    if amount == 2:
        one = jax.random.randint(own_key, (), max(1, total - limit), min(limit, total - 1) + 1)
        return jnp.stack([one, total - one])
    tallies = jnp.asarray(profile(amount, total, limit, lean), jnp.int32)
    twos = (amount - 1) // 2
    donor, taker = tallies[1:1 + 2 * twos:2], tallies[2:2 + 2 * twos:2]
    room = jnp.minimum(donor - 1, limit - taker)
    shifted = jax.random.randint(jax.random.fold_in(own_key, 1), (twos,), 0, 1 << 20) % (room + 1)
    tallies = tallies.at[1:1 + 2 * twos:2].set(donor - shifted).at[2:2 + 2 * twos:2].set(taker + shifted)
    return tallies[jax.random.permutation(jax.random.fold_in(own_key, 2), amount)]


def scatter_about(key, dims, width, reach, cuts=(), kind=jnp.bfloat16):
    drawn = jax.random.normal(key, dims, jnp.float32) * width
    if len(cuts) > 0:
        drawn = block_scale(key, dims, cuts, -0.22, 0.18) * drawn
    return jnp.clip(drawn, min=-reach, max=reach).astype(kind)


def setup_inputs(seed: int = 0) -> dict:
    key_list = jax.random.split(jax.random.key(seed), 7)
    queries = draw_queries(jax.random.fold_in(key_list[6], 71), 0)
    keys = draw_keys(jax.random.fold_in(key_list[6], 71), 0)
    values = scatter_about(key_list[2], (SEQUENCE_TOKENS, KEY_VALUE_HEADS * HEAD_WIDTH), 1.0, 6.0, ((0, 32),))
    dout = scatter_about(key_list[3], (SEQUENCE_TOKENS, QUERY_HEADS * HEAD_WIDTH), 1.0, 6.0, ((0, 32),))
    doc_lengths = uneven_parts(key_list[4], NDOC, SEQUENCE_TOKENS, DOC_MAX, 2).astype(jnp.int32)
    span_order = draw_span_order(jax.random.fold_in(key_list[6], 71), 0)
    return dict(queries=queries, keys=keys, values=values, dout=dout, doc_lengths=doc_lengths, span_order=span_order)


def doc_index(positions, doc_lengths):
    starts = jnp.cumsum(doc_lengths) - doc_lengths
    return lax.optimization_barrier(jnp.sum((starts[None, :] <= positions[:, None]).astype(jnp.int32), axis=1)) - 1

def reference(queries, keys, values, dout, doc_lengths, span_order):
    heads_per_group = QUERY_HEADS // KEY_VALUE_HEADS
    doc_reach = (DOC_MAX - 1) // SPAN_TOKENS + 1
    tolerance_gap = doc_reach * SPAN_TOKENS
    visible_window = tolerance_gap + SPAN_TOKENS
    blocks = jnp.arange(NCHUNK, dtype=jnp.int32)
    inverse = jnp.zeros((NCHUNK,), jnp.int32).at[span_order].set(blocks)

    def to_sequence(source):
        return source.reshape(NCHUNK, SPAN_TOKENS, source.shape[1])[inverse].reshape(SEQUENCE_TOKENS, source.shape[1])

    def to_stored(source):
        return source.reshape(NCHUNK, SPAN_TOKENS, source.shape[1])[span_order].reshape(SEQUENCE_TOKENS, source.shape[1])
    sequence_queries = to_sequence(queries)
    sequence_keys = jnp.pad(to_sequence(keys), ((tolerance_gap, 0), (0, 0)))
    sequence_values = jnp.pad(to_sequence(values), ((tolerance_gap, 0), (0, 0)))
    sequence_output_gradient = to_sequence(dout)
    positions = jnp.arange(SEQUENCE_TOKENS + tolerance_gap, dtype=jnp.int32) - tolerance_gap
    documents = jnp.where(positions >= 0, doc_index(positions, doc_lengths), -1)

    def one_span(state_now, span_index):
        grad_keys, grad_values = state_now
        leading_row = (span_index * SPAN_TOKENS).astype(jnp.int32)
        query_matrix_rows = lax.dynamic_slice_in_dim(sequence_queries, leading_row, SPAN_TOKENS, 0).astype(jnp.float32).reshape(SPAN_TOKENS, KEY_VALUE_HEADS, heads_per_group, HEAD_WIDTH)
        output_gradient_rows = lax.dynamic_slice_in_dim(sequence_output_gradient, leading_row, SPAN_TOKENS, 0).astype(jnp.float32).reshape(SPAN_TOKENS, KEY_VALUE_HEADS, heads_per_group, HEAD_WIDTH)
        key_matrix_rows = lax.dynamic_slice_in_dim(sequence_keys, leading_row, visible_window, 0).astype(jnp.float32).reshape(visible_window, KEY_VALUE_HEADS, HEAD_WIDTH)
        value_matrix_rows = lax.dynamic_slice_in_dim(sequence_values, leading_row, visible_window, 0).astype(jnp.float32).reshape(visible_window, KEY_VALUE_HEADS, HEAD_WIDTH)
        q_pos = lax.dynamic_slice_in_dim(positions, leading_row + tolerance_gap, SPAN_TOKENS, 0)
        q_doc = lax.dynamic_slice_in_dim(documents, leading_row + tolerance_gap, SPAN_TOKENS, 0)
        k_pos = lax.dynamic_slice_in_dim(positions, leading_row, visible_window, 0)
        k_doc = lax.dynamic_slice_in_dim(documents, leading_row, visible_window, 0)
        allowed = (q_doc[:, None] == k_doc[None, :]) & (k_pos[None, :] <= q_pos[:, None])
        scores = jnp.einsum('qhgd,thd->hgqt', query_matrix_rows, key_matrix_rows) / math.sqrt(HEAD_WIDTH)
        scores = jnp.where(allowed, scores, -jnp.inf)
        row_top = lax.optimization_barrier(jnp.max(scores, axis=-1))
        lse = row_top + jnp.log(lax.optimization_barrier(jnp.sum(jnp.exp(scores - row_top[..., None]), axis=-1)))
        probs = jnp.exp(scores - lse[..., None])
        rounded_result = lax.optimization_barrier(probs.astype(jnp.bfloat16)).astype(jnp.float32)
        out_rows = jnp.einsum('hgqt,thd->qhgd', rounded_result, value_matrix_rows).astype(jnp.bfloat16)
        entropy = lse - lax.optimization_barrier(jnp.sum(jnp.where(allowed, probs * scores, 0.0), axis=-1))
        delta = jnp.transpose(lax.optimization_barrier(jnp.sum(output_gradient_rows * out_rows.astype(jnp.float32), axis=-1)), (1, 2, 0))
        dprobs = jnp.einsum('qhgd,thd->hgqt', output_gradient_rows, value_matrix_rows)
        score_gradient = probs * (dprobs - delta[..., None]) / math.sqrt(HEAD_WIDTH)
        score_gradient = lax.optimization_barrier(score_gradient.astype(jnp.bfloat16)).astype(jnp.float32)
        dquery = jnp.einsum('hgqt,thd->qhgd', score_gradient, key_matrix_rows).astype(jnp.bfloat16)
        key_gradient = jnp.einsum('ysfj,fysm->jym', score_gradient, query_matrix_rows).reshape(visible_window, KEY_VALUE_HEADS * HEAD_WIDTH)
        value_gradient = jnp.einsum('ysfj,fysm->jym', rounded_result, output_gradient_rows).reshape(visible_window, KEY_VALUE_HEADS * HEAD_WIDTH)
        grad_keys = lax.dynamic_update_slice_in_dim(grad_keys, lax.dynamic_slice_in_dim(grad_keys, leading_row, visible_window, 0) + key_gradient, leading_row, 0)
        grad_values = lax.dynamic_update_slice_in_dim(grad_values, lax.dynamic_slice_in_dim(grad_values, leading_row, visible_window, 0) + value_gradient, leading_row, 0)
        produced = (out_rows.reshape(SPAN_TOKENS, QUERY_HEADS * HEAD_WIDTH), jnp.transpose(entropy, (2, 0, 1)).reshape(SPAN_TOKENS, QUERY_HEADS), dquery.reshape(SPAN_TOKENS, QUERY_HEADS * HEAD_WIDTH))
        return ((grad_keys, grad_values), produced)
    blank_gradients = jnp.zeros((SEQUENCE_TOKENS + tolerance_gap, KEY_VALUE_HEADS * HEAD_WIDTH), jnp.float32)
    (grad_keys, grad_values), (outs, entropies, dqueries) = lax.scan(one_span, (blank_gradients, blank_gradients), blocks)
    attended = to_stored(outs.reshape(SEQUENCE_TOKENS, QUERY_HEADS * HEAD_WIDTH))
    entropy = to_stored(entropies.reshape(SEQUENCE_TOKENS, QUERY_HEADS))
    grad_query = to_stored(dqueries.reshape(SEQUENCE_TOKENS, QUERY_HEADS * HEAD_WIDTH))
    grad_key = to_stored(grad_keys[tolerance_gap:].astype(jnp.bfloat16))
    grad_value = to_stored(grad_values[tolerance_gap:].astype(jnp.bfloat16))
    return (attended, entropy, grad_query, grad_key, grad_value)
```

```python
import functools
import math

import jax
import jax.numpy as jnp
from jax import lax
from jax.experimental import pallas as pl
from jax.experimental.pallas import tpu as pltpu
from jax.sharding import PartitionSpec as P

QUERY_HEADS = 64
KEY_VALUE_HEADS = 8
HEAD_WIDTH = 128
GROUP = QUERY_HEADS // KEY_VALUE_HEADS
SCALE = 1.0 / math.sqrt(HEAD_WIDTH)
MASKED = -1e30
CONTEXT = ("inner", "outer")
CHUNKS = 1
NT = (((1,), (1,)), ((), ()))
NN = (((1,), (0,)), ((), ()))


def attention_kernel(units, doc_ref, first_ref, q_ref, do_ref, *refs):
    unit_refs = refs[:units]
    att_ref, dq_ref, ent_ref, own_ref = refs[units : units + 4]
    term_refs = refs[units + 4 : 2 * units + 3]
    bias_ref, pb_ref, ds_ref, qs_ref, dos_ref = refs[2 * units + 3 :]
    rows = q_ref.shape[0]
    window = units * rows
    g = pl.program_id(0)
    count = own_ref.shape[1] // (2 * HEAD_WIDTH)

    @pl.when(g == 0)
    def _():
        first = first_ref[0]
        q_pos = first + lax.broadcasted_iota(jnp.int32, (1, rows), 1)

        def step(index, carry):
            at, start = carry
            return at + doc_ref[index], jnp.where(at <= q_pos, at, start)

        _, start = lax.fori_loop(
            0, doc_ref.shape[0], step, (jnp.int32(0), jnp.zeros((1, rows), jnp.int32))
        )
        k_pos = first - (units - 1) * rows + lax.broadcasted_iota(jnp.int32, (window, rows), 0)
        bias_ref[...] = jnp.where((k_pos >= start) & (k_pos <= q_pos), 0.0, MASKED)

    half = count // 2
    base = (g // half) * count + g % half
    k_cols = pl.ds(pl.multiple_of(base * HEAD_WIDTH, HEAD_WIDTH), HEAD_WIDTH)
    v_cols = pl.ds(pl.multiple_of((base + half) * HEAD_WIDTH, HEAD_WIDTH), HEAD_WIDTH)
    k_rows = jnp.concatenate([unit[:, k_cols] for unit in unit_refs], axis=0)
    v_rows = jnp.concatenate([unit[:, v_cols] for unit in unit_refs], axis=0)
    heads = [slice(h * HEAD_WIDTH, (h + 1) * HEAD_WIDTH) for h in range(GROUP)]
    spots = [slice(h * rows, (h + 1) * rows) for h in range(GROUP)]
    for head, spot in zip(heads, spots):
        qs_ref[spot, :] = q_ref[:, head]
        dos_ref[spot, :] = do_ref[:, head]
    q_all = qs_ref[...]
    do_all = dos_ref[...]
    bias = jnp.concatenate([bias_ref[...]] * GROUP, axis=1)
    s = lax.dot_general(k_rows, q_all, NT, preferred_element_type=jnp.float32) + bias
    top = jnp.max(s, axis=0, keepdims=True)
    t = (s - top) * (SCALE * math.log2(math.e))
    e = jnp.exp2(t)
    total = jnp.sum(e, axis=0, keepdims=True)
    inv = 1.0 / total
    entropy = jnp.log(total) - jnp.sum(e * t, axis=0, keepdims=True) * inv * math.log(2.0)
    for h, spot in enumerate(spots):
        ent_ref[h : h + 1, :] = entropy[:, spot]
    p = e * inv
    pb = p.astype(jnp.bfloat16)
    pb_ref[...] = pb
    out = lax.dot_general(v_rows.T, pb, NN, preferred_element_type=jnp.float32)
    out = out.astype(jnp.bfloat16).T
    dp = lax.dot_general(v_rows, do_all, NT, preferred_element_type=jnp.float32)
    delta = jnp.sum(p * dp, axis=0, keepdims=True)
    ds = (p * (dp - delta)).astype(jnp.bfloat16)
    ds_ref[...] = ds
    dq = lax.dot_general(k_rows.T, ds, NN, preferred_element_type=jnp.float32)
    dq = (dq * SCALE).astype(jnp.bfloat16).T
    for head, spot in zip(heads, spots):
        att_ref[:, head] = out[spot, :]
        dq_ref[:, head] = dq[spot, :]
    dv = lax.dot_general(pb_ref[...], do_all, NN, preferred_element_type=jnp.float32)
    dk = lax.dot_general(ds_ref[...], q_all, NN, preferred_element_type=jnp.float32) * SCALE
    own_ref[:, k_cols] = dk[window - rows :]
    own_ref[:, v_cols] = dv[window - rows :]
    for index, term in enumerate(term_refs):
        part = slice(index * rows, (index + 1) * rows)
        term[:, k_cols] = dk[part].astype(jnp.bfloat16)
        term[:, v_cols] = dv[part].astype(jnp.bfloat16)


def attention(doc_lengths, first, queries, dout, unit_rows, chunk, earlier):
    rows = queries.shape[0]
    units = len(unit_rows)
    window = units * rows
    width = unit_rows[0].shape[1]
    count = width // (2 * HEAD_WIDTH)
    whole = pl.BlockSpec((rows, width), lambda g, *_: (0, 0))
    block = pl.BlockSpec((rows, GROUP * HEAD_WIDTH), lambda g, *_: (0, chunk * count + g))
    aliases = {4 + units: 0, 5 + units: 1} if earlier else {}

    def kernel(doc_ref, first_ref, q_ref, do_ref, *refs):
        kept = refs[:units] + refs[units + len(earlier) :]
        attention_kernel(units, doc_ref, first_ref, q_ref, do_ref, *kept)

    wide = jax.ShapeDtypeStruct(queries.shape, jnp.bfloat16)
    return pl.pallas_call(
        kernel,
        grid_spec=pltpu.PrefetchScalarGridSpec(
            num_scalar_prefetch=2,
            grid=(count,),
            in_specs=[block, block]
            + [whole] * units
            + [pl.BlockSpec(memory_space=pl.ANY)] * len(earlier),
            out_specs=[block, block, pl.BlockSpec((GROUP, rows), lambda g, *_: (g, 0))]
            + [whole] * units,
            scratch_shapes=[
                pltpu.VMEM((window, rows), jnp.float32),
                pltpu.VMEM((window, GROUP * rows), jnp.bfloat16),
                pltpu.VMEM((window, GROUP * rows), jnp.bfloat16),
                pltpu.VMEM((GROUP * rows, HEAD_WIDTH), jnp.bfloat16),
                pltpu.VMEM((GROUP * rows, HEAD_WIDTH), jnp.bfloat16),
            ],
        ),
        out_shape=[
            wide,
            wide,
            jax.ShapeDtypeStruct((count * GROUP, rows), jnp.float32),
            jax.ShapeDtypeStruct((rows, width), jnp.float32),
        ]
        + [jax.ShapeDtypeStruct((rows, width), jnp.bfloat16)] * (units - 1),
        input_output_aliases=aliases,
        compiler_params=pltpu.CompilerParams(vmem_limit_bytes=40 * 2**20),
        cost_estimate=pl.CostEstimate(
            flops=12 * count * window * GROUP * rows * HEAD_WIDTH,
            bytes_accessed=16 * count * GROUP * rows * HEAD_WIDTH,
            transcendentals=count * window * GROUP * rows,
        ),
    )(doc_lengths, first, queries, dout, *unit_rows, *earlier)


def along_context(value, steps):
    size = lax.axis_size(CONTEXT)
    low, high = max(0, -steps), min(size, size - steps)
    return lax.ppermute(value, CONTEXT, [(s, s + steps) for s in range(low, high)])


def body(queries, keys, values, dout, doc_lengths, span_order):
    rows = queries.shape[0]
    size = lax.axis_size("head")
    subs = size // 2
    here = lax.axis_index("head")
    side, sub = here // subs, here % subs
    context = lax.axis_index(CONTEXT)
    is_top = context == lax.axis_size(CONTEXT) - 1
    span = lax.dynamic_index_in_dim(span_order, 2 * context + side, keepdims=False)
    is_low = span == context
    first = ((span * subs + sub) * rows).reshape(1)
    across = [(j, (j + subs) % size) for j in range(size)]

    def around(value, steps):
        pairs = [(j, j // subs * subs + (j + steps) % subs) for j in range(size)]
        return lax.ppermute(value, "head", pairs)

    half_width = keys.shape[1] // (2 * CHUNKS)

    def packed(chunk):
        parts = []
        for half in range(2):
            cols = slice((2 * chunk + half) * half_width, (2 * chunk + half + 1) * half_width)
            parts += [keys[:, cols], values[:, cols]]
        return jnp.concatenate(parts, axis=1)

    def halves(value):
        left, right = jnp.split(value, 2, axis=1)
        return jnp.where(side == 0, left, right), jnp.where(side == 0, right, left)

    def joined(mine, other):
        return jnp.concatenate(
            [jnp.where(side == 0, mine, other), jnp.where(side == 0, other, mine)], axis=1
        )

    def swap_if(condition, one, two):
        return jnp.where(condition, one, two), jnp.where(condition, two, one)

    def earlier_span(own):
        keep, give = halves(own)
        got = lax.ppermute(give, "head", across)
        low, high = swap_if(is_low, keep, got)
        from_below = along_context(low, 1)
        from_above = jnp.where(is_top, low, along_context(high, -1))
        mine, theirs = swap_if(is_low, from_below, from_above)
        return joined(mine, lax.ppermute(theirs, "head", across))

    def key_window(own):
        before = earlier_span(own)
        near = [
            around(jnp.where(sub + steps < subs, own, before), steps)
            for steps in range(subs - 1, 0, -1)
        ]
        return [before] + near + [own]

    def returned(own, terms):
        before = terms[0].astype(jnp.float32)
        for index, steps in enumerate(range(subs - 1, 0, -1)):
            got = around(terms[index + 1], -steps).astype(jnp.float32)
            within = sub + steps < subs
            own = own + jnp.where(within, got, 0.0)
            before = before + jnp.where(within, 0.0, got)
        keep, give = halves(before.astype(jnp.bfloat16))
        got = lax.ppermute(give, "head", across)
        low, high = swap_if(is_low, keep, got)
        from_upper = jnp.where(is_top, high, along_context(low, -1))
        from_lower = along_context(high, 1)
        mine, theirs = swap_if(is_low, from_upper, from_lower)
        other = lax.ppermute(theirs, "head", across)
        return (own + joined(mine, other).astype(jnp.float32)).astype(jnp.bfloat16)

    windows = [key_window(packed(chunk)) for chunk in range(CHUNKS)]
    earlier = []
    entropies, grads = [], []
    for chunk, window in enumerate(windows):
        results = attention(doc_lengths, first, queries, dout, window, chunk, earlier)
        earlier = results[:2]
        entropies.append(results[2])
        grads.append(returned(results[3], results[4:]))
    attended, grad_query = earlier
    entropy = lax.all_to_all(
        jnp.concatenate(entropies, axis=0).T, "head", split_axis=1, concat_axis=0, tiled=True
    )
    grad_key, grad_value = [], []
    for grad in grads:
        parts = jnp.split(grad, 4, axis=1)
        grad_key += [parts[0], parts[2]]
        grad_value += [parts[1], parts[3]]
    return (
        attended,
        entropy,
        grad_query,
        jnp.concatenate(grad_key, axis=1),
        jnp.concatenate(grad_value, axis=1),
    )


def solution(mesh):
    rows = P(("inner", "outer", "head"), None)
    return jax.shard_map(
        body,
        mesh=mesh,
        in_specs=(rows, rows, rows, rows, P(), P()),
        out_specs=(rows, P(("inner", "outer"), "head"), rows, rows, rows),
        check_vma=False,
    )
```

```python
import math

import jax
import jax.numpy as jnp
from jax import lax
from jax.experimental import pallas as pl
from jax.experimental.pallas import tpu as pltpu
from jax.sharding import PartitionSpec as P

QUERY_HEADS = 64
KEY_VALUE_HEADS = 8
WIDTH = 128
GROUP = QUERY_HEADS // KEY_VALUE_HEADS
SCALE = 1.0 / math.sqrt(WIDTH)
MASKED = -1e30
CONTEXT = ("inner", "outer")
CHUNKS = 2
NT = (((1,), (1,)), ((), ()))
NN = (((1,), (0,)), ((), ()))


def dot(left, right, dims):
    return lax.dot_general(left, right, dims, preferred_element_type=jnp.float32)


def attention_kernel(near, doc_ref, first_ref, q_ref, do_ref, *refs):
    units = near + 2
    kv_refs, refs = refs[: 2 * units], refs[2 * units :]
    att_ref, dq_ref, ent_ref = refs[:3]
    term_refs, refs = refs[3 : 3 + 2 * units], refs[3 + 2 * units :]
    bias_ref, pb_ref, ds_ref, qs_ref, dos_ref = refs
    rows = q_ref.shape[0]
    window = units * rows
    heads = [slice(h * WIDTH, (h + 1) * WIDTH) for h in range(GROUP)]
    spots = [slice(h * rows, (h + 1) * rows) for h in range(GROUP)]

    @pl.when(pl.program_id(0) == 0)
    def _():
        first = first_ref[0]
        q_pos = first + lax.broadcasted_iota(jnp.int32, (1, rows), 1)

        def step(index, carry):
            at, start = carry
            return at + doc_ref[index], jnp.where(at <= q_pos, at, start)

        _, start = lax.fori_loop(
            0, doc_ref.shape[0], step, (jnp.int32(0), jnp.zeros((1, rows), jnp.int32))
        )
        k_pos = first - (units - 1) * rows + lax.broadcasted_iota(jnp.int32, (window, rows), 0)
        bias_ref[...] = jnp.where((k_pos >= start) & (k_pos <= q_pos), 0.0, MASKED)

    k_rows = jnp.concatenate([ref[...] for ref in kv_refs[:units]], axis=0)
    v_rows = jnp.concatenate([ref[...] for ref in kv_refs[units:]], axis=0)
    for head, spot in zip(heads, spots):
        qs_ref[spot, :] = q_ref[:, head]
        dos_ref[spot, :] = do_ref[:, head]
    scores = dot(k_rows, qs_ref[...], NT)
    dprobs = dot(v_rows, dos_ref[...], NT)
    for h in range(0, GROUP, 2):
        cols = slice(h * rows, (h + 2) * rows)
        s = scores[:, cols] + jnp.concatenate([bias_ref[...]] * 2, axis=1)
        t = (s - jnp.max(s, axis=0, keepdims=True)) * (SCALE * math.log2(math.e))
        e = jnp.exp2(t)
        total = jnp.sum(e, axis=0, keepdims=True)
        inv = 1.0 / total
        entropy = jnp.log(total) - jnp.sum(e * t, axis=0, keepdims=True) * inv * math.log(2.0)
        ent_ref[h : h + 1, :] = entropy[:, :rows]
        ent_ref[h + 1 : h + 2, :] = entropy[:, rows:]
        p = e * inv
        pb_ref[:, cols] = p.astype(jnp.bfloat16)
        dp = dprobs[:, cols]
        delta = jnp.sum(p * dp, axis=0, keepdims=True)
        ds_ref[:, cols] = (p * (dp - delta)).astype(jnp.bfloat16)
    out = dot(v_rows.T, pb_ref[...], NN).astype(jnp.bfloat16).T
    dq = (dot(k_rows.T, ds_ref[...], NN) * SCALE).astype(jnp.bfloat16).T
    for head, spot in zip(heads, spots):
        att_ref[:, head] = out[spot, :]
        dq_ref[:, head] = dq[spot, :]
    dv = dot(pb_ref[...], dos_ref[...], NN)
    dk = dot(ds_ref[...], qs_ref[...], NN) * SCALE
    for index in range(units):
        part = slice(index * rows, (index + 1) * rows)
        term_refs[index][...] = dk[part].astype(term_refs[index].dtype)
        term_refs[units + index][...] = dv[part].astype(term_refs[units + index].dtype)


def attention(doc_lengths, first, queries, dout, own, before, near, chunk, earlier):
    rows = queries.shape[0]
    units = len(near) + 2
    window = units * rows
    count = KEY_VALUE_HEADS // CHUNKS
    block = pl.BlockSpec((rows, GROUP * WIDTH), lambda g, *_: (0, chunk * count + g))
    of_own = pl.BlockSpec((rows, WIDTH), lambda g, *_: (0, chunk * count + g))
    left = pl.BlockSpec((rows, WIDTH), lambda g, *_: (0, g))
    right = pl.BlockSpec((rows, WIDTH), lambda g, *_: (0, count + g))
    keys = [before[0], *near, own[0]]
    values = [before[1], *near, own[1]]
    stay = pl.BlockSpec(memory_space=pl.ANY)

    def kernel(doc_ref, first_ref, q_ref, do_ref, *refs):
        kept = refs[: 2 * units] + refs[2 * units + len(earlier) :]
        attention_kernel(len(near), doc_ref, first_ref, q_ref, do_ref, *kept)

    wide = jax.ShapeDtypeStruct(queries.shape, jnp.bfloat16)
    narrow = [jax.ShapeDtypeStruct((rows, count * WIDTH), jnp.bfloat16)] * (units - 1)
    narrow.append(jax.ShapeDtypeStruct((rows, count * WIDTH), jnp.float32))
    results = pl.pallas_call(
        kernel,
        grid_spec=pltpu.PrefetchScalarGridSpec(
            num_scalar_prefetch=2,
            grid=(count,),
            in_specs=[block, block]
            + [left] * (units - 1)
            + [of_own, left]
            + [right] * len(near)
            + [of_own]
            + [stay] * len(earlier),
            out_specs=[block, block, pl.BlockSpec((GROUP, rows), lambda g, *_: (g, 0))]
            + [left] * (2 * units),
            scratch_shapes=[
                pltpu.VMEM((window, rows), jnp.float32),
                pltpu.VMEM((window, GROUP * rows), jnp.bfloat16),
                pltpu.VMEM((window, GROUP * rows), jnp.bfloat16),
                pltpu.VMEM((GROUP * rows, WIDTH), jnp.bfloat16),
                pltpu.VMEM((GROUP * rows, WIDTH), jnp.bfloat16),
            ],
        ),
        out_shape=[wide, wide, jax.ShapeDtypeStruct((count * GROUP, rows), jnp.float32)]
        + narrow * 2,
        input_output_aliases={4 + 2 * units: 0, 5 + 2 * units: 1} if earlier else {},
        compiler_params=pltpu.CompilerParams(vmem_limit_bytes=32 * 2**20),
        cost_estimate=pl.CostEstimate(
            flops=12 * count * window * GROUP * rows * WIDTH,
            bytes_accessed=16 * count * GROUP * rows * WIDTH,
            transcendentals=count * window * GROUP * rows,
        ),
    )(doc_lengths, first, queries, dout, *keys, *values, *earlier)
    terms = results[3:]
    return results[:2], results[2], terms[:units], terms[units:]


def body(queries, keys, values, dout, doc_lengths, span_order):
    rows = queries.shape[0]
    size = lax.axis_size("head")
    subs = size // 2
    here = lax.axis_index("head")
    side, sub = here // subs, here % subs
    contexts = lax.axis_size(CONTEXT)
    context = lax.axis_index(CONTEXT)
    is_top = context == contexts - 1
    span = lax.dynamic_index_in_dim(span_order, 2 * context + side, keepdims=False)
    is_low = span == context
    in_step = is_low == (context % 2 == 0)
    first = ((span * subs + sub) * rows).reshape(1)
    width = keys.shape[1] // CHUNKS

    def across(value):
        return lax.ppermute(value, "head", [(j, (j + subs) % size) for j in range(size)])

    def around(value, steps):
        pairs = [(j, j // subs * subs + (j + steps) % subs) for j in range(size)]
        return lax.ppermute(value, "head", pairs)

    def edges(value, start):
        pairs = [(c, c + 1) for c in range(start, contexts - 1, 2)]
        return lax.ppermute(value, CONTEXT, pairs + [(b, a) for a, b in pairs])

    def choose(condition, one, two):
        return jnp.where(condition, one, two), jnp.where(condition, two, one)

    def moved(key_part, value_part, backward):
        keep, give = choose(side == 0, key_part, value_part)
        got = across(give)
        upward = is_low != backward
        even_out, odd_out = choose(upward == (context % 2 == 0), keep, got)
        even_in = edges(even_out, 0)
        odd_in = jnp.where(is_top, choose(is_low != backward, keep, got)[0], edges(odd_out, 1))
        mine, theirs = choose(in_step, *((even_in, odd_in) if backward else (odd_in, even_in)))
        return choose(side == 0, mine, across(theirs))

    def key_window(chunk):
        cols = slice(chunk * width, (chunk + 1) * width)
        before = moved(keys[:, cols], values[:, cols], False)
        own_both = jnp.concatenate([keys[:, cols], values[:, cols]], axis=1)
        before_both = jnp.concatenate(before, axis=1)
        near = [
            around(jnp.where(sub + steps < subs, own_both, before_both), steps)
            for steps in range(subs - 1, 0, -1)
        ]
        return before, near

    def returned(dk, dv):
        own = [dk[-1], dv[-1]]
        before = [dk[0].astype(jnp.float32), dv[0].astype(jnp.float32)]
        for index, steps in enumerate(range(subs - 1, 0, -1)):
            got = around(jnp.concatenate([dk[index + 1], dv[index + 1]], axis=1), -steps)
            within = sub + steps < subs
            for which, part in enumerate(jnp.split(got.astype(jnp.float32), 2, axis=1)):
                own[which] = own[which] + jnp.where(within, part, 0.0)
                before[which] = before[which] + jnp.where(within, 0.0, part)
        back = moved(before[0].astype(jnp.bfloat16), before[1].astype(jnp.bfloat16), True)
        return [
            (mine + theirs.astype(jnp.float32)).astype(jnp.bfloat16)
            for mine, theirs in zip(own, back)
        ]

    windows = [key_window(chunk) for chunk in range(CHUNKS)]
    wide = []
    entropies, grads = [], []
    for chunk, window in enumerate(windows):
        wide, entropy, dk, dv = attention(
            doc_lengths, first, queries, dout, (keys, values), *window, chunk, wide
        )
        entropies.append(entropy)
        grads.append(returned(dk, dv))
    attended, grad_query = wide
    entropy = lax.all_to_all(
        jnp.concatenate(entropies, axis=0).T, "head", split_axis=1, concat_axis=0, tiled=True
    )
    grad_key, grad_value = [jnp.concatenate(parts, axis=1) for parts in zip(*grads)]
    return attended, entropy, grad_query, grad_key, grad_value


def solution(mesh):
    rows = P(("inner", "outer", "head"), None)
    return jax.shard_map(
        body,
        mesh=mesh,
        in_specs=(rows, rows, rows, rows, P(), P()),
        out_specs=(rows, P(("inner", "outer"), "head"), rows, rows, rows),
        check_vma=False,
    )
```

```python
import functools
import math

import jax
import jax.numpy as jnp
from jax import lax
from jax.experimental import pallas as pl
from jax.experimental.pallas import tpu as pltpu
from jax.sharding import PartitionSpec as P

QUERY_HEADS = 64
KEY_VALUE_HEADS = 8
WIDTH = 128
GROUP = QUERY_HEADS // KEY_VALUE_HEADS
SCALE = 1.0 / math.sqrt(WIDTH)
MASKED = -1e30
CONTEXT = ("inner", "outer")
CHUNKS = 1
UNROLL = 2
EXTRA = 16
BEHIND = (2, 4, 2)
LOG2E = math.log2(math.e)
VMEM_SMALL = 8 * 2**20
VMEM_LARGE = 16 * 2**20
NT = (((1,), (1,)), ((), ()))
NN = (((1,), (0,)), ((), ()))


def dot(left, right, dims):
    return lax.dot_general(left, right, dims, preferred_element_type=jnp.float32)


def lanes(index, width=WIDTH):
    if isinstance(index, int):
        return slice(index * width, (index + 1) * width)
    return pl.ds(pl.multiple_of(index * width, WIDTH), width)


def group_rows(ref, g):
    return jnp.concatenate([ref[:, lanes(g * GROUP + h)] for h in range(GROUP)], axis=0)


def tiled(bias):
    return jnp.concatenate([bias] * GROUP, axis=1)


def own_kernel(bias_ref, *refs):
    sources, refs = refs[:4], refs[4:]
    loaded, (stat_ref, sems) = refs[:4], refs[4:]
    q_ref, do_ref, k_ref, v_ref = loaded
    rows = q_ref.shape[0]
    last = bias_ref.shape[0] - rows
    heads = k_ref.shape[1] // WIDTH
    narrow = [pltpu.make_async_copy(sources[i], loaded[i], sems.at[i, 0]) for i in (2, 3)]

    def wide(g):
        cols = lanes(g, GROUP * WIDTH)
        return [
            pltpu.make_async_copy(sources[i].at[:, cols], loaded[i].at[:, cols], sems.at[i, g])
            for i in (0, 1)
        ]

    copies = narrow + [copy for g in range(heads) for copy in wide(g)]
    for copy in copies:
        copy.start()
    for copy in narrow:
        copy.wait()

    def step(g, _):
        for copy in wide(g):
            copy.wait()
        s = dot(k_ref[:, lanes(g)], group_rows(q_ref, g), NT) + tiled(bias_ref[last:, :])
        dp = dot(v_ref[:, lanes(g)], group_rows(do_ref, g), NT)
        top = jnp.max(s, axis=0, keepdims=True)
        t = (s - top) * (SCALE * LOG2E)
        e = jnp.exp2(t)
        stat_ref[g, 0:1, :] = top
        stat_ref[g, 1:2, :] = jnp.sum(e, axis=0, keepdims=True)
        stat_ref[g, 2:3, :] = jnp.sum(e * t, axis=0, keepdims=True)
        stat_ref[g, 3:4, :] = jnp.sum(e * dp, axis=0, keepdims=True)
        return 0

    lax.fori_loop(0, heads, step, 0)


def earlier_kernel(start, count, near, q_ref, do_ref, bias_ref, first_k, first_v, *refs):
    near_refs, (stat_ref, *refs) = refs[:near], refs[near:]
    ent_ref, row_ref, p_ref, ds_ref = refs[:4]
    dk_refs, dv_refs = refs[4 : 5 + near], refs[5 + near :]
    rows = q_ref.shape[0]
    width = first_k.shape[1] // WIDTH
    window = (near + 1) * rows

    def head(at, _):
        g = start + at
        k_rows = jnp.concatenate(
            [first_k[:, lanes(at)], *[ref[:, lanes(at)] for ref in near_refs]], axis=0
        )
        v_rows = jnp.concatenate(
            [first_v[:, lanes(at)], *[ref[:, lanes(at + width)] for ref in near_refs]], axis=0
        )
        q_all, do_all = group_rows(q_ref, g), group_rows(do_ref, g)
        s = dot(k_rows, q_all, NT) + tiled(bias_ref[:window, :])
        dp = dot(v_rows, do_all, NT)
        own_top, own_total = stat_ref[g, 0:1, :], stat_ref[g, 1:2, :]
        top = jnp.maximum(jnp.max(s, axis=0, keepdims=True), own_top)
        t = (s - top) * (SCALE * LOG2E)
        e = jnp.exp2(t)
        shift = (own_top - top) * (SCALE * LOG2E)
        ratio = jnp.exp2(shift)
        total = own_total * ratio + jnp.sum(e, axis=0, keepdims=True)
        inv = 1.0 / total
        spread = (stat_ref[g, 2:3, :] + shift * own_total) * ratio
        spread = spread + jnp.sum(e * t, axis=0, keepdims=True)
        entropy = jnp.log(total) - spread * inv * math.log(2.0)
        for h in range(GROUP):
            ent_ref[at, h : h + 1, :] = entropy[:, h * rows : (h + 1) * rows]
        delta = stat_ref[g, 3:4, :] * ratio + jnp.sum(e * dp, axis=0, keepdims=True)
        delta = delta * inv
        row_ref[at, 0:1, :] = top * (SCALE * LOG2E) + jnp.log2(total)
        row_ref[at, 1:2, :] = delta
        p = e * inv
        pb = p.astype(jnp.bfloat16)
        ds = (p * (dp - delta)).astype(jnp.bfloat16)
        p_ref[at] = pb
        ds_ref[at] = ds
        dv = dot(pb, do_all, NN)
        dk = dot(ds, q_all, NN) * SCALE
        for unit in range(near + 1):
            part = slice(unit * rows, (unit + 1) * rows)
            dk_refs[unit][:, lanes(at)] = dk[part].astype(jnp.bfloat16)
            dv_refs[unit][:, lanes(at)] = dv[part].astype(jnp.bfloat16)

        return 0

    lax.fori_loop(0, count, head, 0, unroll=UNROLL)


def rest_kernel(start, skip, near, q_ref, do_ref, bias_ref, first_k, first_v, *refs):
    near_refs, (own_k, own_v), refs = refs[:near], refs[near : near + 2], refs[near + 2 :]
    row_ref, p_ref, ds_ref, att_ref, dq_ref, dk_ref, dv_ref = refs
    rows = q_ref.shape[0]
    width = first_k.shape[1] // WIDTH
    last = bias_ref.shape[0] - rows
    index = pl.program_id(0)
    at, g = skip + index, start + skip + index
    own_keys, own_values = own_k[:, lanes(g)], own_v[:, lanes(g)]
    k_rows = jnp.concatenate(
        [first_k[:, lanes(at)], *[ref[:, lanes(at)] for ref in near_refs], own_keys], axis=0
    )
    v_rows = jnp.concatenate(
        [first_v[:, lanes(at)], *[ref[:, lanes(at + width)] for ref in near_refs], own_values],
        axis=0,
    )
    q_all, do_all = group_rows(q_ref, g), group_rows(do_ref, g)
    s = dot(own_keys, q_all, NT) + tiled(bias_ref[last:, :])
    dp = dot(own_values, do_all, NT)
    p = jnp.exp2(s * (SCALE * LOG2E) - row_ref[at, 0:1, :])
    pb = p.astype(jnp.bfloat16)
    ds = (p * (dp - row_ref[at, 1:2, :])).astype(jnp.bfloat16)
    dv_ref[:, lanes(index)] = dot(pb, do_all, NN)
    dk_ref[:, lanes(index)] = dot(ds, q_all, NN) * SCALE
    p_all = jnp.concatenate([p_ref[at], pb], axis=0)
    ds_all = jnp.concatenate([ds_ref[at], ds], axis=0)
    out = dot(v_rows.T, p_all, NN).astype(jnp.bfloat16).T
    dq = (dot(k_rows.T, ds_all, NN) * SCALE).astype(jnp.bfloat16).T
    for h in range(GROUP):
        spot = slice(h * rows, (h + 1) * rows)
        att_ref[:, lanes(h)] = out[spot, :]
        dq_ref[:, lanes(h)] = dq[spot, :]


def whole(count, space=pltpu.VMEM):
    return [pl.BlockSpec(memory_space=space)] * count


def near_by(value):
    return pltpu.with_memory_space_constraint(value, pltpu.VMEM)


def in_scalars(value):
    return pltpu.with_memory_space_constraint(value, pltpu.SMEM)


def small(kernel, flags, inputs, outs, behind=()):
    def body(*refs):
        kernel(*refs[: 1 + len(inputs)], *refs[1 + len(inputs) + len(behind) :])

    return pl.pallas_call(
        body,
        in_specs=whole(1, pltpu.SMEM) + whole(len(inputs)) + whole(len(behind), pl.ANY),
        out_specs=whole(len(outs)),
        out_shape=[pltpu.VMEM(shape, dtype) for shape, dtype in outs],
        compiler_params=pltpu.CompilerParams(vmem_limit_bytes=VMEM_SMALL),
    )(in_scalars(flags), *[near_by(value) for value in inputs], *behind)


def cost(count, rows, products):
    return pl.CostEstimate(
        flops=16 * products * count * rows * GROUP * rows * WIDTH,
        bytes_accessed=1,
        transcendentals=0,
    )


def large(kernel, inputs, outs, price, behind=()):
    def body(*refs):
        kernel(*refs[: len(inputs)], *refs[len(inputs) + len(behind) :])

    return pl.pallas_call(
        body,
        in_specs=whole(len(inputs)) + whole(len(behind), pl.ANY),
        out_specs=whole(len(outs)),
        out_shape=[pltpu.VMEM(shape, dtype) for shape, dtype in outs],
        compiler_params=pltpu.CompilerParams(vmem_limit_bytes=VMEM_LARGE),
        cost_estimate=price,
    )(*[near_by(value) for value in inputs], *behind)


def far(value):
    return pltpu.with_memory_space_constraint(value, pltpu.HBM)


def own_sums(bias, *arrays):
    rows = arrays[0].shape[0]
    heads = arrays[2].shape[1] // WIDTH
    return pl.pallas_call(
        own_kernel,
        in_specs=whole(1) + whole(4, pl.ANY),
        out_specs=whole(5),
        out_shape=[pltpu.VMEM(array.shape, array.dtype) for array in arrays]
        + [pltpu.VMEM((heads, 8, GROUP * rows), jnp.float32)],
        scratch_shapes=[pltpu.SemaphoreType.DMA((4, heads))],
        compiler_params=pltpu.CompilerParams(vmem_limit_bytes=VMEM_LARGE),
        cost_estimate=cost(heads, rows, 2),
    )(near_by(bias), *[far(array) for array in arrays])


def earlier_terms(queries, dout, bias, before, near, stats, start, behind=()):
    rows = queries.shape[0]
    units = len(near) + 1
    count = before[0].shape[1] // WIDTH
    wide = (count, units * rows, GROUP * rows)
    outs = [
        ((count, GROUP, rows), jnp.float32),
        ((count, 8, GROUP * rows), jnp.float32),
        (wide, jnp.bfloat16),
        (wide, jnp.bfloat16),
    ] + [((rows, count * WIDTH), jnp.bfloat16)] * (2 * units)
    kernel = functools.partial(earlier_kernel, start, count, len(near))
    inputs = [queries, dout, bias, *before, *near, stats]
    results = large(kernel, inputs, outs, cost(count, rows, 4 * units), behind)
    return results[0], results[1:4], results[4 : 4 + units], results[4 + units :]


def the_rest(queries, dout, bias, before, near, own, kept, start, skip, count, earlier, behind=()):
    rows = queries.shape[0]
    block = pl.BlockSpec((rows, GROUP * WIDTH), lambda g: (0, start + skip + g))
    inputs = [near_by(v) for v in (queries, dout, bias, *before, *near, *own, *kept)]
    extra = [*earlier, *behind]

    def kernel(*refs):
        refs = refs[: len(inputs)] + refs[len(inputs) + len(extra) :]
        rest_kernel(start, skip, len(near), *refs)

    wide = jax.ShapeDtypeStruct(queries.shape, jnp.bfloat16)
    results = pl.pallas_call(
        kernel,
        grid=(count,),
        in_specs=whole(len(inputs)) + whole(len(extra), pl.ANY),
        out_specs=[block, block] + whole(2),
        out_shape=[wide, wide] + [pltpu.VMEM((rows, count * WIDTH), jnp.float32)] * 2,
        input_output_aliases={len(inputs): 0, len(inputs) + 1: 1} if earlier else {},
        compiler_params=pltpu.CompilerParams(vmem_limit_bytes=VMEM_LARGE),
        cost_estimate=cost(count, rows, 10),
    )(*inputs, *extra)
    return results[:2], results[2:]


def route(flag, first, second, one, two):
    @pl.when(flag != 0)
    def _():
        one[...] = first[...]
        two[...] = second[...]

    @pl.when(flag == 0)
    def _():
        one[...] = second[...]
        two[...] = first[...]


def body(queries, keys, values, dout, doc_lengths, span_order):
    rows = queries.shape[0]
    size = lax.axis_size("head")
    subs = size // 2
    here = lax.axis_index("head")
    side, sub = here // subs, here % subs
    contexts = lax.axis_size(CONTEXT)
    context = lax.axis_index(CONTEXT)
    place = jnp.stack([context, side, sub, context % 2]).astype(jnp.int32)

    def place_flags(place, spans, flag):
        span = spans[2 * place[0] + place[1]]
        flag[0] = (span * subs + place[2]) * rows
        for index in (1, 2):
            flag[index] = place[index]
        flag[3] = (span == place[0]).astype(jnp.int32)
        flag[4] = place[3]
        flag[5] = (place[0] == contexts - 1).astype(jnp.int32)

    flags = pl.pallas_call(
        place_flags,
        in_specs=whole(2, pltpu.SMEM),
        out_specs=whole(1, pltpu.SMEM)[0],
        out_shape=pltpu.SMEM((6,), jnp.int32),
    )(place, span_order)
    width = keys.shape[1] // CHUNKS
    half = ((rows, width), jnp.bfloat16)

    def across(value):
        return lax.ppermute(value, "head", [(j, (j + subs) % size) for j in range(size)])

    def around(value, steps):
        pairs = [(j, j // subs * subs + (j + steps) % subs) for j in range(size)]
        return lax.ppermute(value, "head", pairs)

    def edges(value, start):
        pairs = [(c, c + 1) for c in range(start, contexts - 1, 2)]
        return lax.ppermute(value, CONTEXT, pairs + [(b, a) for a, b in pairs])

    def pick_in(place, keys, values, give, sem):
        for flag, source in ((0, values), (1, keys)):

            @pl.when(place[1] == flag)
            def _(source=source):
                copy = pltpu.make_async_copy(source, give, sem)
                copy.start()
                copy.wait()

    give = pl.pallas_call(
        pick_in,
        in_specs=whole(1, pltpu.SMEM) + whole(2, pl.ANY),
        out_specs=whole(1)[0],
        out_shape=pltpu.VMEM(keys.shape, keys.dtype),
        scratch_shapes=[pltpu.SemaphoreType.DMA],
        compiler_params=pltpu.CompilerParams(vmem_limit_bytes=VMEM_SMALL),
    )(place, far(keys), far(values))

    def mask(flag, doc_ref, bias_ref):
        first = flag[0]
        window = bias_ref.shape[0]
        q_pos = first + lax.broadcasted_iota(jnp.int32, (1, rows), 1)

        def step(index, carry):
            at, start = carry
            return at + doc_ref[index], jnp.where(at <= q_pos, at, start)

        _, start = lax.fori_loop(
            0, doc_ref.shape[0], step, (jnp.int32(0), jnp.zeros((1, rows), jnp.int32))
        )
        k_pos = first + rows - window + lax.broadcasted_iota(jnp.int32, (window, rows), 0)
        bias_ref[...] = jnp.where((k_pos >= start) & (k_pos <= q_pos), 0.0, MASKED)

    bias = pl.pallas_call(
        mask,
        in_specs=whole(2, pltpu.SMEM),
        out_specs=whole(1)[0],
        out_shape=pltpu.VMEM(((subs + 1) * rows, rows), jnp.float32),
        compiler_params=pltpu.CompilerParams(vmem_limit_bytes=VMEM_SMALL),
    )(in_scalars(flags), doc_lengths)

    def out_of_step(flag, backward):
        return (flag[3] + flag[4] + (1 if backward else 0)) % 2

    def edge_parts(own, got, backward, behind=()):
        def kernel(flag, *refs):
            own, (got, even, odd) = refs[:-3], refs[-3:]
            for which, keep in enumerate(own):

                @pl.when((flag[1] == which) | (len(own) == 1))
                def _(keep=keep):
                    route(out_of_step(flag, backward), keep, got.at[:rows], even, odd)

        return small(kernel, flags, [*own, got], [half, half], behind)

    def edge_done(own, got, even, odd, backward, behind=()):
        def kernel(flag, *refs):
            own, (got, even, odd, mine, theirs) = refs[:-5], refs[-5:]
            takes_odd = (flag[3] + flag[4]) % 2
            if backward:
                takes_odd = 1 - takes_odd

            @pl.when(flag[5] == 0)
            def _():
                route(takes_odd, odd, even, mine, theirs)

            kept = (flag[3] + (1 if backward else 0)) % 2
            for which, keep in enumerate(own):

                @pl.when((flag[5] != 0) & (kept != 0) & ((flag[1] == which) | (len(own) == 1)))
                def _(keep=keep):
                    route(takes_odd, keep, even, mine, theirs)

            @pl.when((flag[5] != 0) & (kept == 0))
            def _():
                route(takes_odd, got.at[:rows], even, mine, theirs)

        return small(kernel, flags, [*own, got, even, odd], [half, half], behind)

    def window_parts(own, mine, other, behind=()):
        def kernel(flag, own_key, own_value, mine, other, key, value, *sent):
            route(flag[1], other, mine, key, value)
            for index, out in enumerate(sent):
                inside = flag[2] + (subs - 1 - index) < subs

                @pl.when(inside)
                def _():
                    out[:, :width] = own_key[...]
                    out[:, width:] = own_value[...]

                @pl.when(jnp.logical_not(inside))
                def _():
                    out[:, :width] = key[...]
                    out[:, width:] = value[...]

        both = ((rows, 2 * width), jnp.bfloat16)
        outs = small(kernel, flags, [*own, mine, other], [half, half] + [both] * (subs - 1), behind)
        return outs[:2], [around(out, subs - 1 - i) for i, out in enumerate(outs[2:])]

    per_device = KEY_VALUE_HEADS // size

    def two_parts(out, lo, block):
        block = block.reshape(-1, rows)
        if block.shape[0] < EXTRA:
            fill = jnp.zeros((EXTRA - block.shape[0], rows), jnp.float32)
            block = jnp.concatenate([block, fill], axis=0)
        high = block.astype(jnp.bfloat16)
        out[rows:, lo : lo + rows] = high
        lo += WIDTH
        out[rows:, lo : lo + rows] = (block - high.astype(jnp.float32)).astype(jnp.bfloat16)

    def one_part(ref, lo):
        high, low = ref[rows:, lo : lo + rows], ref[rows:, lo + WIDTH : lo + WIDTH + rows]
        return high.astype(jnp.float32) + low.astype(jnp.float32)

    def near_terms(dk, dv, entropies):
        def kernel(flag, ent, *refs):
            for index in range(subs - 1):
                out = refs[2 * (subs - 1) + index]
                out[:rows, :width] = refs[index][...]
                out[:rows, width:] = refs[subs - 1 + index][...]
                to = lax.rem(flag[2] + index + 1, subs)
                for which in range(2):
                    block = ent[pl.ds((which * subs + to) * per_device, per_device)]
                    two_parts(out, 2 * which * WIDTH, block)

        both = ((rows + EXTRA, 2 * width), jnp.bfloat16)
        outs = small(kernel, flags, [entropies, *dk[1:], *dv[1:]], [both] * (subs - 1))
        return [around(out, index + 1 - subs) for index, out in enumerate(outs)]

    def collect(dk, dv, entropies, arrived, behind=()):
        def kernel(flag, dk, dv, ent, *refs):
            got = refs[: subs - 1]
            keep, give, own_key, own_value, ent_out = refs[subs - 1 :]
            for which, term, own in ((0, dk, own_key), (1, dv, own_value)):
                before = term[...].astype(jnp.float32)
                mine = jnp.zeros_like(before)
                for index, ref in enumerate(got):
                    part = ref[:rows, which * width : (which + 1) * width].astype(jnp.float32)
                    within = flag[2] + (subs - 1 - index) < subs
                    mine = mine + jnp.where(within, part, 0.0)
                    before = before + jnp.where(within, 0.0, part)
                own[...] = mine
                before = before.astype(jnp.bfloat16)

                @pl.when(flag[1] == which)
                def _():
                    keep[...] = before

                @pl.when(flag[1] != which)
                def _():
                    give[:rows, :] = before

            for which in range(2):
                block = ent[pl.ds((which * subs + flag[2]) * per_device, per_device)]
                blocks = [block.reshape(-1, rows)]
                blocks += [one_part(ref, 2 * which * WIDTH)[: blocks[0].shape[0]] for ref in got]

                @pl.when(flag[1] == which)
                def _(blocks=blocks):
                    for index, block in enumerate(blocks):
                        ent_out[index] = block

                @pl.when(flag[1] != which)
                def _(blocks=blocks):
                    for index, block in enumerate(blocks):
                        two_parts(give, 2 * index * WIDTH, block)

        full = ((rows, width), jnp.float32)
        kept = ((subs, per_device * GROUP, rows), jnp.float32)
        given = ((rows + EXTRA, width), jnp.bfloat16)
        inputs = [dk[0], dv[0], entropies, *arrived]
        return small(kernel, flags, inputs, [half, given, full, full, kept], behind)

    def finish(own_key, own_value, pieces, mine, other, entropies, got):
        spots = [0]
        for dk, dv in pieces:
            spots.append(spots[-1] + dk.shape[1])
        local = [own_key, own_value, mine, other, *[term for piece in pieces for term in piece]]
        local += [entropies, got]
        count = per_device * GROUP

        def kernel(flag, own_key, own_value, mine, other, *refs):
            terms, refs = refs[: 2 * len(pieces)], refs[2 * len(pieces) :]
            ent, got, out_key, out_value, out_ent = refs
            is_key = flag[1] == 0
            for index in range(len(pieces)):
                cols = slice(spots[index], spots[index + 1])
                here = mine[:, cols].astype(jnp.float32)
                there = other[:, cols].astype(jnp.float32)
                for out, own, term, back in (
                    (out_key, own_key, terms[2 * index], jnp.where(is_key, here, there)),
                    (out_value, own_value, terms[2 * index + 1], jnp.where(is_key, there, here)),
                ):
                    out[:, cols] = (own[:, cols] + term[...] + back).astype(jnp.bfloat16)
            for index in range(subs):
                steps = 0 if index == 0 else subs - index
                source = lax.rem(flag[2] + steps, subs)
                for way, block in ((flag[1], ent[index]), (1 - flag[1], one_part(got, 2 * index * WIDTH))):
                    for spot in range(size):

                        @pl.when(way * subs + source == spot)
                        def _(spot=spot, block=block):
                            out_ent[:, spot * rows : (spot + 1) * rows] = block[:count]

        return pl.pallas_call(
            kernel,
            grid=(1,),
            in_specs=whole(1, pltpu.SMEM) + whole(len(local)),
            out_specs=[pl.BlockSpec((rows, width), lambda g: (0, 0))] * 2
            + [pl.BlockSpec((count, size * rows), lambda g: (0, 0))],
            out_shape=[jax.ShapeDtypeStruct(keys.shape, jnp.bfloat16)] * 2
            + [jax.ShapeDtypeStruct((count, size * rows), jnp.float32)],
            compiler_params=pltpu.CompilerParams(vmem_limit_bytes=VMEM_SMALL),
        )(in_scalars(flags), *[near_by(v) for v in local])

    def travel(keep, got, backward, behind=()):
        even, odd = edge_parts(keep, got, backward, behind)
        return edges(even, 0), edges(odd, 1)

    def land(keep, got, even, odd, backward, behind=()):
        mine, theirs = edge_done(keep, got, even, odd, backward, behind)
        return mine, across(theirs)

    got = across(give)
    q_near, do_near, *own, stats = own_sums(bias, queries, dout, keys, values)
    even, odd = travel(own, got, False, [stats])
    mine, other = land(own, got, even, odd, False)
    before, near = window_parts(own, mine, other)
    entropies, kept, dk, dv = earlier_terms(q_near, do_near, bias, before, near, stats, 0)
    arrived = near_terms(dk, dv, entropies)
    keep, give, own_key, own_value, entropies = collect(dk, dv, entropies, arrived)
    got = across(give)
    wide, pieces, done = [], [], 0
    for count in BEHIND:
        wide, piece = the_rest(
            q_near, do_near, bias, before, near, own, kept, 0, done, count, wide, [give]
        )
        pieces.append(piece)
        done += count
    even, odd = travel([keep], got, True, pieces[0][:1])
    mine, other = land([keep], got, even, odd, True, pieces[1][:1])
    grad_key, grad_value, entropy = finish(
        own_key, own_value, pieces, mine, other, entropies, got
    )
    return wide[0], entropy.T, wide[1], grad_key, grad_value


def solution(mesh):
    rows = P(("inner", "outer", "head"), None)
    return jax.shard_map(
        body,
        mesh=mesh,
        in_specs=(rows, rows, rows, rows, P(), P()),
        out_specs=(rows, P(("inner", "outer"), "head"), rows, rows, rows),
        check_vma=False,
    )
```

```python
import functools
import math

import jax
import jax.numpy as jnp
from jax import lax
from jax.experimental import pallas as pl
from jax.experimental.pallas import tpu as pltpu
from jax.sharding import PartitionSpec as P

QUERY_HEADS = 64
KEY_VALUE_HEADS = 8
WIDTH = 128
GROUP = QUERY_HEADS // KEY_VALUE_HEADS
SCALE = 1.0 / math.sqrt(WIDTH)
MASKED = -1e30
CONTEXT = ("inner", "outer")
CHUNKS = 2
UNROLL = 2
EXTRA = 16
BEHIND = ((2, 2), (2, 2))
LOG2E = math.log2(math.e)
VMEM_SMALL = 8 * 2**20
VMEM_LARGE = 16 * 2**20
NT = (((1,), (1,)), ((), ()))
NN = (((1,), (0,)), ((), ()))


def dot(left, right, dims):
    return lax.dot_general(left, right, dims, preferred_element_type=jnp.float32)


def lanes(index, width=WIDTH):
    if isinstance(index, int):
        return slice(index * width, (index + 1) * width)
    return pl.ds(pl.multiple_of(index * width, WIDTH), width)


def group_rows(ref, g):
    return jnp.concatenate([ref[:, lanes(g * GROUP + h)] for h in range(GROUP)], axis=0)


def tiled(bias):
    return jnp.concatenate([bias] * GROUP, axis=1)


def row_sums(g, at, q_ref, do_ref, k_ref, v_ref, bias, stat_ref):
    s = dot(k_ref[:, lanes(g)], group_rows(q_ref, g), NT) + tiled(bias)
    dp = dot(v_ref[:, lanes(g)], group_rows(do_ref, g), NT)
    top = jnp.max(s, axis=0, keepdims=True)
    t = (s - top) * (SCALE * LOG2E)
    e = jnp.exp2(t)
    stat_ref[at, 0:1, :] = top
    stat_ref[at, 1:2, :] = jnp.sum(e, axis=0, keepdims=True)
    stat_ref[at, 2:3, :] = jnp.sum(e * t, axis=0, keepdims=True)
    stat_ref[at, 3:4, :] = jnp.sum(e * dp, axis=0, keepdims=True)


def first_kernel(contexts, count, place, *refs):
    sources, refs = refs[:4], refs[4:]
    spans_far, docs_far, refs = refs[0], refs[1], refs[2:]
    loaded, (flag, bias_ref, stat_ref, sems, spans, docs) = refs[:4], refs[4:]
    q_ref, do_ref, k_ref, v_ref = loaded
    rows = q_ref.shape[0]
    heads = k_ref.shape[1] // WIDTH
    short = [
        pltpu.make_async_copy(spans_far, spans, sems.at[2, 1]),
        pltpu.make_async_copy(docs_far, docs, sems.at[3, 1]),
    ]
    narrow = [pltpu.make_async_copy(sources[i], loaded[i], sems.at[i, 0]) for i in (2, 3)]

    def wide(g):
        cols = lanes(g, GROUP * WIDTH)
        return [
            pltpu.make_async_copy(sources[i].at[:, cols], loaded[i].at[:, cols], sems.at[i, g])
            for i in (0, 1)
        ]

    copies = short + narrow + [copy for g in range(heads) for copy in wide(g)]
    for copy in copies:
        copy.start()
    for copy in short:
        copy.wait()
    span = spans[2 * place[0] + place[1]]
    subs = bias_ref.shape[0] // rows - 1
    first = (span * subs + place[2]) * rows
    flag[0] = first
    for index in (1, 2):
        flag[index] = place[index]
    flag[3] = (span == place[0]).astype(jnp.int32)
    flag[4] = place[3]
    flag[5] = (place[0] == contexts - 1).astype(jnp.int32)
    q_pos = first + lax.broadcasted_iota(jnp.int32, (1, rows), 1)
    at = jnp.int32(0)
    start = jnp.zeros((1, rows), jnp.int32)

    def later(index, carry):
        at, start = carry
        return at + docs[index], jnp.where(at <= q_pos, at, start)

    _, start = lax.fori_loop(0, docs.shape[0], later, (at, start))
    window = bias_ref.shape[0]
    k_pos = first + rows - window + lax.broadcasted_iota(jnp.int32, (window, rows), 0)
    bias = jnp.where((k_pos >= start) & (k_pos <= q_pos), 0.0, MASKED)
    bias_ref[...] = bias
    for copy in narrow:
        copy.wait()

    def step(g, _):
        for copy in wide(g):
            copy.wait()
        row_sums(g, g, q_ref, do_ref, k_ref, v_ref, bias_ref[window - rows :, :], stat_ref)
        return 0

    lax.fori_loop(0, count, step, 0)
    for g in range(count, heads):
        for copy in wide(g):
            copy.wait()


def sums_kernel(start, count, q_ref, do_ref, k_ref, v_ref, bias_ref, stat_ref):
    last = bias_ref.shape[0] - q_ref.shape[0]

    def step(at, _):
        row_sums(start + at, at, q_ref, do_ref, k_ref, v_ref, bias_ref[last:, :], stat_ref)
        return 0

    lax.fori_loop(0, count, step, 0)


def earlier_kernel(start, count, near, q_ref, do_ref, bias_ref, first_k, first_v, *refs):
    near_refs, (stat_ref, *refs) = refs[:near], refs[near:]
    ent_ref, row_ref, p_ref, ds_ref = refs[:4]
    dk_refs, dv_refs = refs[4 : 5 + near], refs[5 + near :]
    rows = q_ref.shape[0]
    width = first_k.shape[1] // WIDTH
    window = (near + 1) * rows

    def head(at, _):
        g = start + at
        k_rows = jnp.concatenate(
            [first_k[:, lanes(at)], *[ref[:, lanes(at)] for ref in near_refs]], axis=0
        )
        v_rows = jnp.concatenate(
            [first_v[:, lanes(at)], *[ref[:, lanes(at + width)] for ref in near_refs]], axis=0
        )
        q_all, do_all = group_rows(q_ref, g), group_rows(do_ref, g)
        s = dot(k_rows, q_all, NT) + tiled(bias_ref[:window, :])
        dp = dot(v_rows, do_all, NT)
        own_top, own_total = stat_ref[at, 0:1, :], stat_ref[at, 1:2, :]
        top = jnp.maximum(jnp.max(s, axis=0, keepdims=True), own_top)
        t = (s - top) * (SCALE * LOG2E)
        e = jnp.exp2(t)
        shift = (own_top - top) * (SCALE * LOG2E)
        ratio = jnp.exp2(shift)
        total = own_total * ratio + jnp.sum(e, axis=0, keepdims=True)
        inv = 1.0 / total
        spread = (stat_ref[at, 2:3, :] + shift * own_total) * ratio
        spread = spread + jnp.sum(e * t, axis=0, keepdims=True)
        entropy = jnp.log(total) - spread * inv * math.log(2.0)
        for h in range(GROUP):
            ent_ref[at, h : h + 1, :] = entropy[:, h * rows : (h + 1) * rows]
        delta = stat_ref[at, 3:4, :] * ratio + jnp.sum(e * dp, axis=0, keepdims=True)
        delta = delta * inv
        row_ref[at, 0:1, :] = top * (SCALE * LOG2E) + jnp.log2(total)
        row_ref[at, 1:2, :] = delta
        p = e * inv
        pb = p.astype(jnp.bfloat16)
        ds = (p * (dp - delta)).astype(jnp.bfloat16)
        p_ref[at] = pb
        ds_ref[at] = ds
        dv = dot(pb, do_all, NN)
        dk = dot(ds, q_all, NN) * SCALE
        for unit in range(near + 1):
            part = slice(unit * rows, (unit + 1) * rows)
            dk_refs[unit][:, lanes(at)] = dk[part].astype(jnp.bfloat16)
            dv_refs[unit][:, lanes(at)] = dv[part].astype(jnp.bfloat16)

        return 0

    lax.fori_loop(0, count, head, 0, unroll=UNROLL)


def rest_kernel(start, skip, near, q_ref, do_ref, bias_ref, first_k, first_v, *refs):
    near_refs, (own_k, own_v), refs = refs[:near], refs[near : near + 2], refs[near + 2 :]
    row_ref, p_ref, ds_ref, att_ref, dq_ref, dk_ref, dv_ref = refs
    rows = q_ref.shape[0]
    width = first_k.shape[1] // WIDTH
    last = bias_ref.shape[0] - rows
    index = pl.program_id(0)
    at, g = skip + index, start + skip + index
    own_keys, own_values = own_k[:, lanes(g)], own_v[:, lanes(g)]
    k_rows = jnp.concatenate(
        [first_k[:, lanes(at)], *[ref[:, lanes(at)] for ref in near_refs], own_keys], axis=0
    )
    v_rows = jnp.concatenate(
        [first_v[:, lanes(at)], *[ref[:, lanes(at + width)] for ref in near_refs], own_values],
        axis=0,
    )
    q_all, do_all = group_rows(q_ref, g), group_rows(do_ref, g)
    s = dot(own_keys, q_all, NT) + tiled(bias_ref[last:, :])
    dp = dot(own_values, do_all, NT)
    p = jnp.exp2(s * (SCALE * LOG2E) - row_ref[at, 0:1, :])
    pb = p.astype(jnp.bfloat16)
    ds = (p * (dp - row_ref[at, 1:2, :])).astype(jnp.bfloat16)
    dv_ref[:, lanes(index)] = dot(pb, do_all, NN)
    dk_ref[:, lanes(index)] = dot(ds, q_all, NN) * SCALE
    p_all = jnp.concatenate([p_ref[at], pb], axis=0)
    ds_all = jnp.concatenate([ds_ref[at], ds], axis=0)
    out = dot(v_rows.T, p_all, NN).astype(jnp.bfloat16).T
    dq = (dot(k_rows.T, ds_all, NN) * SCALE).astype(jnp.bfloat16).T
    for h in range(GROUP):
        spot = slice(h * rows, (h + 1) * rows)
        att_ref[:, lanes(h)] = out[spot, :]
        dq_ref[:, lanes(h)] = dq[spot, :]


def whole(count, space=pltpu.VMEM):
    return [pl.BlockSpec(memory_space=space)] * count


def near_by(value):
    return pltpu.with_memory_space_constraint(value, pltpu.VMEM)


def in_scalars(value):
    return pltpu.with_memory_space_constraint(value, pltpu.SMEM)


def small(kernel, flags, inputs, outs, behind=()):
    def body(*refs):
        kernel(*refs[: 1 + len(inputs)], *refs[1 + len(inputs) + len(behind) :])

    return pl.pallas_call(
        body,
        in_specs=whole(1, pltpu.SMEM) + whole(len(inputs)) + whole(len(behind), pl.ANY),
        out_specs=whole(len(outs)),
        out_shape=[pltpu.VMEM(shape, dtype) for shape, dtype in outs],
        compiler_params=pltpu.CompilerParams(vmem_limit_bytes=VMEM_SMALL),
    )(in_scalars(flags), *[near_by(value) for value in inputs], *behind)


def cost(count, rows, products):
    return pl.CostEstimate(
        flops=16 * products * count * rows * GROUP * rows * WIDTH,
        bytes_accessed=1,
        transcendentals=0,
    )


def large(kernel, inputs, outs, price, behind=()):
    def body(*refs):
        kernel(*refs[: len(inputs)], *refs[len(inputs) + len(behind) :])

    return pl.pallas_call(
        body,
        in_specs=whole(len(inputs)) + whole(len(behind), pl.ANY),
        out_specs=whole(len(outs)),
        out_shape=[pltpu.VMEM(shape, dtype) for shape, dtype in outs],
        compiler_params=pltpu.CompilerParams(vmem_limit_bytes=VMEM_LARGE),
        cost_estimate=price,
    )(*[near_by(value) for value in inputs], *behind)


def far(value):
    return pltpu.with_memory_space_constraint(value, pltpu.HBM)


def first_step(contexts, subs, count, place, arrays, spans, docs, behind):
    rows = arrays[0].shape[0]
    heads = arrays[2].shape[1] // WIDTH

    def kernel(place, *refs):
        first_kernel(contexts, count, place, *refs[:6], *refs[7:])

    results = pl.pallas_call(
        kernel,
        in_specs=whole(1, pltpu.SMEM) + whole(7, pl.ANY),
        out_specs=whole(4) + whole(1, pltpu.SMEM) + whole(2),
        out_shape=[pltpu.VMEM(array.shape, array.dtype) for array in arrays]
        + [
            pltpu.SMEM((6,), jnp.int32),
            pltpu.VMEM(((subs + 1) * rows, rows), jnp.float32),
            pltpu.VMEM((count, 8, GROUP * rows), jnp.float32),
        ],
        scratch_shapes=[
            pltpu.SemaphoreType.DMA((4, heads)),
            pltpu.SMEM(spans.shape, jnp.int32),
            pltpu.SMEM(docs.shape, jnp.int32),
        ],
        compiler_params=pltpu.CompilerParams(vmem_limit_bytes=VMEM_LARGE),
        cost_estimate=cost(count, rows, 3),
    )(place, *[far(array) for array in (*arrays, spans, docs)], behind)
    return results[4], results[:2], results[2:4], results[5], results[6]


def more_sums(wide, own, bias, start, count, behind=()):
    rows = wide[0].shape[0]
    kernel = functools.partial(sums_kernel, start, count)
    outs = [((count, 8, GROUP * rows), jnp.float32)]
    return large(kernel, [*wide, *own, bias], outs, cost(count, rows, 2), behind)[0]


def earlier_terms(queries, dout, bias, before, near, stats, start, behind=()):
    rows = queries.shape[0]
    units = len(near) + 1
    count = before[0].shape[1] // WIDTH
    wide = (count, units * rows, GROUP * rows)
    outs = [
        ((count, GROUP, rows), jnp.float32),
        ((count, 8, GROUP * rows), jnp.float32),
        (wide, jnp.bfloat16),
        (wide, jnp.bfloat16),
    ] + [((rows, count * WIDTH), jnp.bfloat16)] * (2 * units)
    kernel = functools.partial(earlier_kernel, start, count, len(near))
    inputs = [queries, dout, bias, *before, *near, stats]
    results = large(kernel, inputs, outs, cost(count, rows, 4 * units), behind)
    return results[0], results[1:4], results[4 : 4 + units], results[4 + units :]


def the_rest(queries, dout, bias, before, near, own, kept, start, skip, count, earlier, behind=()):
    rows = queries.shape[0]
    block = pl.BlockSpec((rows, GROUP * WIDTH), lambda g: (0, start + skip + g))
    inputs = [near_by(v) for v in (queries, dout, bias, *before, *near, *own, *kept)]
    extra = [*earlier, *behind]

    def kernel(*refs):
        refs = refs[: len(inputs)] + refs[len(inputs) + len(extra) :]
        rest_kernel(start, skip, len(near), *refs)

    wide = jax.ShapeDtypeStruct(queries.shape, jnp.bfloat16)
    results = pl.pallas_call(
        kernel,
        grid=(count,),
        in_specs=whole(len(inputs)) + whole(len(extra), pl.ANY),
        out_specs=[block, block] + whole(2),
        out_shape=[wide, wide] + [pltpu.VMEM((rows, count * WIDTH), jnp.float32)] * 2,
        input_output_aliases={len(inputs): 0, len(inputs) + 1: 1} if earlier else {},
        compiler_params=pltpu.CompilerParams(vmem_limit_bytes=VMEM_LARGE),
        cost_estimate=cost(count, rows, 10),
    )(*inputs, *extra)
    return results[:2], results[2:]


def route(flag, first, second, one, two):
    @pl.when(flag != 0)
    def _():
        one[...] = first[...]
        two[...] = second[...]

    @pl.when(flag == 0)
    def _():
        one[...] = second[...]
        two[...] = first[...]


def body(queries, keys, values, dout, doc_lengths, span_order):
    rows = queries.shape[0]
    size = lax.axis_size("head")
    subs = size // 2
    here = lax.axis_index("head")
    side, sub = here // subs, here % subs
    contexts = lax.axis_size(CONTEXT)
    context = lax.axis_index(CONTEXT)
    place = jnp.stack([context, side, sub, context % 2]).astype(jnp.int32)

    width = keys.shape[1] // CHUNKS
    half = ((rows, width), jnp.bfloat16)

    def across(value):
        return lax.ppermute(value, "head", [(j, (j + subs) % size) for j in range(size)])

    def around(value, steps):
        pairs = [(j, j // subs * subs + (j + steps) % subs) for j in range(size)]
        return lax.ppermute(value, "head", pairs)

    def edges(value, start):
        pairs = [(c, c + 1) for c in range(start, contexts - 1, 2)]
        return lax.ppermute(value, CONTEXT, pairs + [(b, a) for a, b in pairs])

    def columns(chunk):
        return slice(chunk * width, (chunk + 1) * width)

    def pick_in(place, keys, values, give, sem):
        for flag, source in ((0, values), (1, keys)):

            @pl.when(place[1] == flag)
            def _(source=source):
                copy = pltpu.make_async_copy(source.at[:, columns(0)], give, sem)
                copy.start()
                copy.wait()

    first_give = pl.pallas_call(
        pick_in,
        in_specs=whole(1, pltpu.SMEM) + whole(2, pl.ANY),
        out_specs=whole(1)[0],
        out_shape=pltpu.VMEM(*half),
        scratch_shapes=[pltpu.SemaphoreType.DMA],
        compiler_params=pltpu.CompilerParams(vmem_limit_bytes=VMEM_SMALL),
    )(place, far(keys), far(values))

    def later_give(own, chunk, behind):
        def kernel(flag, key, value, give):
            for which, source in ((0, value), (1, key)):

                @pl.when(flag[1] == which)
                def _(source=source):
                    give[...] = source[:, columns(chunk)]

        return small(kernel, flags, own, [half], behind)[0]

    def out_of_step(flag, backward):
        return (flag[3] + flag[4] + (1 if backward else 0)) % 2

    def edge_parts(own, got, backward, cols=slice(None), behind=()):
        def kernel(flag, *refs):
            own, (got, even, odd) = refs[:-3], refs[-3:]
            for which, keep in enumerate(own):

                @pl.when((flag[1] == which) | (len(own) == 1))
                def _(keep=keep):
                    route(out_of_step(flag, backward), keep.at[:, cols], got.at[:rows], even, odd)

        return small(kernel, flags, [*own, got], [half, half], behind)

    def edge_done(own, got, even, odd, backward, cols=slice(None), behind=()):
        def kernel(flag, *refs):
            own, (got, even, odd, mine, theirs) = refs[:-5], refs[-5:]
            takes_odd = (flag[3] + flag[4]) % 2
            if backward:
                takes_odd = 1 - takes_odd

            @pl.when(flag[5] == 0)
            def _():
                route(takes_odd, odd, even, mine, theirs)

            kept = (flag[3] + (1 if backward else 0)) % 2
            for which, keep in enumerate(own):

                @pl.when((flag[5] != 0) & (kept != 0) & ((flag[1] == which) | (len(own) == 1)))
                def _(keep=keep):
                    route(takes_odd, keep.at[:, cols], even, mine, theirs)

            @pl.when((flag[5] != 0) & (kept == 0))
            def _():
                route(takes_odd, got.at[:rows], even, mine, theirs)

        return small(kernel, flags, [*own, got, even, odd], [half, half], behind)

    def window_parts(own, mine, other, cols, behind=()):
        def kernel(flag, own_key, own_value, mine, other, key, value, *sent):
            route(flag[1], other, mine, key, value)
            for index, out in enumerate(sent):
                inside = flag[2] + (subs - 1 - index) < subs

                @pl.when(inside)
                def _():
                    out[:, :width] = own_key[:, cols]
                    out[:, width:] = own_value[:, cols]

                @pl.when(jnp.logical_not(inside))
                def _():
                    out[:, :width] = key[...]
                    out[:, width:] = value[...]

        both = ((rows, 2 * width), jnp.bfloat16)
        outs = small(kernel, flags, [*own, mine, other], [half, half] + [both] * (subs - 1), behind)
        return outs[:2], [around(out, subs - 1 - i) for i, out in enumerate(outs[2:])]

    per_device = KEY_VALUE_HEADS // size

    def two_parts(out, lo, block):
        block = block.reshape(-1, rows)
        if block.shape[0] < EXTRA:
            fill = jnp.zeros((EXTRA - block.shape[0], rows), jnp.float32)
            block = jnp.concatenate([block, fill], axis=0)
        high = block.astype(jnp.bfloat16)
        out[rows:, lo : lo + rows] = high
        lo += rows
        out[rows:, lo : lo + rows] = (block - high.astype(jnp.float32)).astype(jnp.bfloat16)

    def one_part(ref, lo):
        high, low = ref[rows:, lo : lo + rows], ref[rows:, lo + rows : lo + 2 * rows]
        return high.astype(jnp.float32) + low.astype(jnp.float32)

    def near_terms(dk, dv, entropies=(), behind=()):
        extra = EXTRA if entropies else 0

        def kernel(flag, *refs):
            ents, refs = refs[: len(entropies)], refs[len(entropies) :]
            for index in range(subs - 1):
                out = refs[2 * (subs - 1) + index]
                out[:rows, :width] = refs[index][...]
                out[:rows, width:] = refs[subs - 1 + index][...]
                to = lax.rem(flag[2] + index + 1, subs)
                for which, ent in enumerate(ents):
                    two_parts(out, 2 * which * rows, ent[pl.ds(to * per_device, per_device)])

        both = ((rows + extra, 2 * width), jnp.bfloat16)
        outs = small(kernel, flags, [*entropies, *dk[1:], *dv[1:]], [both] * (subs - 1), behind)
        return [around(out, index + 1 - subs) for index, out in enumerate(outs)]

    def collect(dk, dv, arrived, entropies=(), behind=()):
        extra = EXTRA if entropies else 0

        def kernel(flag, dk, dv, *refs):
            ents, refs = refs[: len(entropies)], refs[len(entropies) :]
            got = refs[: subs - 1]
            keep, give, own_key, own_value = refs[subs - 1 : subs + 3]
            for which, term, own in ((0, dk, own_key), (1, dv, own_value)):
                before = term[...].astype(jnp.float32)
                mine = jnp.zeros_like(before)
                for index, ref in enumerate(got):
                    part = ref[:rows, which * width : (which + 1) * width].astype(jnp.float32)
                    within = flag[2] + (subs - 1 - index) < subs
                    mine = mine + jnp.where(within, part, 0.0)
                    before = before + jnp.where(within, 0.0, part)
                own[...] = mine
                before = before.astype(jnp.bfloat16)

                @pl.when(flag[1] == which)
                def _():
                    keep[...] = before

                @pl.when(flag[1] != which)
                def _():
                    give[:rows, :] = before

            for which, ent in enumerate(ents):
                block = ent[pl.ds(flag[2] * per_device, per_device)]
                blocks = [block.reshape(-1, rows)]
                blocks += [one_part(ref, 2 * which * rows)[: blocks[0].shape[0]] for ref in got]

                @pl.when(flag[1] == which)
                def _(blocks=blocks):
                    for index, block in enumerate(blocks):
                        refs[subs + 3][index] = block

                @pl.when(flag[1] != which)
                def _(blocks=blocks):
                    for index, block in enumerate(blocks):
                        two_parts(give, 2 * index * rows, block)

        full = ((rows, width), jnp.float32)
        outs = [half, ((rows + extra, width), jnp.bfloat16), full, full]
        if entropies:
            outs.append(((subs, per_device * GROUP, rows), jnp.float32))
        return small(kernel, flags, [dk[0], dv[0], *entropies, *arrived], outs, behind)

    def finish(chunks, entropies, got):
        local, plans = [entropies, got], []
        for chunk, (own_key, own_value, pieces, mine, other) in enumerate(chunks):
            spot = 0
            for dk, dv in pieces:
                cols = slice(spot, spot + dk.shape[1])
                plans.append((len(local), cols, slice(cols.start + chunk * width, cols.stop + chunk * width)))
                local += [own_key, own_value, mine, other, dk, dv]
                spot = cols.stop
        count = per_device * GROUP

        def kernel(flag, *refs):
            ent, got = refs[:2]
            out_key, out_value, out_ent = refs[-3:]
            is_key = flag[1] == 0
            for at, cols, to in plans:
                own_key, own_value, mine, other, dk, dv = refs[at : at + 6]
                here = mine[:, cols].astype(jnp.float32)
                there = other[:, cols].astype(jnp.float32)
                for out, own, term, back in (
                    (out_key, own_key, dk, jnp.where(is_key, here, there)),
                    (out_value, own_value, dv, jnp.where(is_key, there, here)),
                ):
                    out[:, to] = (own[:, cols] + term[...] + back).astype(jnp.bfloat16)
            for index in range(subs):
                steps = 0 if index == 0 else subs - index
                source = lax.rem(flag[2] + steps, subs)
                for way, block in ((flag[1], ent[index]), (1 - flag[1], one_part(got, 2 * index * rows))):
                    for spot in range(size):

                        @pl.when(way * subs + source == spot)
                        def _(spot=spot, block=block):
                            out_ent[:, spot * rows : (spot + 1) * rows] = block[:count]

        return pl.pallas_call(
            kernel,
            grid=(1,),
            in_specs=whole(1, pltpu.SMEM) + whole(len(local)),
            out_specs=[pl.BlockSpec(keys.shape, lambda g: (0, 0))] * 2
            + [pl.BlockSpec((count, size * rows), lambda g: (0, 0))],
            out_shape=[jax.ShapeDtypeStruct(keys.shape, jnp.bfloat16)] * 2
            + [jax.ShapeDtypeStruct((count, size * rows), jnp.float32)],
            compiler_params=pltpu.CompilerParams(vmem_limit_bytes=VMEM_SMALL),
        )(in_scalars(flags), *[near_by(v) for v in local])

    def over(parts):
        odd = edges(parts[1], 1)
        return edges(parts[0], 0), odd

    per_chunk = KEY_VALUE_HEADS // CHUNKS
    got = [across(first_give)]
    flags, wide_near, own, bias, stats = first_step(
        contexts, subs, per_chunk, place, (queries, dout, keys, values), span_order, doc_lengths, first_give
    )
    got.append(across(later_give(own, 1, got)))
    cols = [columns(chunk) for chunk in range(CHUNKS)]
    in0 = edge_parts(own, got[0], False, cols[0], [stats])
    edge0 = over(in0)
    in1 = edge_parts(own, got[1], False, cols[1])
    edge1 = over(in1)
    stats = [stats, more_sums(wide_near, own, bias, per_chunk, per_chunk, in1[:1])]
    mine0, theirs0 = edge_done(own, got[0], *edge0, False, cols[0], stats[1:])
    other0 = across(theirs0)
    mine1, theirs1 = edge_done(own, got[1], *edge1, False, cols[1], [theirs0])
    other1 = across(theirs1)
    before0, near0 = window_parts(own, mine0, other0, cols[0], [theirs1])
    ent0, kept0, dk0, dv0 = earlier_terms(*wide_near, bias, before0, near0, stats[0], 0)
    before1, near1 = window_parts(own, mine1, other1, cols[1], [ent0])
    keep0, give0, *own0 = collect(dk0, dv0, near_terms(dk0, dv0))
    back0 = across(give0)
    ent1, kept1, dk1, dv1 = earlier_terms(
        *wide_near, bias, before1, near1, stats[1], per_chunk, [give0]
    )
    out0 = edge_parts([keep0], back0, True)
    edge0 = over(out0)
    ents = [ent0, ent1]
    keep1, give1, *own1, entropies = collect(
        dk1, dv1, near_terms(dk1, dv1, ents, out0[:1]), ents
    )
    back1 = across(give1)
    wide, pieces = [], []

    def rest(chunk, piece, behind):
        nonlocal wide
        before, near, kept = ((before0, near0, kept0), (before1, near1, kept1))[chunk]
        skip, count = sum(BEHIND[chunk][:piece]), BEHIND[chunk][piece]
        start = chunk * per_chunk
        wide, terms = the_rest(
            *wide_near, bias, before, near, own, kept, start, skip, count, wide, behind
        )
        pieces.append(terms)
        return terms[:1]

    done = rest(0, 0, [give1])
    out1 = edge_parts([keep1], back1, True, behind=done)
    edge1 = over(out1)
    done = rest(0, 1, out1[:1])
    mine0, theirs0 = edge_done([keep0], back0, *edge0, True, behind=done)
    other0 = across(theirs0)
    done = rest(1, 0, [theirs0, *edge1])
    mine1, theirs1 = edge_done([keep1], back1, *edge1, True, behind=done)
    other1 = across(theirs1)
    rest(1, 1, [theirs1])
    grad_key, grad_value, entropy = finish(
        [(*own0, pieces[:2], mine0, other0), (*own1, pieces[2:], mine1, other1)], entropies, back1
    )
    return wide[0], entropy.T, wide[1], grad_key, grad_value


def solution(mesh):
    rows = P(("inner", "outer", "head"), None)
    return jax.shard_map(
        body,
        mesh=mesh,
        in_specs=(rows, rows, rows, rows, P(), P()),
        out_specs=(rows, P(("inner", "outer"), "head"), rows, rows, rows),
        check_vma=False,
    )
```

```python
import functools
import math

import jax
import jax.numpy as jnp
from jax import lax
from jax.experimental import pallas as pl
from jax.experimental.pallas import tpu as pltpu
from jax.sharding import PartitionSpec as P

QUERY_HEADS = 64
KEY_VALUE_HEADS = 8
WIDTH = 128
GROUP = QUERY_HEADS // KEY_VALUE_HEADS
SCALE = 1.0 / math.sqrt(WIDTH)
MASKED = -1e30
CONTEXT = ("inner", "outer")
CHUNKS = 2
UNROLL = 2
EXTRA = 16
BEHIND = ((1, 1, 2), (2, 2))
LOG2E = math.log2(math.e)
VMEM_SMALL = 8 * 2**20
VMEM_LARGE = 16 * 2**20
NT = (((1,), (1,)), ((), ()))
NN = (((1,), (0,)), ((), ()))


def dot(left, right, dims):
    return lax.dot_general(left, right, dims, preferred_element_type=jnp.float32)


def lanes(index, width=WIDTH):
    if isinstance(index, int):
        return slice(index * width, (index + 1) * width)
    return pl.ds(pl.multiple_of(index * width, WIDTH), width)


def group_rows(ref, g):
    return jnp.concatenate([ref[:, lanes(g * GROUP + h)] for h in range(GROUP)], axis=0)


def tiled(bias):
    return jnp.concatenate([bias] * GROUP, axis=1)


def row_sums(g, at, q_ref, do_ref, k_ref, v_ref, bias, stat_ref):
    s = dot(k_ref[:, lanes(g)], group_rows(q_ref, g), NT) + tiled(bias)
    dp = dot(v_ref[:, lanes(g)], group_rows(do_ref, g), NT)
    top = jnp.max(s, axis=0, keepdims=True)
    t = (s - top) * (SCALE * LOG2E)
    e = jnp.exp2(t)
    stat_ref[at, 0:1, :] = top
    stat_ref[at, 1:2, :] = jnp.sum(e, axis=0, keepdims=True)
    stat_ref[at, 2:3, :] = jnp.sum(e * t, axis=0, keepdims=True)
    stat_ref[at, 3:4, :] = jnp.sum(e * dp, axis=0, keepdims=True)


def first_kernel(contexts, count, *refs):
    sources, refs = refs[:4], refs[4:]
    spans_far, docs_far, refs = refs[0], refs[1], refs[2:]
    loaded, (flag, bias_ref, stat_ref, sems, spans, docs) = refs[:4], refs[4:]
    q_ref, do_ref, k_ref, v_ref = loaded
    rows = q_ref.shape[0]
    heads = k_ref.shape[1] // WIDTH
    short = [
        pltpu.make_async_copy(spans_far, spans, sems.at[2, 1]),
        pltpu.make_async_copy(docs_far, docs, sems.at[3, 1]),
    ]
    narrow = [pltpu.make_async_copy(sources[i], loaded[i], sems.at[i, 0]) for i in (2, 3)]

    def wide(g):
        cols = lanes(g, GROUP * WIDTH)
        return [
            pltpu.make_async_copy(sources[i].at[:, cols], loaded[i].at[:, cols], sems.at[i, g])
            for i in (0, 1)
        ]

    copies = short + narrow + [copy for g in range(heads) for copy in wide(g)]
    for copy in copies:
        copy.start()
    for copy in short:
        copy.wait()
    subs = bias_ref.shape[0] // rows - 1
    here, context = lax.axis_index("head"), lax.axis_index(CONTEXT)
    side, sub = here // subs, lax.rem(here, subs)
    span = spans[2 * context + side]
    first = (span * subs + sub) * rows
    flag[0] = first
    flag[1] = side
    flag[2] = sub
    flag[3] = (span == context).astype(jnp.int32)
    flag[4] = lax.rem(context, 2)
    flag[5] = (context == contexts - 1).astype(jnp.int32)
    q_pos = first + lax.broadcasted_iota(jnp.int32, (1, rows), 1)
    at = jnp.int32(0)
    start = jnp.zeros((1, rows), jnp.int32)

    def later(index, carry):
        at, start = carry
        return at + docs[index], jnp.where(at <= q_pos, at, start)

    _, start = lax.fori_loop(0, docs.shape[0], later, (at, start))
    window = bias_ref.shape[0]
    k_pos = first + rows - window + lax.broadcasted_iota(jnp.int32, (window, rows), 0)
    bias = jnp.where((k_pos >= start) & (k_pos <= q_pos), 0.0, MASKED)
    bias_ref[...] = bias
    for copy in narrow:
        copy.wait()

    def step(g, _):
        for copy in wide(g):
            copy.wait()
        row_sums(g, g, q_ref, do_ref, k_ref, v_ref, bias_ref[window - rows :, :], stat_ref)
        return 0

    lax.fori_loop(0, count, step, 0)
    for g in range(count, heads):
        for copy in wide(g):
            copy.wait()


def sums_kernel(start, count, q_ref, do_ref, k_ref, v_ref, bias_ref, stat_ref):
    last = bias_ref.shape[0] - q_ref.shape[0]

    def step(at, _):
        row_sums(start + at, at, q_ref, do_ref, k_ref, v_ref, bias_ref[last:, :], stat_ref)
        return 0

    lax.fori_loop(0, count, step, 0)


def earlier_kernel(start, count, near, q_ref, do_ref, bias_ref, first_k, first_v, *refs):
    near_refs, (stat_ref, *refs) = refs[:near], refs[near:]
    ent_ref, row_ref, p_ref, ds_ref = refs[:4]
    dk_refs, dv_refs = refs[4 : 5 + near], refs[5 + near :]
    rows = q_ref.shape[0]
    width = first_k.shape[1] // WIDTH
    window = (near + 1) * rows

    def head(at, _):
        g = start + at
        k_rows = jnp.concatenate(
            [first_k[:, lanes(at)], *[ref[:, lanes(at)] for ref in near_refs]], axis=0
        )
        v_rows = jnp.concatenate(
            [first_v[:, lanes(at)], *[ref[:, lanes(at + width)] for ref in near_refs]], axis=0
        )
        q_all, do_all = group_rows(q_ref, g), group_rows(do_ref, g)
        s = dot(k_rows, q_all, NT) + tiled(bias_ref[:window, :])
        dp = dot(v_rows, do_all, NT)
        own_top, own_total = stat_ref[at, 0:1, :], stat_ref[at, 1:2, :]
        top = jnp.maximum(jnp.max(s, axis=0, keepdims=True), own_top)
        t = (s - top) * (SCALE * LOG2E)
        e = jnp.exp2(t)
        shift = (own_top - top) * (SCALE * LOG2E)
        ratio = jnp.exp2(shift)
        total = own_total * ratio + jnp.sum(e, axis=0, keepdims=True)
        inv = 1.0 / total
        spread = (stat_ref[at, 2:3, :] + shift * own_total) * ratio
        spread = spread + jnp.sum(e * t, axis=0, keepdims=True)
        entropy = jnp.log(total) - spread * inv * math.log(2.0)
        for h in range(GROUP):
            ent_ref[at, h : h + 1, :] = entropy[:, h * rows : (h + 1) * rows]
        delta = stat_ref[at, 3:4, :] * ratio + jnp.sum(e * dp, axis=0, keepdims=True)
        delta = delta * inv
        row_ref[at, 0:1, :] = top * (SCALE * LOG2E) + jnp.log2(total)
        row_ref[at, 1:2, :] = delta
        p = e * inv
        pb = p.astype(jnp.bfloat16)
        ds = (p * (dp - delta)).astype(jnp.bfloat16)
        p_ref[at] = pb
        ds_ref[at] = ds
        dv = dot(pb, do_all, NN)
        dk = dot(ds, q_all, NN) * SCALE
        for unit in range(near + 1):
            part = slice(unit * rows, (unit + 1) * rows)
            dk_refs[unit][:, lanes(at)] = dk[part].astype(jnp.bfloat16)
            dv_refs[unit][:, lanes(at)] = dv[part].astype(jnp.bfloat16)

        return 0

    lax.fori_loop(0, count, head, 0, unroll=UNROLL)


def rest_kernel(start, skip, near, q_ref, do_ref, bias_ref, first_k, first_v, *refs):
    near_refs, (own_k, own_v), refs = refs[:near], refs[near : near + 2], refs[near + 2 :]
    row_ref, p_ref, ds_ref, att_ref, dq_ref, dk_ref, dv_ref = refs
    rows = q_ref.shape[0]
    width = first_k.shape[1] // WIDTH
    last = bias_ref.shape[0] - rows
    index = pl.program_id(0)
    at, g = skip + index, start + skip + index
    own_keys, own_values = own_k[:, lanes(g)], own_v[:, lanes(g)]
    k_rows = jnp.concatenate(
        [first_k[:, lanes(at)], *[ref[:, lanes(at)] for ref in near_refs], own_keys], axis=0
    )
    v_rows = jnp.concatenate(
        [first_v[:, lanes(at)], *[ref[:, lanes(at + width)] for ref in near_refs], own_values],
        axis=0,
    )
    q_all, do_all = group_rows(q_ref, g), group_rows(do_ref, g)
    s = dot(own_keys, q_all, NT) + tiled(bias_ref[last:, :])
    dp = dot(own_values, do_all, NT)
    p = jnp.exp2(s * (SCALE * LOG2E) - row_ref[at, 0:1, :])
    pb = p.astype(jnp.bfloat16)
    ds = (p * (dp - row_ref[at, 1:2, :])).astype(jnp.bfloat16)
    dv_ref[:, lanes(index)] = dot(pb, do_all, NN)
    dk_ref[:, lanes(index)] = dot(ds, q_all, NN) * SCALE
    p_all = jnp.concatenate([p_ref[at], pb], axis=0)
    ds_all = jnp.concatenate([ds_ref[at], ds], axis=0)
    out = dot(v_rows.T, p_all, NN).astype(jnp.bfloat16).T
    dq = (dot(k_rows.T, ds_all, NN) * SCALE).astype(jnp.bfloat16).T
    for h in range(GROUP):
        spot = slice(h * rows, (h + 1) * rows)
        att_ref[:, lanes(h)] = out[spot, :]
        dq_ref[:, lanes(h)] = dq[spot, :]


def whole(count, space=pltpu.VMEM):
    return [pl.BlockSpec(memory_space=space)] * count


def near_by(value):
    return pltpu.with_memory_space_constraint(value, pltpu.VMEM)


def in_scalars(value):
    return pltpu.with_memory_space_constraint(value, pltpu.SMEM)


def small(kernel, flags, inputs, outs, behind=()):
    def body(*refs):
        kernel(*refs[: 1 + len(inputs)], *refs[1 + len(inputs) + len(behind) :])

    return pl.pallas_call(
        body,
        in_specs=whole(1, pltpu.SMEM) + whole(len(inputs)) + whole(len(behind), pl.ANY),
        out_specs=whole(len(outs)),
        out_shape=[pltpu.VMEM(shape, dtype) for shape, dtype in outs],
        compiler_params=pltpu.CompilerParams(vmem_limit_bytes=VMEM_SMALL),
    )(in_scalars(flags), *[near_by(value) for value in inputs], *behind)


def cost(count, rows, products):
    return pl.CostEstimate(
        flops=4 * products * count * rows * GROUP * rows * WIDTH,
        bytes_accessed=1,
        transcendentals=0,
    )


def large(kernel, inputs, outs, price, behind=()):
    def body(*refs):
        kernel(*refs[: len(inputs)], *refs[len(inputs) + len(behind) :])

    return pl.pallas_call(
        body,
        in_specs=whole(len(inputs)) + whole(len(behind), pl.ANY),
        out_specs=whole(len(outs)),
        out_shape=[pltpu.VMEM(shape, dtype) for shape, dtype in outs],
        compiler_params=pltpu.CompilerParams(vmem_limit_bytes=VMEM_LARGE),
        cost_estimate=price,
    )(*[near_by(value) for value in inputs], *behind)


def far(value):
    return pltpu.with_memory_space_constraint(value, pltpu.HBM)


def first_step(contexts, subs, count, arrays, spans, docs, behind):
    rows = arrays[0].shape[0]
    heads = arrays[2].shape[1] // WIDTH

    def kernel(*refs):
        first_kernel(contexts, count, *refs[:6], *refs[7:])

    results = pl.pallas_call(
        kernel,
        in_specs=whole(7, pl.ANY),
        out_specs=whole(4) + whole(1, pltpu.SMEM) + whole(2),
        out_shape=[pltpu.VMEM(array.shape, array.dtype) for array in arrays]
        + [
            pltpu.SMEM((6,), jnp.int32),
            pltpu.VMEM(((subs + 1) * rows, rows), jnp.float32),
            pltpu.VMEM((count, 8, GROUP * rows), jnp.float32),
        ],
        scratch_shapes=[
            pltpu.SemaphoreType.DMA((4, heads)),
            pltpu.SMEM(spans.shape, jnp.int32),
            pltpu.SMEM(docs.shape, jnp.int32),
        ],
        compiler_params=pltpu.CompilerParams(vmem_limit_bytes=VMEM_LARGE),
        cost_estimate=cost(count, rows, 3),
    )(*[far(array) for array in (*arrays, spans, docs)], behind)
    return results[4], results[:2], results[2:4], results[5], results[6]


def more_sums(wide, own, bias, start, count, behind=()):
    rows = wide[0].shape[0]
    kernel = functools.partial(sums_kernel, start, count)
    outs = [((count, 8, GROUP * rows), jnp.float32)]
    return large(kernel, [*wide, *own, bias], outs, cost(count, rows, 2), behind)[0]


def earlier_terms(queries, dout, bias, before, near, stats, start, behind=()):
    rows = queries.shape[0]
    units = len(near) + 1
    count = before[0].shape[1] // WIDTH
    wide = (count, units * rows, GROUP * rows)
    outs = [
        ((count, GROUP, rows), jnp.float32),
        ((count, 8, GROUP * rows), jnp.float32),
        (wide, jnp.bfloat16),
        (wide, jnp.bfloat16),
    ] + [((rows, count * WIDTH), jnp.bfloat16)] * (2 * units)
    kernel = functools.partial(earlier_kernel, start, count, len(near))
    inputs = [queries, dout, bias, *before, *near, stats]
    results = large(kernel, inputs, outs, cost(count, rows, 4 * units), behind)
    return results[0], results[1:4], results[4 : 4 + units], results[4 + units :]


def the_rest(queries, dout, bias, before, near, own, kept, start, skip, count, earlier, behind=()):
    rows = queries.shape[0]
    block = pl.BlockSpec((rows, GROUP * WIDTH), lambda g: (0, start + skip + g))
    inputs = [near_by(v) for v in (queries, dout, bias, *before, *near, *own, *kept)]
    extra = [*earlier, *behind]

    def kernel(*refs):
        refs = refs[: len(inputs)] + refs[len(inputs) + len(extra) :]
        rest_kernel(start, skip, len(near), *refs)

    wide = jax.ShapeDtypeStruct(queries.shape, jnp.bfloat16)
    results = pl.pallas_call(
        kernel,
        grid=(count,),
        in_specs=whole(len(inputs)) + whole(len(extra), pl.ANY),
        out_specs=[block, block] + whole(2),
        out_shape=[wide, wide] + [pltpu.VMEM((rows, count * WIDTH), jnp.float32)] * 2,
        input_output_aliases={len(inputs): 0, len(inputs) + 1: 1} if earlier else {},
        compiler_params=pltpu.CompilerParams(vmem_limit_bytes=VMEM_LARGE),
        cost_estimate=cost(count, rows, 10),
    )(*inputs, *extra)
    return results[:2], results[2:]


def route(flag, first, second, one, two):
    @pl.when(flag != 0)
    def _():
        one[...] = first[...]
        two[...] = second[...]

    @pl.when(flag == 0)
    def _():
        one[...] = second[...]
        two[...] = first[...]


def body(queries, keys, values, dout, doc_lengths, span_order):
    rows = queries.shape[0]
    size = lax.axis_size("head")
    subs = size // 2
    contexts = lax.axis_size(CONTEXT)
    width = keys.shape[1] // CHUNKS
    half = ((rows, width), jnp.bfloat16)

    def across(value):
        return lax.ppermute(value, "head", [(j, (j + subs) % size) for j in range(size)])

    def around(value, steps):
        pairs = [(j, j // subs * subs + (j + steps) % subs) for j in range(size)]
        return lax.ppermute(value, "head", pairs)

    def edges(value, start):
        pairs = [(c, c + 1) for c in range(start, contexts - 1, 2)]
        return lax.ppermute(value, CONTEXT, pairs + [(b, a) for a, b in pairs])

    def columns(chunk):
        return slice(chunk * width, (chunk + 1) * width)

    def pick_in(keys, values, give, sem):
        for flag, source in ((0, values), (1, keys)):

            @pl.when(lax.axis_index("head") // subs == flag)
            def _(source=source):
                copy = pltpu.make_async_copy(source.at[:, columns(0)], give, sem)
                copy.start()
                copy.wait()

    first_give = pl.pallas_call(
        pick_in,
        in_specs=whole(2, pl.ANY),
        out_specs=whole(1)[0],
        out_shape=pltpu.VMEM(*half),
        scratch_shapes=[pltpu.SemaphoreType.DMA],
        compiler_params=pltpu.CompilerParams(vmem_limit_bytes=VMEM_SMALL),
    )(far(keys), far(values))

    def later_give(own, chunk, behind):
        def kernel(flag, key, value, give):
            for which, source in ((0, value), (1, key)):

                @pl.when(flag[1] == which)
                def _(source=source):
                    give[...] = source[:, columns(chunk)]

        return small(kernel, flags, own, [half], behind)[0]

    def out_of_step(flag, backward):
        return (flag[3] + flag[4] + (1 if backward else 0)) % 2

    def edge_part(own, got, backward, odd, cols=slice(None), behind=()):
        def kernel(flag, *refs):
            own, (got, out) = refs[:-2], refs[-2:]
            keeps = out_of_step(flag, backward) != odd
            for which, keep in enumerate(own):

                @pl.when(keeps & ((flag[1] == which) | (len(own) == 1)))
                def _(keep=keep):
                    out[...] = keep[:, cols]

            @pl.when(jnp.logical_not(keeps))
            def _():
                out[...] = got[:rows, :]

        return small(kernel, flags, [*own, got], [half], behind)[0]

    def edge_done(own, got, even, odd, backward, cols=slice(None), behind=()):
        def kernel(flag, *refs):
            own, (got, even, odd, mine, theirs) = refs[:-5], refs[-5:]
            takes_odd = (flag[3] + flag[4]) % 2
            if backward:
                takes_odd = 1 - takes_odd

            @pl.when(flag[5] == 0)
            def _():
                route(takes_odd, odd, even, mine, theirs)

            kept = (flag[3] + (1 if backward else 0)) % 2
            for which, keep in enumerate(own):

                @pl.when((flag[5] != 0) & (kept != 0) & ((flag[1] == which) | (len(own) == 1)))
                def _(keep=keep):
                    route(takes_odd, keep.at[:, cols], even, mine, theirs)

            @pl.when((flag[5] != 0) & (kept == 0))
            def _():
                route(takes_odd, got.at[:rows], even, mine, theirs)

        return small(kernel, flags, [*own, got, even, odd], [half, half], behind)

    def window_parts(own, mine, other, cols, behind=()):
        def kernel(flag, own_key, own_value, mine, other, key, value, *sent):
            route(flag[1], other, mine, key, value)
            for index, out in enumerate(sent):
                inside = flag[2] + (subs - 1 - index) < subs

                @pl.when(inside)
                def _():
                    out[:, :width] = own_key[:, cols]
                    out[:, width:] = own_value[:, cols]

                @pl.when(jnp.logical_not(inside))
                def _():
                    out[:, :width] = key[...]
                    out[:, width:] = value[...]

        both = ((rows, 2 * width), jnp.bfloat16)
        outs = small(kernel, flags, [*own, mine, other], [half, half] + [both] * (subs - 1), behind)
        return outs[:2], [around(out, subs - 1 - i) for i, out in enumerate(outs[2:])]

    per_device = KEY_VALUE_HEADS // size

    def two_parts(out, lo, block):
        block = block.reshape(-1, rows)
        if block.shape[0] < EXTRA:
            fill = jnp.zeros((EXTRA - block.shape[0], rows), jnp.float32)
            block = jnp.concatenate([block, fill], axis=0)
        high = block.astype(jnp.bfloat16)
        out[rows:, lo : lo + rows] = high
        lo += rows
        out[rows:, lo : lo + rows] = (block - high.astype(jnp.float32)).astype(jnp.bfloat16)

    def one_part(ref, lo):
        high, low = ref[rows:, lo : lo + rows], ref[rows:, lo + rows : lo + 2 * rows]
        return high.astype(jnp.float32) + low.astype(jnp.float32)

    def near_terms(dk, dv, entropies=(), behind=()):
        extra = EXTRA if entropies else 0

        def kernel(flag, *refs):
            ents, refs = refs[: len(entropies)], refs[len(entropies) :]
            for index in range(subs - 1):
                out = refs[2 * (subs - 1) + index]
                out[:rows, :width] = refs[index][...]
                out[:rows, width:] = refs[subs - 1 + index][...]
                to = lax.rem(flag[2] + index + 1, subs)
                for which, ent in enumerate(ents):
                    two_parts(out, 2 * which * rows, ent[pl.ds(to * per_device, per_device)])

        both = ((rows + extra, 2 * width), jnp.bfloat16)
        outs = small(kernel, flags, [*entropies, *dk[1:], *dv[1:]], [both] * (subs - 1), behind)
        return [around(out, index + 1 - subs) for index, out in enumerate(outs)], outs

    def collect(dk, dv, arrived, entropies=(), behind=()):
        extra = EXTRA if entropies else 0

        def kernel(flag, dk, dv, *refs):
            ents, refs = refs[: len(entropies)], refs[len(entropies) :]
            got = refs[: subs - 1]
            keep, give, own_key, own_value = refs[subs - 1 : subs + 3]
            for which, term, own in ((0, dk, own_key), (1, dv, own_value)):
                before = term[...].astype(jnp.float32)
                mine = jnp.zeros_like(before)
                for index, ref in enumerate(got):
                    part = ref[:rows, which * width : (which + 1) * width].astype(jnp.float32)
                    within = flag[2] + (subs - 1 - index) < subs
                    mine = mine + jnp.where(within, part, 0.0)
                    before = before + jnp.where(within, 0.0, part)
                own[...] = mine
                before = before.astype(jnp.bfloat16)

                @pl.when(flag[1] == which)
                def _():
                    keep[...] = before

                @pl.when(flag[1] != which)
                def _():
                    give[:rows, :] = before

            for which, ent in enumerate(ents):
                block = ent[pl.ds(flag[2] * per_device, per_device)]
                blocks = [block.reshape(-1, rows)]
                blocks += [one_part(ref, 2 * which * rows)[: blocks[0].shape[0]] for ref in got]

                @pl.when(flag[1] == which)
                def _(blocks=blocks):
                    for index, block in enumerate(blocks):
                        refs[subs + 3][index] = block

                @pl.when(flag[1] != which)
                def _(blocks=blocks):
                    for index, block in enumerate(blocks):
                        two_parts(give, 2 * index * rows, block)

        full = ((rows, width), jnp.float32)
        outs = [half, ((rows + extra, width), jnp.bfloat16), full, full]
        if entropies:
            outs.append(((subs, per_device * GROUP, rows), jnp.float32))
        return small(kernel, flags, [dk[0], dv[0], *entropies, *arrived], outs, behind)

    def finish(chunks, entropies, got):
        local, plans = [entropies, got], []
        for chunk, (own_key, own_value, pieces, mine, other) in enumerate(chunks):
            spot = 0
            for dk, dv in pieces:
                cols = slice(spot, spot + dk.shape[1])
                plans.append((len(local), cols, slice(cols.start + chunk * width, cols.stop + chunk * width)))
                local += [own_key, own_value, mine, other, dk, dv]
                spot = cols.stop
        count = per_device * GROUP

        def kernel(flag, *refs):
            ent, got = refs[:2]
            out_key, out_value, out_ent = refs[-3:]
            is_key = flag[1] == 0
            for at, cols, to in plans:
                own_key, own_value, mine, other, dk, dv = refs[at : at + 6]
                here = mine[:, cols].astype(jnp.float32)
                there = other[:, cols].astype(jnp.float32)
                for out, own, term, back in (
                    (out_key, own_key, dk, jnp.where(is_key, here, there)),
                    (out_value, own_value, dv, jnp.where(is_key, there, here)),
                ):
                    out[:, to] = (own[:, cols] + term[...] + back).astype(jnp.bfloat16)
            for index in range(subs):
                steps = 0 if index == 0 else subs - index
                source = lax.rem(flag[2] + steps, subs)
                for way, block in ((flag[1], ent[index]), (1 - flag[1], one_part(got, 2 * index * rows))):
                    for spot in range(size):

                        @pl.when(way * subs + source == spot)
                        def _(spot=spot, block=block):
                            out_ent[:, spot * rows : (spot + 1) * rows] = block[:count]

        return pl.pallas_call(
            kernel,
            grid=(1,),
            in_specs=whole(1, pltpu.SMEM) + whole(len(local)),
            out_specs=[pl.BlockSpec(keys.shape, lambda g: (0, 0))] * 2
            + [pl.BlockSpec((count, size * rows), lambda g: (0, 0))],
            out_shape=[jax.ShapeDtypeStruct(keys.shape, jnp.bfloat16)] * 2
            + [jax.ShapeDtypeStruct((count, size * rows), jnp.float32)],
            compiler_params=pltpu.CompilerParams(vmem_limit_bytes=VMEM_SMALL),
        )(in_scalars(flags), *[near_by(v) for v in local])

    per_chunk = KEY_VALUE_HEADS // CHUNKS
    got = [across(first_give)]
    flags, wide_near, own, bias, stats = first_step(
        contexts, subs, per_chunk, (queries, dout, keys, values), span_order, doc_lengths, first_give
    )
    got.append(across(later_give(own, 1, got)))
    cols = [columns(chunk) for chunk in range(CHUNKS)]
    in0 = [edge_part(own, got[0], False, odd, cols[0], [stats]) for odd in range(2)]
    edge0 = [edges(part, odd) for odd, part in enumerate(in0)]
    in1 = [edge_part(own, got[1], False, odd, cols[1]) for odd in range(2)]
    edge1 = [edges(part, odd) for odd, part in enumerate(in1)]
    mine0, theirs0 = edge_done(own, got[0], *edge0, False, cols[0])
    other0 = across(theirs0)
    stats = [stats, more_sums(wide_near, own, bias, per_chunk, per_chunk, [theirs0])]
    mine1, theirs1 = edge_done(own, got[1], *edge1, False, cols[1], [theirs0])
    other1 = across(theirs1)
    before0, near0 = window_parts(own, mine0, other0, cols[0], [theirs1, stats[1]])
    ent0, kept0, dk0, dv0 = earlier_terms(*wide_near, bias, before0, near0, stats[0], 0)
    before1, near1 = window_parts(own, mine1, other1, cols[1], [ent0])
    wide, pieces = [], []

    def rest(chunk, piece, behind):
        nonlocal wide
        before, near, kept = held[chunk]
        skip, count = sum(BEHIND[chunk][:piece]), BEHIND[chunk][piece]
        start = chunk * per_chunk
        wide, terms = the_rest(
            *wide_near, bias, before, near, own, kept, start, skip, count, wide, behind
        )
        pieces.append(terms)
        return terms[:1]

    held = [(before0, near0, kept0), (before1, near1, None)]
    arrived, sent = near_terms(dk0, dv0)
    done = rest(0, 0, sent[:1])
    keep0, give0, *own0 = collect(dk0, dv0, arrived)
    back0 = across(give0)
    ent1, kept1, dk1, dv1 = earlier_terms(
        *wide_near, bias, before1, near1, stats[1], per_chunk, [give0, *done]
    )
    held[1] = (before1, near1, kept1)
    out0 = edge_part([keep0], back0, True, 0)
    edge0 = [edges(out0, 0)]
    ents = [ent0, ent1]
    arrived, sent = near_terms(dk1, dv1, ents, [out0])
    keep1, give1, *own1, entropies = collect(dk1, dv1, arrived, ents)
    back1 = across(give1)
    edge0.append(edges(edge_part([keep0], back0, True, 1, behind=[give1]), 1))
    done = rest(0, 1, [give1])
    out1 = [edge_part([keep1], back1, True, odd, behind=done) for odd in range(2)]
    edge1 = [edges(part, odd) for odd, part in enumerate(out1)]
    mine0, theirs0 = edge_done([keep0], back0, *edge0, True, behind=out1[:1])
    other0 = across(theirs0)
    done = rest(0, 2, [theirs0])
    done = rest(1, 0, done)
    mine1, theirs1 = edge_done([keep1], back1, *edge1, True, behind=done)
    other1 = across(theirs1)
    rest(1, 1, [theirs1])
    grad_key, grad_value, entropy = finish(
        [(*own0, pieces[:3], mine0, other0), (*own1, pieces[3:], mine1, other1)], entropies, back1
    )
    return wide[0], entropy.T, wide[1], grad_key, grad_value


def solution(mesh):
    rows = P(("inner", "outer", "head"), None)
    return jax.shard_map(
        body,
        mesh=mesh,
        in_specs=(rows, rows, rows, rows, P(), P()),
        out_specs=(rows, P(("inner", "outer"), "head"), rows, rows, rows),
        check_vma=False,
    )
```

```python
import functools
import math

import jax
import jax.numpy as jnp
from jax import lax
from jax.experimental import pallas as pl
from jax.experimental.pallas import tpu as pltpu
from jax.sharding import PartitionSpec as P

QUERY_HEADS = 64
KEY_VALUE_HEADS = 8
WIDTH = 128
GROUP = QUERY_HEADS // KEY_VALUE_HEADS
SCALE = 1.0 / math.sqrt(WIDTH)
MASKED = -1e30
CONTEXT = ("inner", "outer")
CHUNKS = 2
UNROLL = 2
EXTRA = 16
BEHIND = ((1, 1, 2), (1, 3))
LOG2E = math.log2(math.e)
VMEM_SMALL = 8 * 2**20
VMEM_LARGE = 16 * 2**20
NT = (((1,), (1,)), ((), ()))
NN = (((1,), (0,)), ((), ()))


def dot(left, right, dims):
    return lax.dot_general(left, right, dims, preferred_element_type=jnp.float32)


def lanes(index, width=WIDTH):
    if isinstance(index, int):
        return slice(index * width, (index + 1) * width)
    return pl.ds(pl.multiple_of(index * width, WIDTH), width)


def group_rows(ref, g):
    return jnp.concatenate([ref[:, lanes(g * GROUP + h)] for h in range(GROUP)], axis=0)


def tiled(bias):
    return jnp.concatenate([bias] * GROUP, axis=1)


def row_sums(g, at, q_ref, do_ref, k_ref, v_ref, bias, stat_ref):
    s = dot(k_ref[:, lanes(g)], group_rows(q_ref, g), NT) + tiled(bias)
    dp = dot(v_ref[:, lanes(g)], group_rows(do_ref, g), NT)
    top = jnp.max(s, axis=0, keepdims=True)
    t = (s - top) * (SCALE * LOG2E)
    e = jnp.exp2(t)
    stat_ref[at, 0:1, :] = top
    stat_ref[at, 1:2, :] = jnp.sum(e, axis=0, keepdims=True)
    stat_ref[at, 2:3, :] = jnp.sum(e * t, axis=0, keepdims=True)
    stat_ref[at, 3:4, :] = jnp.sum(e * dp, axis=0, keepdims=True)


def first_kernel(contexts, count, *refs):
    sources, refs = refs[:4], refs[4:]
    spans_far, docs_far, refs = refs[0], refs[1], refs[2:]
    loaded, (flag, bias_ref, stat_ref, sems, spans, docs) = refs[:4], refs[4:]
    q_ref, do_ref, k_ref, v_ref = loaded
    rows = q_ref.shape[0]
    heads = k_ref.shape[1] // WIDTH
    short = [
        pltpu.make_async_copy(spans_far, spans, sems.at[2, 1]),
        pltpu.make_async_copy(docs_far, docs, sems.at[3, 1]),
    ]
    narrow = [pltpu.make_async_copy(sources[i], loaded[i], sems.at[i, 0]) for i in (2, 3)]

    def wide(g):
        cols = lanes(g, GROUP * WIDTH)
        return [
            pltpu.make_async_copy(sources[i].at[:, cols], loaded[i].at[:, cols], sems.at[i, g])
            for i in (0, 1)
        ]

    copies = short + narrow + [copy for g in range(heads) for copy in wide(g)]
    for copy in copies:
        copy.start()
    for copy in short:
        copy.wait()
    subs = bias_ref.shape[0] // rows - 1
    here, context = lax.axis_index("head"), lax.axis_index(CONTEXT)
    side, sub = here // subs, lax.rem(here, subs)
    span = spans[2 * context + side]
    first = (span * subs + sub) * rows
    flag[0] = first
    flag[1] = side
    flag[2] = sub
    flag[3] = (span == context).astype(jnp.int32)
    flag[4] = lax.rem(context, 2)
    flag[5] = (context == contexts - 1).astype(jnp.int32)
    q_pos = first + lax.broadcasted_iota(jnp.int32, (1, rows), 1)
    at = jnp.int32(0)
    start = jnp.zeros((1, rows), jnp.int32)

    def later(index, carry):
        at, start = carry
        return at + docs[index], jnp.where(at <= q_pos, at, start)

    _, start = lax.fori_loop(0, docs.shape[0], later, (at, start))
    window = bias_ref.shape[0]
    k_pos = first + rows - window + lax.broadcasted_iota(jnp.int32, (window, rows), 0)
    bias = jnp.where((k_pos >= start) & (k_pos <= q_pos), 0.0, MASKED)
    bias_ref[...] = bias
    for copy in narrow:
        copy.wait()

    def step(g, _):
        for copy in wide(g):
            copy.wait()
        row_sums(g, g, q_ref, do_ref, k_ref, v_ref, bias_ref[window - rows :, :], stat_ref)
        return 0

    lax.fori_loop(0, count, step, 0)
    for g in range(count, heads):
        for copy in wide(g):
            copy.wait()


def sums_kernel(start, count, q_ref, do_ref, k_ref, v_ref, bias_ref, stat_ref):
    last = bias_ref.shape[0] - q_ref.shape[0]

    def step(at, _):
        row_sums(start + at, at, q_ref, do_ref, k_ref, v_ref, bias_ref[last:, :], stat_ref)
        return 0

    lax.fori_loop(0, count, step, 0)


def earlier_kernel(start, count, near, q_ref, do_ref, bias_ref, first_k, first_v, *refs):
    near_refs, (stat_ref, *refs) = refs[:near], refs[near:]
    ent_ref, row_ref, p_ref, ds_ref = refs[:4]
    dk_refs, dv_refs = refs[4 : 5 + near], refs[5 + near :]
    rows = q_ref.shape[0]
    width = first_k.shape[1] // WIDTH
    window = (near + 1) * rows

    def head(at, _):
        g = start + at
        k_rows = jnp.concatenate(
            [first_k[:, lanes(at)], *[ref[:, lanes(at)] for ref in near_refs]], axis=0
        )
        v_rows = jnp.concatenate(
            [first_v[:, lanes(at)], *[ref[:, lanes(at + width)] for ref in near_refs]], axis=0
        )
        q_all, do_all = group_rows(q_ref, g), group_rows(do_ref, g)
        s = dot(k_rows, q_all, NT) + tiled(bias_ref[:window, :])
        dp = dot(v_rows, do_all, NT)
        own_top, own_total = stat_ref[at, 0:1, :], stat_ref[at, 1:2, :]
        top = jnp.maximum(jnp.max(s, axis=0, keepdims=True), own_top)
        t = (s - top) * (SCALE * LOG2E)
        e = jnp.exp2(t)
        shift = (own_top - top) * (SCALE * LOG2E)
        ratio = jnp.exp2(shift)
        total = own_total * ratio + jnp.sum(e, axis=0, keepdims=True)
        inv = 1.0 / total
        spread = (stat_ref[at, 2:3, :] + shift * own_total) * ratio
        spread = spread + jnp.sum(e * t, axis=0, keepdims=True)
        entropy = jnp.log(total) - spread * inv * math.log(2.0)
        for h in range(GROUP):
            ent_ref[at, h : h + 1, :] = entropy[:, h * rows : (h + 1) * rows]
        delta = stat_ref[at, 3:4, :] * ratio + jnp.sum(e * dp, axis=0, keepdims=True)
        delta = delta * inv
        row_ref[at, 0:1, :] = top * (SCALE * LOG2E) + jnp.log2(total)
        row_ref[at, 1:2, :] = delta
        p = e * inv
        pb = p.astype(jnp.bfloat16)
        ds = (p * (dp - delta)).astype(jnp.bfloat16)
        p_ref[at] = pb
        ds_ref[at] = ds
        dv = dot(pb, do_all, NN)
        dk = dot(ds, q_all, NN) * SCALE
        for unit in range(near + 1):
            part = slice(unit * rows, (unit + 1) * rows)
            dk_refs[unit][:, lanes(at)] = dk[part].astype(jnp.bfloat16)
            dv_refs[unit][:, lanes(at)] = dv[part].astype(jnp.bfloat16)

        return 0

    lax.fori_loop(0, count, head, 0, unroll=UNROLL)


def rest_kernel(start, skip, near, q_ref, do_ref, bias_ref, first_k, first_v, *refs):
    near_refs, (own_k, own_v), refs = refs[:near], refs[near : near + 2], refs[near + 2 :]
    row_ref, p_ref, ds_ref, att_ref, dq_ref, dk_ref, dv_ref = refs
    rows = q_ref.shape[0]
    width = first_k.shape[1] // WIDTH
    last = bias_ref.shape[0] - rows
    index = pl.program_id(0)
    at, g = skip + index, start + skip + index
    own_keys, own_values = own_k[:, lanes(g)], own_v[:, lanes(g)]
    k_rows = jnp.concatenate(
        [first_k[:, lanes(at)], *[ref[:, lanes(at)] for ref in near_refs], own_keys], axis=0
    )
    v_rows = jnp.concatenate(
        [first_v[:, lanes(at)], *[ref[:, lanes(at + width)] for ref in near_refs], own_values],
        axis=0,
    )
    q_all, do_all = group_rows(q_ref, g), group_rows(do_ref, g)
    s = dot(own_keys, q_all, NT) + tiled(bias_ref[last:, :])
    dp = dot(own_values, do_all, NT)
    p = jnp.exp2(s * (SCALE * LOG2E) - row_ref[at, 0:1, :])
    pb = p.astype(jnp.bfloat16)
    ds = (p * (dp - row_ref[at, 1:2, :])).astype(jnp.bfloat16)
    dv_ref[:, lanes(index)] = dot(pb, do_all, NN)
    dk_ref[:, lanes(index)] = dot(ds, q_all, NN) * SCALE
    p_all = jnp.concatenate([p_ref[at], pb], axis=0)
    ds_all = jnp.concatenate([ds_ref[at], ds], axis=0)
    out = dot(v_rows.T, p_all, NN).astype(jnp.bfloat16).T
    dq = (dot(k_rows.T, ds_all, NN) * SCALE).astype(jnp.bfloat16).T
    for h in range(GROUP):
        spot = slice(h * rows, (h + 1) * rows)
        att_ref[:, lanes(h)] = out[spot, :]
        dq_ref[:, lanes(h)] = dq[spot, :]


def whole(count, space=pltpu.VMEM):
    return [pl.BlockSpec(memory_space=space)] * count


def near_by(value):
    return pltpu.with_memory_space_constraint(value, pltpu.VMEM)


def in_scalars(value):
    return pltpu.with_memory_space_constraint(value, pltpu.SMEM)


def small(kernel, flags, inputs, outs, behind=()):
    def body(*refs):
        kernel(*refs[: 1 + len(inputs)], *refs[1 + len(inputs) + len(behind) :])

    return pl.pallas_call(
        body,
        in_specs=whole(1, pltpu.SMEM) + whole(len(inputs)) + whole(len(behind), pl.ANY),
        out_specs=whole(len(outs)),
        out_shape=[pltpu.VMEM(shape, dtype) for shape, dtype in outs],
        compiler_params=pltpu.CompilerParams(vmem_limit_bytes=VMEM_SMALL),
    )(in_scalars(flags), *[near_by(value) for value in inputs], *behind)


def cost(count, rows, products):
    return pl.CostEstimate(
        flops=4 * products * count * rows * GROUP * rows * WIDTH,
        bytes_accessed=1,
        transcendentals=0,
    )


def large(kernel, inputs, outs, price, behind=()):
    def body(*refs):
        kernel(*refs[: len(inputs)], *refs[len(inputs) + len(behind) :])

    return pl.pallas_call(
        body,
        in_specs=whole(len(inputs)) + whole(len(behind), pl.ANY),
        out_specs=whole(len(outs)),
        out_shape=[pltpu.VMEM(shape, dtype) for shape, dtype in outs],
        compiler_params=pltpu.CompilerParams(vmem_limit_bytes=VMEM_LARGE),
        cost_estimate=price,
    )(*[near_by(value) for value in inputs], *behind)


def far(value):
    return pltpu.with_memory_space_constraint(value, pltpu.HBM)


def first_step(contexts, subs, count, arrays, spans, docs, behind):
    rows = arrays[0].shape[0]
    heads = arrays[2].shape[1] // WIDTH

    def kernel(*refs):
        first_kernel(contexts, count, *refs[:6], *refs[7:])

    results = pl.pallas_call(
        kernel,
        in_specs=whole(7, pl.ANY),
        out_specs=whole(4) + whole(1, pltpu.SMEM) + whole(2),
        out_shape=[pltpu.VMEM(array.shape, array.dtype) for array in arrays]
        + [
            pltpu.SMEM((6,), jnp.int32),
            pltpu.VMEM(((subs + 1) * rows, rows), jnp.float32),
            pltpu.VMEM((count, 8, GROUP * rows), jnp.float32),
        ],
        scratch_shapes=[
            pltpu.SemaphoreType.DMA((4, heads)),
            pltpu.SMEM(spans.shape, jnp.int32),
            pltpu.SMEM(docs.shape, jnp.int32),
        ],
        compiler_params=pltpu.CompilerParams(vmem_limit_bytes=VMEM_LARGE),
        cost_estimate=cost(count, rows, 3),
    )(*[far(array) for array in (*arrays, spans, docs)], behind)
    return results[4], results[:2], results[2:4], results[5], results[6]


def more_sums(wide, own, bias, start, count, behind=()):
    rows = wide[0].shape[0]
    kernel = functools.partial(sums_kernel, start, count)
    outs = [((count, 8, GROUP * rows), jnp.float32)]
    return large(kernel, [*wide, *own, bias], outs, cost(count, rows, 2), behind)[0]


def earlier_terms(queries, dout, bias, before, near, stats, start, behind=()):
    rows = queries.shape[0]
    units = len(near) + 1
    count = before[0].shape[1] // WIDTH
    wide = (count, units * rows, GROUP * rows)
    outs = [
        ((count, GROUP, rows), jnp.float32),
        ((count, 8, GROUP * rows), jnp.float32),
        (wide, jnp.bfloat16),
        (wide, jnp.bfloat16),
    ] + [((rows, count * WIDTH), jnp.bfloat16)] * (2 * units)
    kernel = functools.partial(earlier_kernel, start, count, len(near))
    inputs = [queries, dout, bias, *before, *near, stats]
    results = large(kernel, inputs, outs, cost(count, rows, 4 * units), behind)
    return results[0], results[1:4], results[4 : 4 + units], results[4 + units :]


def the_rest(queries, dout, bias, before, near, own, kept, start, skip, count, earlier, behind=()):
    rows = queries.shape[0]
    block = pl.BlockSpec((rows, GROUP * WIDTH), lambda g: (0, start + skip + g))
    inputs = [near_by(v) for v in (queries, dout, bias, *before, *near, *own, *kept)]
    extra = [*earlier, *behind]

    def kernel(*refs):
        refs = refs[: len(inputs)] + refs[len(inputs) + len(extra) :]
        rest_kernel(start, skip, len(near), *refs)

    wide = jax.ShapeDtypeStruct(queries.shape, jnp.bfloat16)
    results = pl.pallas_call(
        kernel,
        grid=(count,),
        in_specs=whole(len(inputs)) + whole(len(extra), pl.ANY),
        out_specs=[block, block] + whole(2),
        out_shape=[wide, wide] + [pltpu.VMEM((rows, count * WIDTH), jnp.float32)] * 2,
        input_output_aliases={len(inputs): 0, len(inputs) + 1: 1} if earlier else {},
        compiler_params=pltpu.CompilerParams(vmem_limit_bytes=VMEM_LARGE),
        cost_estimate=cost(count, rows, 10),
    )(*inputs, *extra)
    return results[:2], results[2:]


def route(flag, first, second, one, two):
    @pl.when(flag != 0)
    def _():
        one[...] = first[...]
        two[...] = second[...]

    @pl.when(flag == 0)
    def _():
        one[...] = second[...]
        two[...] = first[...]


def body(queries, keys, values, dout, doc_lengths, span_order):
    rows = queries.shape[0]
    size = lax.axis_size("head")
    subs = size // 2
    contexts = lax.axis_size(CONTEXT)
    width = keys.shape[1] // CHUNKS
    half = ((rows, width), jnp.bfloat16)

    def across(value):
        return lax.ppermute(value, "head", [(j, (j + subs) % size) for j in range(size)])

    def around(value, steps):
        pairs = [(j, j // subs * subs + (j + steps) % subs) for j in range(size)]
        return lax.ppermute(value, "head", pairs)

    def edges(value, start):
        pairs = [(c, c + 1) for c in range(start, contexts - 1, 2)]
        return lax.ppermute(value, CONTEXT, pairs + [(b, a) for a, b in pairs])

    def columns(chunk):
        return slice(chunk * width, (chunk + 1) * width)

    def pick_in(keys, values, give, sem):
        for flag, source in ((0, values), (1, keys)):

            @pl.when(lax.axis_index("head") // subs == flag)
            def _(source=source):
                copy = pltpu.make_async_copy(source.at[:, columns(0)], give, sem)
                copy.start()
                copy.wait()

    first_give = pl.pallas_call(
        pick_in,
        in_specs=whole(2, pl.ANY),
        out_specs=whole(1)[0],
        out_shape=pltpu.VMEM(*half),
        scratch_shapes=[pltpu.SemaphoreType.DMA],
        compiler_params=pltpu.CompilerParams(vmem_limit_bytes=VMEM_SMALL),
    )(far(keys), far(values))

    def later_give(own, chunk, behind):
        def kernel(flag, key, value, give):
            for which, source in ((0, value), (1, key)):

                @pl.when(flag[1] == which)
                def _(source=source):
                    give[...] = source[:, columns(chunk)]

        return small(kernel, flags, own, [half], behind)[0]

    def out_of_step(flag, backward):
        return (flag[3] + flag[4] + (1 if backward else 0)) % 2

    def edge_part(own, got, backward, odd, cols=slice(None), behind=()):
        def kernel(flag, *refs):
            own, (got, out) = refs[:-2], refs[-2:]
            keeps = out_of_step(flag, backward) != odd
            for which, keep in enumerate(own):

                @pl.when(keeps & ((flag[1] == which) | (len(own) == 1)))
                def _(keep=keep):
                    out[...] = keep[:, cols]

            @pl.when(jnp.logical_not(keeps))
            def _():
                out[...] = got[:rows, :]

        return small(kernel, flags, [*own, got], [half], behind)[0]

    def edge_done(own, got, even, odd, backward, cols=slice(None), behind=()):
        def kernel(flag, *refs):
            own, (got, even, odd, mine, theirs) = refs[:-5], refs[-5:]
            takes_odd = (flag[3] + flag[4]) % 2
            if backward:
                takes_odd = 1 - takes_odd

            @pl.when(flag[5] == 0)
            def _():
                route(takes_odd, odd, even, mine, theirs)

            kept = (flag[3] + (1 if backward else 0)) % 2
            for which, keep in enumerate(own):

                @pl.when((flag[5] != 0) & (kept != 0) & ((flag[1] == which) | (len(own) == 1)))
                def _(keep=keep):
                    route(takes_odd, keep.at[:, cols], even, mine, theirs)

            @pl.when((flag[5] != 0) & (kept == 0))
            def _():
                route(takes_odd, got.at[:rows], even, mine, theirs)

        return small(kernel, flags, [*own, got, even, odd], [half, half], behind)

    def window_parts(own, mine, other, cols, behind=()):
        def kernel(flag, own_key, own_value, mine, other, key, value, *sent):
            route(flag[1], other, mine, key, value)
            for index, out in enumerate(sent):
                inside = flag[2] + (subs - 1 - index) < subs

                @pl.when(inside)
                def _():
                    out[:, :width] = own_key[:, cols]
                    out[:, width:] = own_value[:, cols]

                @pl.when(jnp.logical_not(inside))
                def _():
                    out[:, :width] = key[...]
                    out[:, width:] = value[...]

        both = ((rows, 2 * width), jnp.bfloat16)
        outs = small(kernel, flags, [*own, mine, other], [half, half] + [both] * (subs - 1), behind)
        return outs[:2], [around(out, subs - 1 - i) for i, out in enumerate(outs[2:])]

    per_device = KEY_VALUE_HEADS // size

    def two_parts(out, lo, block):
        block = block.reshape(-1, rows)
        if block.shape[0] < EXTRA:
            fill = jnp.zeros((EXTRA - block.shape[0], rows), jnp.float32)
            block = jnp.concatenate([block, fill], axis=0)
        high = block.astype(jnp.bfloat16)
        out[rows:, lo : lo + rows] = high
        lo += rows
        out[rows:, lo : lo + rows] = (block - high.astype(jnp.float32)).astype(jnp.bfloat16)

    def one_part(ref, lo):
        high, low = ref[rows:, lo : lo + rows], ref[rows:, lo + rows : lo + 2 * rows]
        return high.astype(jnp.float32) + low.astype(jnp.float32)

    def near_terms(dk, dv, entropies=(), behind=()):
        extra = EXTRA if entropies else 0

        def kernel(flag, *refs):
            ents, refs = refs[: len(entropies)], refs[len(entropies) :]
            for index in range(subs - 1):
                out = refs[2 * (subs - 1) + index]
                out[:rows, :width] = refs[index][...]
                out[:rows, width:] = refs[subs - 1 + index][...]
                to = lax.rem(flag[2] + index + 1, subs)
                for which, ent in enumerate(ents):
                    two_parts(out, 2 * which * rows, ent[pl.ds(to * per_device, per_device)])

        both = ((rows + extra, 2 * width), jnp.bfloat16)
        outs = small(kernel, flags, [*entropies, *dk[1:], *dv[1:]], [both] * (subs - 1), behind)
        return [around(out, index + 1 - subs) for index, out in enumerate(outs)], outs

    def collect(dk, dv, arrived, entropies=(), behind=()):
        extra = EXTRA if entropies else 0

        def kernel(flag, dk, dv, *refs):
            ents, refs = refs[: len(entropies)], refs[len(entropies) :]
            got = refs[: subs - 1]
            keep, give, own_key, own_value = refs[subs - 1 : subs + 3]
            for which, term, own in ((0, dk, own_key), (1, dv, own_value)):
                before = term[...].astype(jnp.float32)
                mine = jnp.zeros_like(before)
                for index, ref in enumerate(got):
                    part = ref[:rows, which * width : (which + 1) * width].astype(jnp.float32)
                    within = flag[2] + (subs - 1 - index) < subs
                    mine = mine + jnp.where(within, part, 0.0)
                    before = before + jnp.where(within, 0.0, part)
                own[...] = mine
                before = before.astype(jnp.bfloat16)

                @pl.when(flag[1] == which)
                def _():
                    keep[...] = before

                @pl.when(flag[1] != which)
                def _():
                    give[:rows, :] = before

            for which, ent in enumerate(ents):
                block = ent[pl.ds(flag[2] * per_device, per_device)]
                blocks = [block.reshape(-1, rows)]
                blocks += [one_part(ref, 2 * which * rows)[: blocks[0].shape[0]] for ref in got]

                @pl.when(flag[1] == which)
                def _(blocks=blocks):
                    for index, block in enumerate(blocks):
                        refs[subs + 3][index] = block

                @pl.when(flag[1] != which)
                def _(blocks=blocks):
                    for index, block in enumerate(blocks):
                        two_parts(give, 2 * index * rows, block)

        full = ((rows, width), jnp.float32)
        outs = [half, ((rows + extra, width), jnp.bfloat16), full, full]
        if entropies:
            outs.append(((subs, per_device * GROUP, rows), jnp.float32))
        return small(kernel, flags, [dk[0], dv[0], *entropies, *arrived], outs, behind)

    def finish(chunks, entropies, got):
        local, plans = [entropies, got], []
        for chunk, (own_key, own_value, pieces, mine, other) in enumerate(chunks):
            spot = 0
            for dk, dv in pieces:
                cols = slice(spot, spot + dk.shape[1])
                plans.append((len(local), cols, slice(cols.start + chunk * width, cols.stop + chunk * width)))
                local += [own_key, own_value, mine, other, dk, dv]
                spot = cols.stop
        count = per_device * GROUP

        def kernel(flag, *refs):
            ent, got = refs[:2]
            out_key, out_value, out_ent = refs[-3:]
            is_key = flag[1] == 0
            for at, cols, to in plans:
                own_key, own_value, mine, other, dk, dv = refs[at : at + 6]
                here = mine[:, cols].astype(jnp.float32)
                there = other[:, cols].astype(jnp.float32)
                for out, own, term, back in (
                    (out_key, own_key, dk, jnp.where(is_key, here, there)),
                    (out_value, own_value, dv, jnp.where(is_key, there, here)),
                ):
                    out[:, to] = (own[:, cols] + term[...] + back).astype(jnp.bfloat16)
            for index in range(subs):
                steps = 0 if index == 0 else subs - index
                source = lax.rem(flag[2] + steps, subs)
                for way, block in ((flag[1], ent[index]), (1 - flag[1], one_part(got, 2 * index * rows))):
                    for spot in range(size):

                        @pl.when(way * subs + source == spot)
                        def _(spot=spot, block=block):
                            out_ent[:, spot * rows : (spot + 1) * rows] = block[:count]

        return pl.pallas_call(
            kernel,
            grid=(1,),
            in_specs=whole(1, pltpu.SMEM) + whole(len(local)),
            out_specs=[pl.BlockSpec(keys.shape, lambda g: (0, 0))] * 2
            + [pl.BlockSpec((count, size * rows), lambda g: (0, 0))],
            out_shape=[jax.ShapeDtypeStruct(keys.shape, jnp.bfloat16)] * 2
            + [jax.ShapeDtypeStruct((count, size * rows), jnp.float32)],
            compiler_params=pltpu.CompilerParams(vmem_limit_bytes=VMEM_SMALL),
        )(in_scalars(flags), *[near_by(v) for v in local])

    per_chunk = KEY_VALUE_HEADS // CHUNKS
    got = [across(first_give)]
    flags, wide_near, own, bias, stats = first_step(
        contexts, subs, per_chunk, (queries, dout, keys, values), span_order, doc_lengths, first_give
    )
    got.append(across(later_give(own, 1, got)))
    cols = [columns(chunk) for chunk in range(CHUNKS)]
    in0 = [edge_part(own, got[0], False, odd, cols[0], [stats]) for odd in range(2)]
    edge0 = [edges(part, odd) for odd, part in enumerate(in0)]
    in1 = [edge_part(own, got[1], False, odd, cols[1]) for odd in range(2)]
    edge1 = [edges(part, odd) for odd, part in enumerate(in1)]
    mine0, theirs0 = edge_done(own, got[0], *edge0, False, cols[0])
    other0 = across(theirs0)
    stats = [stats, more_sums(wide_near, own, bias, per_chunk, per_chunk, [theirs0])]
    mine1, theirs1 = edge_done(own, got[1], *edge1, False, cols[1], [theirs0])
    other1 = across(theirs1)
    before0, near0 = window_parts(own, mine0, other0, cols[0], [theirs1, stats[1]])
    ent0, kept0, dk0, dv0 = earlier_terms(*wide_near, bias, before0, near0, stats[0], 0)
    before1, near1 = window_parts(own, mine1, other1, cols[1], [ent0])
    wide, pieces = [], []

    def rest(chunk, piece, behind):
        nonlocal wide
        before, near, kept = held[chunk]
        skip, count = sum(BEHIND[chunk][:piece]), BEHIND[chunk][piece]
        start = chunk * per_chunk
        wide, terms = the_rest(
            *wide_near, bias, before, near, own, kept, start, skip, count, wide, behind
        )
        pieces.append(terms)
        return terms[:1]

    held = [(before0, near0, kept0), (before1, near1, None)]
    arrived, sent = near_terms(dk0, dv0)
    done = rest(0, 0, sent[:1])
    keep0, give0, *own0 = collect(dk0, dv0, arrived)
    back0 = across(give0)
    ent1, kept1, dk1, dv1 = earlier_terms(
        *wide_near, bias, before1, near1, stats[1], per_chunk, [give0, *done]
    )
    held[1] = (before1, near1, kept1)
    out0 = edge_part([keep0], back0, True, 0)
    edge0 = [edges(out0, 0)]
    ents = [ent0, ent1]
    arrived, sent = near_terms(dk1, dv1, ents, [out0])
    done = rest(0, 1, sent[:1])
    keep1, give1, *own1, entropies = collect(dk1, dv1, arrived, ents, done)
    back1 = across(give1)
    edge0.append(edges(edge_part([keep0], back0, True, 1, behind=[give1]), 1))
    out1 = [edge_part([keep1], back1, True, odd) for odd in range(2)]
    edge1 = [edges(part, odd) for odd, part in enumerate(out1)]
    mine0, theirs0 = edge_done([keep0], back0, *edge0, True, behind=out1[:1])
    other0 = across(theirs0)
    done = rest(0, 2, [theirs0])
    done = rest(1, 0, done)
    mine1, theirs1 = edge_done([keep1], back1, *edge1, True, behind=done)
    other1 = across(theirs1)
    rest(1, 1, [theirs1])
    grad_key, grad_value, entropy = finish(
        [(*own0, pieces[:3], mine0, other0), (*own1, pieces[3:], mine1, other1)], entropies, back1
    )
    return wide[0], entropy.T, wide[1], grad_key, grad_value


def solution(mesh):
    rows = P(("inner", "outer", "head"), None)
    return jax.shard_map(
        body,
        mesh=mesh,
        in_specs=(rows, rows, rows, rows, P(), P()),
        out_specs=(rows, P(("inner", "outer"), "head"), rows, rows, rows),
        check_vma=False,
    )
```

```python
import functools
import math

import jax
import jax.numpy as jnp
from jax import lax
from jax.experimental import pallas as pl
from jax.experimental.pallas import tpu as pltpu
from jax.sharding import PartitionSpec as P

QUERY_HEADS = 64
KEY_VALUE_HEADS = 8
WIDTH = 128
GROUP = QUERY_HEADS // KEY_VALUE_HEADS
SCALE = 1.0 / math.sqrt(WIDTH)
MASKED = -1e30
CONTEXT = ("inner", "outer")
CHUNKS = 2
UNROLL = 2
EXTRA = 16
BEHIND = ((1, 3), (4,))
LOG2E = math.log2(math.e)
VMEM_SMALL = 8 * 2**20
VMEM_LARGE = 16 * 2**20
NT = (((1,), (1,)), ((), ()))
NN = (((1,), (0,)), ((), ()))


def dot(left, right, dims):
    return lax.dot_general(left, right, dims, preferred_element_type=jnp.float32)


def lanes(index, width=WIDTH):
    if isinstance(index, int):
        return slice(index * width, (index + 1) * width)
    return pl.ds(pl.multiple_of(index * width, WIDTH), width)


def group_rows(ref, g):
    return jnp.concatenate([ref[:, lanes(g * GROUP + h)] for h in range(GROUP)], axis=0)


def tiled(bias):
    return jnp.concatenate([bias] * GROUP, axis=1)


def row_sums(g, at, q_ref, do_ref, k_ref, v_ref, bias, stat_ref):
    s = dot(k_ref[:, lanes(g)], group_rows(q_ref, g), NT) + tiled(bias)
    dp = dot(v_ref[:, lanes(g)], group_rows(do_ref, g), NT)
    top = jnp.max(s, axis=0, keepdims=True)
    t = (s - top) * (SCALE * LOG2E)
    e = jnp.exp2(t)
    stat_ref[at, 0:1, :] = top
    stat_ref[at, 1:2, :] = jnp.sum(e, axis=0, keepdims=True)
    stat_ref[at, 2:3, :] = jnp.sum(e * t, axis=0, keepdims=True)
    stat_ref[at, 3:4, :] = jnp.sum(e * dp, axis=0, keepdims=True)


def first_kernel(contexts, count, *refs):
    sources, refs = refs[:4], refs[4:]
    spans_far, docs_far, refs = refs[0], refs[1], refs[2:]
    loaded, (flag, bias_ref, stat_ref, sems, spans, docs) = refs[:4], refs[4:]
    q_ref, do_ref, k_ref, v_ref = loaded
    rows = q_ref.shape[0]
    heads = k_ref.shape[1] // WIDTH
    short = [
        pltpu.make_async_copy(spans_far, spans, sems.at[2, 1]),
        pltpu.make_async_copy(docs_far, docs, sems.at[3, 1]),
    ]
    narrow = [pltpu.make_async_copy(sources[i], loaded[i], sems.at[i, 0]) for i in (2, 3)]

    def wide(g):
        cols = lanes(g, GROUP * WIDTH)
        return [
            pltpu.make_async_copy(sources[i].at[:, cols], loaded[i].at[:, cols], sems.at[i, g])
            for i in (0, 1)
        ]

    copies = short + narrow + [copy for g in range(heads) for copy in wide(g)]
    for copy in copies:
        copy.start()
    for copy in short:
        copy.wait()
    subs = bias_ref.shape[0] // rows - 1
    here, context = lax.axis_index("head"), lax.axis_index(CONTEXT)
    side, sub = here // subs, lax.rem(here, subs)
    span = spans[2 * context + side]
    first = (span * subs + sub) * rows
    flag[0] = first
    flag[1] = side
    flag[2] = sub
    flag[3] = (span == context).astype(jnp.int32)
    flag[4] = lax.rem(context, 2)
    flag[5] = (context == contexts - 1).astype(jnp.int32)
    q_pos = first + lax.broadcasted_iota(jnp.int32, (1, rows), 1)
    at = jnp.int32(0)
    start = jnp.zeros((1, rows), jnp.int32)

    def later(index, carry):
        at, start = carry
        return at + docs[index], jnp.where(at <= q_pos, at, start)

    _, start = lax.fori_loop(0, docs.shape[0], later, (at, start))
    window = bias_ref.shape[0]
    k_pos = first + rows - window + lax.broadcasted_iota(jnp.int32, (window, rows), 0)
    bias = jnp.where((k_pos >= start) & (k_pos <= q_pos), 0.0, MASKED)
    bias_ref[...] = bias
    for copy in narrow:
        copy.wait()

    def step(g, _):
        for copy in wide(g):
            copy.wait()
        row_sums(g, g, q_ref, do_ref, k_ref, v_ref, bias_ref[window - rows :, :], stat_ref)
        return 0

    lax.fori_loop(0, count, step, 0)
    for g in range(count, heads):
        for copy in wide(g):
            copy.wait()


def sums_kernel(start, count, q_ref, do_ref, k_ref, v_ref, bias_ref, stat_ref):
    last = bias_ref.shape[0] - q_ref.shape[0]

    def step(at, _):
        row_sums(start + at, at, q_ref, do_ref, k_ref, v_ref, bias_ref[last:, :], stat_ref)
        return 0

    lax.fori_loop(0, count, step, 0)


def earlier_kernel(start, count, near, q_ref, do_ref, bias_ref, first_k, first_v, *refs):
    near_refs, (stat_ref, *refs) = refs[:near], refs[near:]
    ent_ref, row_ref, p_ref, ds_ref = refs[:4]
    dk_refs, dv_refs = refs[4 : 5 + near], refs[5 + near :]
    rows = q_ref.shape[0]
    width = first_k.shape[1] // WIDTH
    window = (near + 1) * rows

    def head(at, _):
        g = start + at
        k_rows = jnp.concatenate(
            [first_k[:, lanes(at)], *[ref[:, lanes(at)] for ref in near_refs]], axis=0
        )
        v_rows = jnp.concatenate(
            [first_v[:, lanes(at)], *[ref[:, lanes(at + width)] for ref in near_refs]], axis=0
        )
        q_all, do_all = group_rows(q_ref, g), group_rows(do_ref, g)
        s = dot(k_rows, q_all, NT) + tiled(bias_ref[:window, :])
        dp = dot(v_rows, do_all, NT)
        own_top, own_total = stat_ref[at, 0:1, :], stat_ref[at, 1:2, :]
        top = jnp.maximum(jnp.max(s, axis=0, keepdims=True), own_top)
        t = (s - top) * (SCALE * LOG2E)
        e = jnp.exp2(t)
        shift = (own_top - top) * (SCALE * LOG2E)
        ratio = jnp.exp2(shift)
        total = own_total * ratio + jnp.sum(e, axis=0, keepdims=True)
        inv = 1.0 / total
        spread = (stat_ref[at, 2:3, :] + shift * own_total) * ratio
        spread = spread + jnp.sum(e * t, axis=0, keepdims=True)
        entropy = jnp.log(total) - spread * inv * math.log(2.0)
        for h in range(GROUP):
            ent_ref[at, h : h + 1, :] = entropy[:, h * rows : (h + 1) * rows]
        delta = stat_ref[at, 3:4, :] * ratio + jnp.sum(e * dp, axis=0, keepdims=True)
        delta = delta * inv
        row_ref[at, 0:1, :] = top * (SCALE * LOG2E) + jnp.log2(total)
        row_ref[at, 1:2, :] = delta
        p = e * inv
        pb = p.astype(jnp.bfloat16)
        ds = (p * (dp - delta)).astype(jnp.bfloat16)
        p_ref[at] = pb
        ds_ref[at] = ds
        dv = dot(pb, do_all, NN)
        dk = dot(ds, q_all, NN) * SCALE
        for unit in range(near + 1):
            part = slice(unit * rows, (unit + 1) * rows)
            dk_refs[unit][:, lanes(at)] = dk[part].astype(jnp.bfloat16)
            dv_refs[unit][:, lanes(at)] = dv[part].astype(jnp.bfloat16)

        return 0

    lax.fori_loop(0, count, head, 0, unroll=UNROLL)


def rest_kernel(start, skip, near, q_ref, do_ref, bias_ref, first_k, first_v, *refs):
    near_refs, (own_k, own_v), refs = refs[:near], refs[near : near + 2], refs[near + 2 :]
    row_ref, p_ref, ds_ref, att_ref, dq_ref, dk_ref, dv_ref = refs
    rows = q_ref.shape[0]
    width = first_k.shape[1] // WIDTH
    last = bias_ref.shape[0] - rows
    index = pl.program_id(0)
    at, g = skip + index, start + skip + index
    own_keys, own_values = own_k[:, lanes(g)], own_v[:, lanes(g)]
    k_rows = jnp.concatenate(
        [first_k[:, lanes(at)], *[ref[:, lanes(at)] for ref in near_refs], own_keys], axis=0
    )
    v_rows = jnp.concatenate(
        [first_v[:, lanes(at)], *[ref[:, lanes(at + width)] for ref in near_refs], own_values],
        axis=0,
    )
    q_all, do_all = group_rows(q_ref, g), group_rows(do_ref, g)
    s = dot(own_keys, q_all, NT) + tiled(bias_ref[last:, :])
    dp = dot(own_values, do_all, NT)
    p = jnp.exp2(s * (SCALE * LOG2E) - row_ref[at, 0:1, :])
    pb = p.astype(jnp.bfloat16)
    ds = (p * (dp - row_ref[at, 1:2, :])).astype(jnp.bfloat16)
    dv_ref[:, lanes(index)] = dot(pb, do_all, NN)
    dk_ref[:, lanes(index)] = dot(ds, q_all, NN) * SCALE
    p_all = jnp.concatenate([p_ref[at], pb], axis=0)
    ds_all = jnp.concatenate([ds_ref[at], ds], axis=0)
    out = dot(v_rows.T, p_all, NN).astype(jnp.bfloat16).T
    dq = (dot(k_rows.T, ds_all, NN) * SCALE).astype(jnp.bfloat16).T
    for h in range(GROUP):
        spot = slice(h * rows, (h + 1) * rows)
        att_ref[:, lanes(h)] = out[spot, :]
        dq_ref[:, lanes(h)] = dq[spot, :]


def whole(count, space=pltpu.VMEM):
    return [pl.BlockSpec(memory_space=space)] * count


def near_by(value):
    return pltpu.with_memory_space_constraint(value, pltpu.VMEM)


def in_scalars(value):
    return pltpu.with_memory_space_constraint(value, pltpu.SMEM)


def small(kernel, flags, inputs, outs, behind=(), price=None):
    def body(*refs):
        kernel(*refs[: 1 + len(inputs)], *refs[1 + len(inputs) + len(behind) :])

    return pl.pallas_call(
        body,
        in_specs=whole(1, pltpu.SMEM) + whole(len(inputs)) + whole(len(behind), pl.ANY),
        out_specs=whole(len(outs)),
        out_shape=[pltpu.VMEM(shape, dtype) for shape, dtype in outs],
        compiler_params=pltpu.CompilerParams(vmem_limit_bytes=VMEM_SMALL),
        cost_estimate=price,
    )(in_scalars(flags), *[near_by(value) for value in inputs], *behind)


def cost(count, rows, products):
    return pl.CostEstimate(
        flops=4 * products * count * rows * GROUP * rows * WIDTH,
        bytes_accessed=1,
        transcendentals=0,
    )


def large(kernel, inputs, outs, price, behind=()):
    def body(*refs):
        kernel(*refs[: len(inputs)], *refs[len(inputs) + len(behind) :])

    return pl.pallas_call(
        body,
        in_specs=whole(len(inputs)) + whole(len(behind), pl.ANY),
        out_specs=whole(len(outs)),
        out_shape=[pltpu.VMEM(shape, dtype) for shape, dtype in outs],
        compiler_params=pltpu.CompilerParams(vmem_limit_bytes=VMEM_LARGE),
        cost_estimate=price,
    )(*[near_by(value) for value in inputs], *behind)


def far(value):
    return pltpu.with_memory_space_constraint(value, pltpu.HBM)


def first_step(contexts, subs, count, arrays, spans, docs, behind):
    rows = arrays[0].shape[0]
    heads = arrays[2].shape[1] // WIDTH

    def kernel(*refs):
        first_kernel(contexts, count, *refs[:6], *refs[7:])

    results = pl.pallas_call(
        kernel,
        in_specs=whole(7, pl.ANY),
        out_specs=whole(4) + whole(1, pltpu.SMEM) + whole(2),
        out_shape=[pltpu.VMEM(array.shape, array.dtype) for array in arrays]
        + [
            pltpu.SMEM((6,), jnp.int32),
            pltpu.VMEM(((subs + 1) * rows, rows), jnp.float32),
            pltpu.VMEM((count, 8, GROUP * rows), jnp.float32),
        ],
        scratch_shapes=[
            pltpu.SemaphoreType.DMA((4, heads)),
            pltpu.SMEM(spans.shape, jnp.int32),
            pltpu.SMEM(docs.shape, jnp.int32),
        ],
        compiler_params=pltpu.CompilerParams(vmem_limit_bytes=VMEM_LARGE),
        cost_estimate=cost(count, rows, 3),
    )(*[far(array) for array in (*arrays, spans, docs)], behind)
    return results[4], results[:2], results[2:4], results[5], results[6]


def more_sums(wide, own, bias, start, count, behind=()):
    rows = wide[0].shape[0]
    kernel = functools.partial(sums_kernel, start, count)
    outs = [((count, 8, GROUP * rows), jnp.float32)]
    return large(kernel, [*wide, *own, bias], outs, cost(count, rows, 2), behind)[0]


def earlier_terms(queries, dout, bias, before, near, stats, start, behind=()):
    rows = queries.shape[0]
    units = len(near) + 1
    count = before[0].shape[1] // WIDTH
    wide = (count, units * rows, GROUP * rows)
    outs = [
        ((count, GROUP, rows), jnp.float32),
        ((count, 8, GROUP * rows), jnp.float32),
        (wide, jnp.bfloat16),
        (wide, jnp.bfloat16),
    ] + [((rows, count * WIDTH), jnp.bfloat16)] * (2 * units)
    kernel = functools.partial(earlier_kernel, start, count, len(near))
    inputs = [queries, dout, bias, *before, *near, stats]
    results = large(kernel, inputs, outs, cost(count, rows, 4 * units), behind)
    return results[0], results[1:4], results[4 : 4 + units], results[4 + units :]


def the_rest(queries, dout, bias, before, near, own, kept, start, skip, count, earlier, behind=()):
    rows = queries.shape[0]
    block = pl.BlockSpec((rows, GROUP * WIDTH), lambda g: (0, start + skip + g))
    inputs = [near_by(v) for v in (queries, dout, bias, *before, *near, *own, *kept)]
    extra = [*earlier, *behind]

    def kernel(*refs):
        refs = refs[: len(inputs)] + refs[len(inputs) + len(extra) :]
        rest_kernel(start, skip, len(near), *refs)

    wide = jax.ShapeDtypeStruct(queries.shape, jnp.bfloat16)
    results = pl.pallas_call(
        kernel,
        grid=(count,),
        in_specs=whole(len(inputs)) + whole(len(extra), pl.ANY),
        out_specs=[block, block] + whole(2),
        out_shape=[wide, wide] + [pltpu.VMEM((rows, count * WIDTH), jnp.float32)] * 2,
        input_output_aliases={len(inputs): 0, len(inputs) + 1: 1} if earlier else {},
        compiler_params=pltpu.CompilerParams(vmem_limit_bytes=VMEM_LARGE),
        cost_estimate=cost(count, rows, 10),
    )(*inputs, *extra)
    return results[:2], results[2:]


def route(flag, first, second, one, two):
    @pl.when(flag != 0)
    def _():
        one[...] = first[...]
        two[...] = second[...]

    @pl.when(flag == 0)
    def _():
        one[...] = second[...]
        two[...] = first[...]


def body(queries, keys, values, dout, doc_lengths, span_order):
    rows = queries.shape[0]
    size = lax.axis_size("head")
    subs = size // 2
    contexts = lax.axis_size(CONTEXT)
    width = keys.shape[1] // CHUNKS
    half = ((rows, width), jnp.bfloat16)

    def across(value):
        return lax.ppermute(value, "head", [(j, (j + subs) % size) for j in range(size)])

    def around(value, steps):
        pairs = [(j, j // subs * subs + (j + steps) % subs) for j in range(size)]
        return lax.ppermute(value, "head", pairs)

    def edges(value, start):
        pairs = [(c, c + 1) for c in range(start, contexts - 1, 2)]
        return lax.ppermute(value, CONTEXT, pairs + [(b, a) for a, b in pairs])

    def columns(chunk):
        return slice(chunk * width, (chunk + 1) * width)

    def pick_in(keys, values, give, sem):
        for flag, source in ((0, values), (1, keys)):

            @pl.when(lax.axis_index("head") // subs == flag)
            def _(source=source):
                copy = pltpu.make_async_copy(source.at[:, columns(0)], give, sem)
                copy.start()
                copy.wait()

    first_give = pl.pallas_call(
        pick_in,
        in_specs=whole(2, pl.ANY),
        out_specs=whole(1)[0],
        out_shape=pltpu.VMEM(*half),
        scratch_shapes=[pltpu.SemaphoreType.DMA],
        compiler_params=pltpu.CompilerParams(vmem_limit_bytes=VMEM_SMALL),
    )(far(keys), far(values))

    def later_give(own, chunk, behind):
        def kernel(flag, key, value, give):
            for which, source in ((0, value), (1, key)):

                @pl.when(flag[1] == which)
                def _(source=source):
                    give[...] = source[:, columns(chunk)]

        return small(kernel, flags, own, [half], behind)[0]

    def out_of_step(flag, backward):
        return (flag[3] + flag[4] + (1 if backward else 0)) % 2

    def edge_part(own, got, backward, odd, cols=slice(None), behind=(), price=None):
        def kernel(flag, *refs):
            own, (got, out) = refs[:-2], refs[-2:]
            keeps = out_of_step(flag, backward) != odd
            for which, keep in enumerate(own):

                @pl.when(keeps & ((flag[1] == which) | (len(own) == 1)))
                def _(keep=keep):
                    out[...] = keep[:, cols]

            @pl.when(jnp.logical_not(keeps))
            def _():
                out[...] = got[:rows, :]

        return small(kernel, flags, [*own, got], [half], behind, price)[0]

    def edge_done(own, got, even, odd, backward, cols=slice(None), behind=()):
        def kernel(flag, *refs):
            own, (got, even, odd, mine, theirs) = refs[:-5], refs[-5:]
            takes_odd = (flag[3] + flag[4]) % 2
            if backward:
                takes_odd = 1 - takes_odd

            @pl.when(flag[5] == 0)
            def _():
                route(takes_odd, odd, even, mine, theirs)

            kept = (flag[3] + (1 if backward else 0)) % 2
            for which, keep in enumerate(own):

                @pl.when((flag[5] != 0) & (kept != 0) & ((flag[1] == which) | (len(own) == 1)))
                def _(keep=keep):
                    route(takes_odd, keep.at[:, cols], even, mine, theirs)

            @pl.when((flag[5] != 0) & (kept == 0))
            def _():
                route(takes_odd, got.at[:rows], even, mine, theirs)

        return small(kernel, flags, [*own, got, even, odd], [half, half], behind)

    def window_parts(own, mine, other, cols, behind=()):
        def kernel(flag, own_key, own_value, mine, other, key, value, *sent):
            route(flag[1], other, mine, key, value)
            for index, out in enumerate(sent):
                inside = flag[2] + (subs - 1 - index) < subs

                @pl.when(inside)
                def _():
                    out[:, :width] = own_key[:, cols]
                    out[:, width:] = own_value[:, cols]

                @pl.when(jnp.logical_not(inside))
                def _():
                    out[:, :width] = key[...]
                    out[:, width:] = value[...]

        both = ((rows, 2 * width), jnp.bfloat16)
        outs = small(kernel, flags, [*own, mine, other], [half, half] + [both] * (subs - 1), behind)
        return outs[:2], [around(out, subs - 1 - i) for i, out in enumerate(outs[2:])]

    per_device = KEY_VALUE_HEADS // size

    def two_parts(out, lo, block):
        block = block.reshape(-1, rows)
        if block.shape[0] < EXTRA:
            fill = jnp.zeros((EXTRA - block.shape[0], rows), jnp.float32)
            block = jnp.concatenate([block, fill], axis=0)
        high = block.astype(jnp.bfloat16)
        out[rows:, lo : lo + rows] = high
        lo += rows
        out[rows:, lo : lo + rows] = (block - high.astype(jnp.float32)).astype(jnp.bfloat16)

    def one_part(ref, lo):
        high, low = ref[rows:, lo : lo + rows], ref[rows:, lo + rows : lo + 2 * rows]
        return high.astype(jnp.float32) + low.astype(jnp.float32)

    def near_terms(dk, dv, entropies=(), behind=()):
        extra = EXTRA if entropies else 0

        def kernel(flag, *refs):
            ents, refs = refs[: len(entropies)], refs[len(entropies) :]
            for index in range(subs - 1):
                out = refs[2 * (subs - 1) + index]
                out[:rows, :width] = refs[index][...]
                out[:rows, width:] = refs[subs - 1 + index][...]
                to = lax.rem(flag[2] + index + 1, subs)
                for which, ent in enumerate(ents):
                    two_parts(out, 2 * which * rows, ent[pl.ds(to * per_device, per_device)])

        both = ((rows + extra, 2 * width), jnp.bfloat16)
        outs = small(kernel, flags, [*entropies, *dk[1:], *dv[1:]], [both] * (subs - 1), behind)
        return [around(out, index + 1 - subs) for index, out in enumerate(outs)], outs

    def collect(dk, dv, arrived, entropies=(), behind=()):
        extra = EXTRA if entropies else 0

        def kernel(flag, dk, dv, *refs):
            ents, refs = refs[: len(entropies)], refs[len(entropies) :]
            got = refs[: subs - 1]
            keep, give, own_key, own_value = refs[subs - 1 : subs + 3]
            for which, term, own in ((0, dk, own_key), (1, dv, own_value)):
                before = term[...].astype(jnp.float32)
                mine = jnp.zeros_like(before)
                for index, ref in enumerate(got):
                    part = ref[:rows, which * width : (which + 1) * width].astype(jnp.float32)
                    within = flag[2] + (subs - 1 - index) < subs
                    mine = mine + jnp.where(within, part, 0.0)
                    before = before + jnp.where(within, 0.0, part)
                own[...] = mine
                before = before.astype(jnp.bfloat16)

                @pl.when(flag[1] == which)
                def _():
                    keep[...] = before

                @pl.when(flag[1] != which)
                def _():
                    give[:rows, :] = before

            for which, ent in enumerate(ents):
                block = ent[pl.ds(flag[2] * per_device, per_device)]
                blocks = [block.reshape(-1, rows)]
                blocks += [one_part(ref, 2 * which * rows)[: blocks[0].shape[0]] for ref in got]

                @pl.when(flag[1] == which)
                def _(blocks=blocks):
                    for index, block in enumerate(blocks):
                        refs[subs + 3][index] = block

                @pl.when(flag[1] != which)
                def _(blocks=blocks):
                    for index, block in enumerate(blocks):
                        two_parts(give, 2 * index * rows, block)

        full = ((rows, width), jnp.float32)
        outs = [half, ((rows + extra, width), jnp.bfloat16), full, full]
        if entropies:
            outs.append(((subs, per_device * GROUP, rows), jnp.float32))
        return small(kernel, flags, [dk[0], dv[0], *entropies, *arrived], outs, behind)

    def finish(chunks, entropies, got):
        local, plans = [entropies, got], []
        for chunk, (own_key, own_value, pieces, mine, other) in enumerate(chunks):
            spot = 0
            for dk, dv in pieces:
                cols = slice(spot, spot + dk.shape[1])
                plans.append((len(local), cols, slice(cols.start + chunk * width, cols.stop + chunk * width)))
                local += [own_key, own_value, mine, other, dk, dv]
                spot = cols.stop
        count = per_device * GROUP

        def kernel(flag, *refs):
            ent, got = refs[:2]
            out_key, out_value, out_ent = refs[-3:]
            is_key = flag[1] == 0
            for at, cols, to in plans:
                own_key, own_value, mine, other, dk, dv = refs[at : at + 6]
                here = mine[:, cols].astype(jnp.float32)
                there = other[:, cols].astype(jnp.float32)
                for out, own, term, back in (
                    (out_key, own_key, dk, jnp.where(is_key, here, there)),
                    (out_value, own_value, dv, jnp.where(is_key, there, here)),
                ):
                    out[:, to] = (own[:, cols] + term[...] + back).astype(jnp.bfloat16)
            for index in range(subs):
                steps = 0 if index == 0 else subs - index
                source = lax.rem(flag[2] + steps, subs)
                for way, block in ((flag[1], ent[index]), (1 - flag[1], one_part(got, 2 * index * rows))):
                    for spot in range(size):

                        @pl.when(way * subs + source == spot)
                        def _(spot=spot, block=block):
                            out_ent[:, spot * rows : (spot + 1) * rows] = block[:count]

        return pl.pallas_call(
            kernel,
            grid=(1,),
            in_specs=whole(1, pltpu.SMEM) + whole(len(local)),
            out_specs=[pl.BlockSpec(keys.shape, lambda g: (0, 0))] * 2
            + [pl.BlockSpec((count, size * rows), lambda g: (0, 0))],
            out_shape=[jax.ShapeDtypeStruct(keys.shape, jnp.bfloat16)] * 2
            + [jax.ShapeDtypeStruct((count, size * rows), jnp.float32)],
            compiler_params=pltpu.CompilerParams(vmem_limit_bytes=VMEM_SMALL),
        )(in_scalars(flags), *[near_by(v) for v in local])

    def taken(value, behind=(), price=None):
        def kernel(flag, value, out):
            out[...] = value[...]

        return small(kernel, flags, [value], [half], behind, price)[0]

    per_chunk = KEY_VALUE_HEADS // CHUNKS
    got = [across(first_give)]
    flags, wide_near, own, bias, stats = first_step(
        contexts, subs, per_chunk, (queries, dout, keys, values), span_order, doc_lengths, first_give
    )
    got.append(across(later_give(own, 1, got)))
    cols = [columns(chunk) for chunk in range(CHUNKS)]
    in0 = [edge_part(own, got[0], False, odd, cols[0], [stats]) for odd in range(2)]
    edge0 = [edges(part, odd) for odd, part in enumerate(in0)]
    in1 = [edge_part(own, got[1], False, odd, cols[1]) for odd in range(2)]
    edge1 = [edges(part, odd) for odd, part in enumerate(in1)]
    mine0, theirs0 = edge_done(own, got[0], *edge0, False, cols[0])
    other0 = across(theirs0)
    stats = [stats, more_sums(wide_near, own, bias, per_chunk, per_chunk, [theirs0])]
    mine1, theirs1 = edge_done(own, got[1], *edge1, False, cols[1], [theirs0])
    other1 = across(theirs1)
    before0, near0 = window_parts(own, mine0, other0, cols[0], [theirs1, stats[1]])
    ent0, kept0, dk0, dv0 = earlier_terms(*wide_near, bias, before0, near0, stats[0], 0)
    before1, near1 = window_parts(own, mine1, other1, cols[1], [ent0])
    wide, pieces = [], []

    def rest(chunk, piece, behind):
        nonlocal wide
        before, near, kept = held[chunk]
        skip, count = sum(BEHIND[chunk][:piece]), BEHIND[chunk][piece]
        start = chunk * per_chunk
        wide, terms = the_rest(
            *wide_near, bias, before, near, own, kept, start, skip, count, wide, behind
        )
        pieces.append(terms)
        return terms[:1]

    held = [(before0, near0, kept0), (before1, near1, None)]
    arrived, sent = near_terms(dk0, dv0)
    done = rest(0, 0, sent[:1])
    keep0, give0, *own0 = collect(dk0, dv0, arrived)
    back0 = across(give0)
    ent1, kept1, dk1, dv1 = earlier_terms(
        *wide_near, bias, before1, near1, stats[1], per_chunk, [give0, *done]
    )
    held[1] = (before1, near1, kept1)
    out0 = edge_part([keep0], back0, True, 0)
    edge0 = [edges(out0, 0)]
    ents = [ent0, ent1]
    arrived, sent = near_terms(dk1, dv1, ents, [out0])
    keep1, give1, *own1, entropies = collect(dk1, dv1, arrived, ents)
    back1 = across(give1)
    edge0.append(edges(edge_part([keep0], back0, True, 1, behind=[give1], price=cost(4, rows, 10)), 1))
    out1 = [edge_part([keep1], back1, True, odd) for odd in range(2)]
    edge1 = [edges(part, odd) for odd, part in enumerate(out1)]
    mine0, theirs0 = edge_done([keep0], back0, *edge0, True, behind=out1[:1])
    other0 = across(theirs0)
    done = rest(0, 1, [theirs0])
    edge1[0] = taken(taken(edge1[0], done), price=cost(4, rows, 10))
    mine1, theirs1 = edge_done([keep1], back1, *edge1, True, behind=done)
    other1 = across(theirs1)
    rest(1, 0, [theirs1])
    grad_key, grad_value, entropy = finish(
        [(*own0, pieces[:2], mine0, other0), (*own1, pieces[2:], mine1, other1)], entropies, back1
    )
    return wide[0], entropy.T, wide[1], grad_key, grad_value


def solution(mesh):
    rows = P(("inner", "outer", "head"), None)
    return jax.shard_map(
        body,
        mesh=mesh,
        in_specs=(rows, rows, rows, rows, P(), P()),
        out_specs=(rows, P(("inner", "outer"), "head"), rows, rows, rows),
        check_vma=False,
    )
```

```python
import functools
import math

import jax
import jax.numpy as jnp
from jax import lax
from jax.experimental import pallas as pl
from jax.experimental.pallas import tpu as pltpu
from jax.sharding import PartitionSpec as P

QUERY_HEADS = 64
KEY_VALUE_HEADS = 8
WIDTH = 128
GROUP = QUERY_HEADS // KEY_VALUE_HEADS
SCALE = 1.0 / math.sqrt(WIDTH)
MASKED = -1e30
CONTEXT = ("inner", "outer")
CHUNKS = 2
UNROLL = 2
EXTRA = 16
BEHIND = ((1, 3), (4,))
LOG2E = math.log2(math.e)
VMEM_SMALL = 8 * 2**20
VMEM_LARGE = 16 * 2**20
NT = (((1,), (1,)), ((), ()))
NN = (((1,), (0,)), ((), ()))


def dot(left, right, dims):
    return lax.dot_general(left, right, dims, preferred_element_type=jnp.float32)


def lanes(index, width=WIDTH):
    if isinstance(index, int):
        return slice(index * width, (index + 1) * width)
    return pl.ds(pl.multiple_of(index * width, WIDTH), width)


def group_rows(ref, g):
    return jnp.concatenate([ref[:, lanes(g * GROUP + h)] for h in range(GROUP)], axis=0)


def tiled(bias):
    return jnp.concatenate([bias] * GROUP, axis=1)


def row_sums(g, at, q_ref, do_ref, k_ref, v_ref, bias, stat_ref):
    s = dot(k_ref[:, lanes(g)], group_rows(q_ref, g), NT) + tiled(bias)
    dp = dot(v_ref[:, lanes(g)], group_rows(do_ref, g), NT)
    top = jnp.max(s, axis=0, keepdims=True)
    t = (s - top) * (SCALE * LOG2E)
    e = jnp.exp2(t)
    stat_ref[at, 0:1, :] = top
    stat_ref[at, 1:2, :] = jnp.sum(e, axis=0, keepdims=True)
    stat_ref[at, 2:3, :] = jnp.sum(e * t, axis=0, keepdims=True)
    stat_ref[at, 3:4, :] = jnp.sum(e * dp, axis=0, keepdims=True)


def first_kernel(contexts, count, *refs):
    sources, refs = refs[:4], refs[4:]
    spans_far, docs_far, refs = refs[0], refs[1], refs[2:]
    loaded, (flag, bias_ref, stat_ref, sems, spans, docs) = refs[:4], refs[4:]
    q_ref, do_ref, k_ref, v_ref = loaded
    rows = q_ref.shape[0]
    heads = k_ref.shape[1] // WIDTH
    short = [
        pltpu.make_async_copy(spans_far, spans, sems.at[2, 1]),
        pltpu.make_async_copy(docs_far, docs, sems.at[3, 1]),
    ]
    narrow = [pltpu.make_async_copy(sources[i], loaded[i], sems.at[i, 0]) for i in (2, 3)]

    def wide(g):
        cols = lanes(g, GROUP * WIDTH)
        return [
            pltpu.make_async_copy(sources[i].at[:, cols], loaded[i].at[:, cols], sems.at[i, g])
            for i in (0, 1)
        ]

    copies = short + narrow + [copy for g in range(heads) for copy in wide(g)]
    for copy in copies:
        copy.start()
    for copy in short:
        copy.wait()
    subs = bias_ref.shape[0] // rows - 1
    here, context = lax.axis_index("head"), lax.axis_index(CONTEXT)
    side, sub = here // subs, lax.rem(here, subs)
    span = spans[2 * context + side]
    first = (span * subs + sub) * rows
    flag[0] = first
    flag[1] = side
    flag[2] = sub
    flag[3] = (span == context).astype(jnp.int32)
    flag[4] = lax.rem(context, 2)
    flag[5] = (context == contexts - 1).astype(jnp.int32)
    q_pos = first + lax.broadcasted_iota(jnp.int32, (1, rows), 1)
    at = jnp.int32(0)
    start = jnp.zeros((1, rows), jnp.int32)

    def later(index, carry):
        at, start = carry
        return at + docs[index], jnp.where(at <= q_pos, at, start)

    _, start = lax.fori_loop(0, docs.shape[0], later, (at, start))
    window = bias_ref.shape[0]
    k_pos = first + rows - window + lax.broadcasted_iota(jnp.int32, (window, rows), 0)
    bias = jnp.where((k_pos >= start) & (k_pos <= q_pos), 0.0, MASKED)
    bias_ref[...] = bias
    for copy in narrow:
        copy.wait()

    def step(g, _):
        for copy in wide(g):
            copy.wait()
        row_sums(g, g, q_ref, do_ref, k_ref, v_ref, bias_ref[window - rows :, :], stat_ref)
        return 0

    lax.fori_loop(0, count, step, 0)
    for g in range(count, heads):
        for copy in wide(g):
            copy.wait()


def sums_kernel(start, count, q_ref, do_ref, k_ref, v_ref, bias_ref, stat_ref):
    last = bias_ref.shape[0] - q_ref.shape[0]

    def step(at, _):
        row_sums(start + at, at, q_ref, do_ref, k_ref, v_ref, bias_ref[last:, :], stat_ref)
        return 0

    lax.fori_loop(0, count, step, 0)


def earlier_kernel(start, count, near, q_ref, do_ref, bias_ref, first_k, first_v, *refs):
    near_refs, (stat_ref, *refs) = refs[:near], refs[near:]
    ent_ref, row_ref, p_ref, ds_ref = refs[:4]
    dk_refs, dv_refs = refs[4 : 5 + near], refs[5 + near :]
    rows = q_ref.shape[0]
    width = first_k.shape[1] // WIDTH
    window = (near + 1) * rows

    def head(at, _):
        g = start + at
        k_rows = jnp.concatenate(
            [first_k[:, lanes(at)], *[ref[:, lanes(at)] for ref in near_refs]], axis=0
        )
        v_rows = jnp.concatenate(
            [first_v[:, lanes(at)], *[ref[:, lanes(at + width)] for ref in near_refs]], axis=0
        )
        q_all, do_all = group_rows(q_ref, g), group_rows(do_ref, g)
        s = dot(k_rows, q_all, NT) + tiled(bias_ref[:window, :])
        dp = dot(v_rows, do_all, NT)
        own_top, own_total = stat_ref[at, 0:1, :], stat_ref[at, 1:2, :]
        top = jnp.maximum(jnp.max(s, axis=0, keepdims=True), own_top)
        t = (s - top) * (SCALE * LOG2E)
        e = jnp.exp2(t)
        shift = (own_top - top) * (SCALE * LOG2E)
        ratio = jnp.exp2(shift)
        total = own_total * ratio + jnp.sum(e, axis=0, keepdims=True)
        inv = 1.0 / total
        spread = (stat_ref[at, 2:3, :] + shift * own_total) * ratio
        spread = spread + jnp.sum(e * t, axis=0, keepdims=True)
        entropy = jnp.log(total) - spread * inv * math.log(2.0)
        for h in range(GROUP):
            ent_ref[at, h : h + 1, :] = entropy[:, h * rows : (h + 1) * rows]
        delta = stat_ref[at, 3:4, :] * ratio + jnp.sum(e * dp, axis=0, keepdims=True)
        delta = delta * inv
        row_ref[at, 0:1, :] = top * (SCALE * LOG2E) + jnp.log2(total)
        row_ref[at, 1:2, :] = delta
        p = e * inv
        pb = p.astype(jnp.bfloat16)
        ds = (p * (dp - delta)).astype(jnp.bfloat16)
        p_ref[at] = pb
        ds_ref[at] = ds
        dv = dot(pb, do_all, NN)
        dk = dot(ds, q_all, NN) * SCALE
        for unit in range(near + 1):
            part = slice(unit * rows, (unit + 1) * rows)
            dk_refs[unit][:, lanes(at)] = dk[part].astype(jnp.bfloat16)
            dv_refs[unit][:, lanes(at)] = dv[part].astype(jnp.bfloat16)

        return 0

    lax.fori_loop(0, count, head, 0, unroll=UNROLL)


def rest_kernel(start, skip, near, q_ref, do_ref, bias_ref, first_k, first_v, *refs):
    near_refs, (own_k, own_v), refs = refs[:near], refs[near : near + 2], refs[near + 2 :]
    row_ref, p_ref, ds_ref, att_ref, dq_ref, dk_ref, dv_ref = refs
    rows = q_ref.shape[0]
    width = first_k.shape[1] // WIDTH
    last = bias_ref.shape[0] - rows
    index = pl.program_id(0)
    at, g = skip + index, start + skip + index
    own_keys, own_values = own_k[:, lanes(g)], own_v[:, lanes(g)]
    k_rows = jnp.concatenate(
        [first_k[:, lanes(at)], *[ref[:, lanes(at)] for ref in near_refs], own_keys], axis=0
    )
    v_rows = jnp.concatenate(
        [first_v[:, lanes(at)], *[ref[:, lanes(at + width)] for ref in near_refs], own_values],
        axis=0,
    )
    q_all, do_all = group_rows(q_ref, g), group_rows(do_ref, g)
    s = dot(own_keys, q_all, NT) + tiled(bias_ref[last:, :])
    dp = dot(own_values, do_all, NT)
    p = jnp.exp2(s * (SCALE * LOG2E) - row_ref[at, 0:1, :])
    pb = p.astype(jnp.bfloat16)
    ds = (p * (dp - row_ref[at, 1:2, :])).astype(jnp.bfloat16)
    dv_ref[:, lanes(index)] = dot(pb, do_all, NN)
    dk_ref[:, lanes(index)] = dot(ds, q_all, NN) * SCALE
    p_all = jnp.concatenate([p_ref[at], pb], axis=0)
    ds_all = jnp.concatenate([ds_ref[at], ds], axis=0)
    out = dot(v_rows.T, p_all, NN).astype(jnp.bfloat16).T
    dq = (dot(k_rows.T, ds_all, NN) * SCALE).astype(jnp.bfloat16).T
    for h in range(GROUP):
        spot = slice(h * rows, (h + 1) * rows)
        att_ref[:, lanes(h)] = out[spot, :]
        dq_ref[:, lanes(h)] = dq[spot, :]


def whole(count, space=pltpu.VMEM):
    return [pl.BlockSpec(memory_space=space)] * count


def near_by(value):
    return pltpu.with_memory_space_constraint(value, pltpu.VMEM)


def in_scalars(value):
    return pltpu.with_memory_space_constraint(value, pltpu.SMEM)


def small(kernel, flags, inputs, outs, behind=(), price=None):
    def body(*refs):
        kernel(*refs[: 1 + len(inputs)], *refs[1 + len(inputs) + len(behind) :])

    return pl.pallas_call(
        body,
        in_specs=whole(1, pltpu.SMEM) + whole(len(inputs)) + whole(len(behind), pl.ANY),
        out_specs=whole(len(outs)),
        out_shape=[pltpu.VMEM(shape, dtype) for shape, dtype in outs],
        compiler_params=pltpu.CompilerParams(vmem_limit_bytes=VMEM_SMALL),
        cost_estimate=price,
    )(in_scalars(flags), *[near_by(value) for value in inputs], *behind)


def cost(count, rows, products):
    return pl.CostEstimate(
        flops=4 * products * count * rows * GROUP * rows * WIDTH,
        bytes_accessed=1,
        transcendentals=0,
    )


def large(kernel, inputs, outs, price, behind=()):
    def body(*refs):
        kernel(*refs[: len(inputs)], *refs[len(inputs) + len(behind) :])

    return pl.pallas_call(
        body,
        in_specs=whole(len(inputs)) + whole(len(behind), pl.ANY),
        out_specs=whole(len(outs)),
        out_shape=[pltpu.VMEM(shape, dtype) for shape, dtype in outs],
        compiler_params=pltpu.CompilerParams(vmem_limit_bytes=VMEM_LARGE),
        cost_estimate=price,
    )(*[near_by(value) for value in inputs], *behind)


def far(value):
    return pltpu.with_memory_space_constraint(value, pltpu.HBM)


def first_step(contexts, subs, count, arrays, spans, docs, behind):
    rows = arrays[0].shape[0]
    heads = arrays[2].shape[1] // WIDTH

    def kernel(*refs):
        first_kernel(contexts, count, *refs[:6], *refs[7:])

    results = pl.pallas_call(
        kernel,
        in_specs=whole(7, pl.ANY),
        out_specs=whole(4) + whole(1, pltpu.SMEM) + whole(2),
        out_shape=[pltpu.VMEM(array.shape, array.dtype) for array in arrays]
        + [
            pltpu.SMEM((6,), jnp.int32),
            pltpu.VMEM(((subs + 1) * rows, rows), jnp.float32),
            pltpu.VMEM((count, 8, GROUP * rows), jnp.float32),
        ],
        scratch_shapes=[
            pltpu.SemaphoreType.DMA((4, heads)),
            pltpu.SMEM(spans.shape, jnp.int32),
            pltpu.SMEM(docs.shape, jnp.int32),
        ],
        compiler_params=pltpu.CompilerParams(vmem_limit_bytes=VMEM_LARGE),
        cost_estimate=cost(count, rows, 3),
    )(*[far(array) for array in (*arrays, spans, docs)], behind)
    return results[4], results[:2], results[2:4], results[5], results[6]


def more_sums(wide, own, bias, start, count, behind=()):
    rows = wide[0].shape[0]
    kernel = functools.partial(sums_kernel, start, count)
    outs = [((count, 8, GROUP * rows), jnp.float32)]
    return large(kernel, [*wide, *own, bias], outs, cost(count, rows, 2), behind)[0]


def earlier_terms(queries, dout, bias, before, near, stats, start, behind=()):
    rows = queries.shape[0]
    units = len(near) + 1
    count = before[0].shape[1] // WIDTH
    wide = (count, units * rows, GROUP * rows)
    outs = [
        ((count, GROUP, rows), jnp.float32),
        ((count, 8, GROUP * rows), jnp.float32),
        (wide, jnp.bfloat16),
        (wide, jnp.bfloat16),
    ] + [((rows, count * WIDTH), jnp.bfloat16)] * (2 * units)
    kernel = functools.partial(earlier_kernel, start, count, len(near))
    inputs = [queries, dout, bias, *before, *near, stats]
    results = large(kernel, inputs, outs, cost(count, rows, 4 * units), behind)
    return results[0], results[1:4], results[4 : 4 + units], results[4 + units :]


def the_rest(queries, dout, bias, before, near, own, kept, start, skip, count, earlier, behind=()):
    rows = queries.shape[0]
    block = pl.BlockSpec((rows, GROUP * WIDTH), lambda g: (0, start + skip + g))
    inputs = [near_by(v) for v in (queries, dout, bias, *before, *near, *own, *kept)]
    extra = [*earlier, *behind]

    def kernel(*refs):
        refs = refs[: len(inputs)] + refs[len(inputs) + len(extra) :]
        rest_kernel(start, skip, len(near), *refs)

    wide = jax.ShapeDtypeStruct(queries.shape, jnp.bfloat16)
    results = pl.pallas_call(
        kernel,
        grid=(count,),
        in_specs=whole(len(inputs)) + whole(len(extra), pl.ANY),
        out_specs=[block, block] + whole(2),
        out_shape=[wide, wide] + [pltpu.VMEM((rows, count * WIDTH), jnp.float32)] * 2,
        input_output_aliases={len(inputs): 0, len(inputs) + 1: 1} if earlier else {},
        compiler_params=pltpu.CompilerParams(vmem_limit_bytes=VMEM_LARGE),
        cost_estimate=cost(count, rows, 5),
    )(*inputs, *extra)
    return results[:2], results[2:]


def route(flag, first, second, one, two):
    @pl.when(flag != 0)
    def _():
        one[...] = first[...]
        two[...] = second[...]

    @pl.when(flag == 0)
    def _():
        one[...] = second[...]
        two[...] = first[...]


def body(queries, keys, values, dout, doc_lengths, span_order):
    rows = queries.shape[0]
    size = lax.axis_size("head")
    subs = size // 2
    contexts = lax.axis_size(CONTEXT)
    width = keys.shape[1] // CHUNKS
    half = ((rows, width), jnp.bfloat16)

    def across(value):
        return lax.ppermute(value, "head", [(j, (j + subs) % size) for j in range(size)])

    def around(value, steps):
        pairs = [(j, j // subs * subs + (j + steps) % subs) for j in range(size)]
        return lax.ppermute(value, "head", pairs)

    def edges(value, start):
        pairs = [(c, c + 1) for c in range(start, contexts - 1, 2)]
        return lax.ppermute(value, CONTEXT, pairs + [(b, a) for a, b in pairs])

    def columns(chunk):
        return slice(chunk * width, (chunk + 1) * width)

    def pick_in(keys, values, give, sem):
        for flag, source in ((0, values), (1, keys)):

            @pl.when(lax.axis_index("head") // subs == flag)
            def _(source=source):
                copy = pltpu.make_async_copy(source.at[:, columns(0)], give, sem)
                copy.start()
                copy.wait()

    first_give = pl.pallas_call(
        pick_in,
        in_specs=whole(2, pl.ANY),
        out_specs=whole(1)[0],
        out_shape=pltpu.VMEM(*half),
        scratch_shapes=[pltpu.SemaphoreType.DMA],
        compiler_params=pltpu.CompilerParams(vmem_limit_bytes=VMEM_SMALL),
    )(far(keys), far(values))

    def later_give(own, chunk, behind):
        def kernel(flag, key, value, give):
            for which, source in ((0, value), (1, key)):

                @pl.when(flag[1] == which)
                def _(source=source):
                    give[...] = source[:, columns(chunk)]

        return small(kernel, flags, own, [half], behind)[0]

    def out_of_step(flag, backward):
        return (flag[3] + flag[4] + (1 if backward else 0)) % 2

    def edge_part(own, got, backward, odd, cols=slice(None), behind=(), price=None):
        def kernel(flag, *refs):
            own, (got, out) = refs[:-2], refs[-2:]
            keeps = out_of_step(flag, backward) != odd
            for which, keep in enumerate(own):

                @pl.when(keeps & ((flag[1] == which) | (len(own) == 1)))
                def _(keep=keep):
                    out[...] = keep[:, cols]

            @pl.when(jnp.logical_not(keeps))
            def _():
                out[...] = got[:rows, :]

        return small(kernel, flags, [*own, got], [half], behind, price)[0]

    def edge_done(own, got, even, odd, backward, cols=slice(None), behind=()):
        def kernel(flag, *refs):
            own, (got, even, odd, mine, theirs) = refs[:-5], refs[-5:]
            takes_odd = (flag[3] + flag[4]) % 2
            if backward:
                takes_odd = 1 - takes_odd

            @pl.when(flag[5] == 0)
            def _():
                route(takes_odd, odd, even, mine, theirs)

            kept = (flag[3] + (1 if backward else 0)) % 2
            for which, keep in enumerate(own):

                @pl.when((flag[5] != 0) & (kept != 0) & ((flag[1] == which) | (len(own) == 1)))
                def _(keep=keep):
                    route(takes_odd, keep.at[:, cols], even, mine, theirs)

            @pl.when((flag[5] != 0) & (kept == 0))
            def _():
                route(takes_odd, got.at[:rows], even, mine, theirs)

        return small(kernel, flags, [*own, got, even, odd], [half, half], behind)

    def window_parts(own, mine, other, cols, behind=()):
        def kernel(flag, own_key, own_value, mine, other, key, value, *sent):
            route(flag[1], other, mine, key, value)
            for index, out in enumerate(sent):
                inside = flag[2] + (subs - 1 - index) < subs

                @pl.when(inside)
                def _():
                    out[:, :width] = own_key[:, cols]
                    out[:, width:] = own_value[:, cols]

                @pl.when(jnp.logical_not(inside))
                def _():
                    out[:, :width] = key[...]
                    out[:, width:] = value[...]

        both = ((rows, 2 * width), jnp.bfloat16)
        outs = small(kernel, flags, [*own, mine, other], [half, half] + [both] * (subs - 1), behind)
        return outs[:2], [around(out, subs - 1 - i) for i, out in enumerate(outs[2:])]

    per_device = KEY_VALUE_HEADS // size

    def two_parts(out, lo, block):
        block = block.reshape(-1, rows)
        if block.shape[0] < EXTRA:
            fill = jnp.zeros((EXTRA - block.shape[0], rows), jnp.float32)
            block = jnp.concatenate([block, fill], axis=0)
        high = block.astype(jnp.bfloat16)
        out[rows:, lo : lo + rows] = high
        lo += rows
        out[rows:, lo : lo + rows] = (block - high.astype(jnp.float32)).astype(jnp.bfloat16)

    def one_part(ref, lo):
        high, low = ref[rows:, lo : lo + rows], ref[rows:, lo + rows : lo + 2 * rows]
        return high.astype(jnp.float32) + low.astype(jnp.float32)

    def near_terms(dk, dv, entropies=(), behind=()):
        extra = EXTRA if entropies else 0

        def kernel(flag, *refs):
            ents, refs = refs[: len(entropies)], refs[len(entropies) :]
            for index in range(subs - 1):
                out = refs[2 * (subs - 1) + index]
                out[:rows, :width] = refs[index][...]
                out[:rows, width:] = refs[subs - 1 + index][...]
                to = lax.rem(flag[2] + index + 1, subs)
                for which, ent in enumerate(ents):
                    two_parts(out, 2 * which * rows, ent[pl.ds(to * per_device, per_device)])

        both = ((rows + extra, 2 * width), jnp.bfloat16)
        outs = small(kernel, flags, [*entropies, *dk[1:], *dv[1:]], [both] * (subs - 1), behind)
        return [around(out, index + 1 - subs) for index, out in enumerate(outs)], outs

    def collect(dk, dv, arrived, entropies=(), behind=()):
        extra = EXTRA if entropies else 0

        def kernel(flag, dk, dv, *refs):
            ents, refs = refs[: len(entropies)], refs[len(entropies) :]
            got = refs[: subs - 1]
            keep, give, own_key, own_value = refs[subs - 1 : subs + 3]
            for which, term, own in ((0, dk, own_key), (1, dv, own_value)):
                before = term[...].astype(jnp.float32)
                mine = jnp.zeros_like(before)
                for index, ref in enumerate(got):
                    part = ref[:rows, which * width : (which + 1) * width].astype(jnp.float32)
                    within = flag[2] + (subs - 1 - index) < subs
                    mine = mine + jnp.where(within, part, 0.0)
                    before = before + jnp.where(within, 0.0, part)
                own[...] = mine
                before = before.astype(jnp.bfloat16)

                @pl.when(flag[1] == which)
                def _():
                    keep[...] = before

                @pl.when(flag[1] != which)
                def _():
                    give[:rows, :] = before

            for which, ent in enumerate(ents):
                block = ent[pl.ds(flag[2] * per_device, per_device)]
                blocks = [block.reshape(-1, rows)]
                blocks += [one_part(ref, 2 * which * rows)[: blocks[0].shape[0]] for ref in got]

                @pl.when(flag[1] == which)
                def _(blocks=blocks):
                    for index, block in enumerate(blocks):
                        refs[subs + 3][index] = block

                @pl.when(flag[1] != which)
                def _(blocks=blocks):
                    for index, block in enumerate(blocks):
                        two_parts(give, 2 * index * rows, block)

        full = ((rows, width), jnp.float32)
        outs = [half, ((rows + extra, width), jnp.bfloat16), full, full]
        if entropies:
            outs.append(((subs, per_device * GROUP, rows), jnp.float32))
        return small(kernel, flags, [dk[0], dv[0], *entropies, *arrived], outs, behind)

    def finish(chunks, entropies, got):
        local, plans = [entropies, got], []
        for chunk, (own_key, own_value, pieces, mine, other) in enumerate(chunks):
            spot = 0
            for dk, dv in pieces:
                cols = slice(spot, spot + dk.shape[1])
                plans.append((len(local), cols, slice(cols.start + chunk * width, cols.stop + chunk * width)))
                local += [own_key, own_value, mine, other, dk, dv]
                spot = cols.stop
        count = per_device * GROUP

        def kernel(flag, *refs):
            ent, got = refs[:2]
            out_key, out_value, out_ent = refs[-3:]
            is_key = flag[1] == 0
            for at, cols, to in plans:
                own_key, own_value, mine, other, dk, dv = refs[at : at + 6]
                here = mine[:, cols].astype(jnp.float32)
                there = other[:, cols].astype(jnp.float32)
                for out, own, term, back in (
                    (out_key, own_key, dk, jnp.where(is_key, here, there)),
                    (out_value, own_value, dv, jnp.where(is_key, there, here)),
                ):
                    out[:, to] = (own[:, cols] + term[...] + back).astype(jnp.bfloat16)
            for index in range(subs):
                steps = 0 if index == 0 else subs - index
                source = lax.rem(flag[2] + steps, subs)
                for way, block in ((flag[1], ent[index]), (1 - flag[1], one_part(got, 2 * index * rows))):
                    for spot in range(size):

                        @pl.when(way * subs + source == spot)
                        def _(spot=spot, block=block):
                            out_ent[:, spot * rows : (spot + 1) * rows] = block[:count]

        return pl.pallas_call(
            kernel,
            grid=(1,),
            in_specs=whole(1, pltpu.SMEM) + whole(len(local)),
            out_specs=[pl.BlockSpec(keys.shape, lambda g: (0, 0))] * 2
            + [pl.BlockSpec((count, size * rows), lambda g: (0, 0))],
            out_shape=[jax.ShapeDtypeStruct(keys.shape, jnp.bfloat16)] * 2
            + [jax.ShapeDtypeStruct((count, size * rows), jnp.float32)],
            compiler_params=pltpu.CompilerParams(vmem_limit_bytes=VMEM_SMALL),
        )(in_scalars(flags), *[near_by(v) for v in local])

    def taken(value, behind=(), price=None):
        def kernel(flag, value, out):
            out[...] = value[...]

        return small(kernel, flags, [value], [half], behind, price)[0]

    per_chunk = KEY_VALUE_HEADS // CHUNKS
    got = [across(first_give)]
    flags, wide_near, own, bias, stats = first_step(
        contexts, subs, per_chunk, (queries, dout, keys, values), span_order, doc_lengths, first_give
    )
    got.append(across(later_give(own, 1, got)))
    cols = [columns(chunk) for chunk in range(CHUNKS)]
    in0 = [edge_part(own, got[0], False, odd, cols[0], [stats]) for odd in range(2)]
    edge0 = [edges(part, odd) for odd, part in enumerate(in0)]
    in1 = [edge_part(own, got[1], False, odd, cols[1]) for odd in range(2)]
    edge1 = [edges(part, odd) for odd, part in enumerate(in1)]
    mine0, theirs0 = edge_done(own, got[0], *edge0, False, cols[0])
    other0 = across(theirs0)
    stats = [stats, more_sums(wide_near, own, bias, per_chunk, per_chunk, [theirs0])]
    mine1, theirs1 = edge_done(own, got[1], *edge1, False, cols[1], [theirs0])
    other1 = across(theirs1)
    before0, near0 = window_parts(own, mine0, other0, cols[0], [theirs1, stats[1]])
    ent0, kept0, dk0, dv0 = earlier_terms(*wide_near, bias, before0, near0, stats[0], 0)
    before1, near1 = window_parts(own, mine1, other1, cols[1], [ent0])
    wide, pieces = [], []

    def rest(chunk, piece, behind):
        nonlocal wide
        before, near, kept = held[chunk]
        skip, count = sum(BEHIND[chunk][:piece]), BEHIND[chunk][piece]
        start = chunk * per_chunk
        wide, terms = the_rest(
            *wide_near, bias, before, near, own, kept, start, skip, count, wide, behind
        )
        pieces.append(terms)
        return terms[:1]

    held = [(before0, near0, kept0), (before1, near1, None)]
    arrived, sent = near_terms(dk0, dv0)
    done = rest(0, 0, sent[:1])
    keep0, give0, *own0 = collect(dk0, dv0, arrived)
    back0 = across(give0)
    ent1, kept1, dk1, dv1 = earlier_terms(
        *wide_near, bias, before1, near1, stats[1], per_chunk, [give0, *done]
    )
    held[1] = (before1, near1, kept1)
    out0 = edge_part([keep0], back0, True, 0)
    edge0 = [edges(out0, 0)]
    ents = [ent0, ent1]
    arrived, sent = near_terms(dk1, dv1, ents, [out0])
    keep1, give1, *own1, entropies = collect(dk1, dv1, arrived, ents)
    back1 = across(give1)
    edge0.append(edges(edge_part([keep0], back0, True, 1, behind=[give1], price=cost(4, rows, 10)), 1))
    out1 = [edge_part([keep1], back1, True, odd) for odd in range(2)]
    edge1 = [edges(part, odd) for odd, part in enumerate(out1)]
    mine0, theirs0 = edge_done([keep0], back0, *edge0, True, behind=out1[:1])
    other0 = across(theirs0)
    done = rest(0, 1, [theirs0])
    edge1[0] = taken(taken(edge1[0], done), price=cost(4, rows, 10))
    mine1, theirs1 = edge_done([keep1], back1, *edge1, True, behind=done)
    other1 = across(theirs1)
    rest(1, 0, [theirs1])
    grad_key, grad_value, entropy = finish(
        [(*own0, pieces[:2], mine0, other0), (*own1, pieces[2:], mine1, other1)], entropies, back1
    )
    return wide[0], entropy.T, wide[1], grad_key, grad_value


def solution(mesh):
    rows = P(("inner", "outer", "head"), None)
    return jax.shard_map(
        body,
        mesh=mesh,
        in_specs=(rows, rows, rows, rows, P(), P()),
        out_specs=(rows, P(("inner", "outer"), "head"), rows, rows, rows),
        check_vma=False,
    )
```

```python
import functools
import math

import jax
import jax.numpy as jnp
from jax import lax
from jax.experimental import pallas as pl
from jax.experimental.pallas import tpu as pltpu
from jax.sharding import PartitionSpec as P

QUERY_HEADS = 64
KEY_VALUE_HEADS = 8
WIDTH = 128
GROUP = QUERY_HEADS // KEY_VALUE_HEADS
SCALE = 1.0 / math.sqrt(WIDTH)
MASKED = -1e30
CONTEXT = ("inner", "outer")
CHUNKS = 2
UNROLL = 2
EXTRA = 16
BEHIND = (((3, 1, 1), (0, 3, 1)), ((0, 4, 2),))
LOG2E = math.log2(math.e)
VMEM_SMALL = 8 * 2**20
VMEM_LARGE = 16 * 2**20
NT = (((1,), (1,)), ((), ()))
NN = (((1,), (0,)), ((), ()))


def dot(left, right, dims):
    return lax.dot_general(left, right, dims, preferred_element_type=jnp.float32)


def lanes(index, width=WIDTH):
    if isinstance(index, int):
        return slice(index * width, (index + 1) * width)
    return pl.ds(pl.multiple_of(index * width, WIDTH), width)


def group_rows(ref, g):
    return jnp.concatenate([ref[:, lanes(g * GROUP + h)] for h in range(GROUP)], axis=0)


def tiled(bias):
    return jnp.concatenate([bias] * GROUP, axis=1)


def row_sums(g, at, q_ref, do_ref, k_ref, v_ref, bias, stat_ref):
    s = dot(k_ref[:, lanes(g)], group_rows(q_ref, g), NT) + tiled(bias)
    dp = dot(v_ref[:, lanes(g)], group_rows(do_ref, g), NT)
    top = jnp.max(s, axis=0, keepdims=True)
    t = (s - top) * (SCALE * LOG2E)
    e = jnp.exp2(t)
    stat_ref[at, 0:1, :] = top
    stat_ref[at, 1:2, :] = jnp.sum(e, axis=0, keepdims=True)
    stat_ref[at, 2:3, :] = jnp.sum(e * t, axis=0, keepdims=True)
    stat_ref[at, 3:4, :] = jnp.sum(e * dp, axis=0, keepdims=True)


def first_kernel(contexts, count, *refs):
    sources, refs = refs[:4], refs[4:]
    spans_far, docs_far, refs = refs[0], refs[1], refs[2:]
    loaded, (flag, bias_ref, stat_ref, sems, spans, docs) = refs[:4], refs[4:]
    q_ref, do_ref, k_ref, v_ref = loaded
    rows = q_ref.shape[0]
    heads = k_ref.shape[1] // WIDTH
    short = [
        pltpu.make_async_copy(spans_far, spans, sems.at[2, 1]),
        pltpu.make_async_copy(docs_far, docs, sems.at[3, 1]),
    ]
    narrow = [pltpu.make_async_copy(sources[i], loaded[i], sems.at[i, 0]) for i in (2, 3)]

    def wide(g):
        cols = lanes(g, GROUP * WIDTH)
        return [
            pltpu.make_async_copy(sources[i].at[:, cols], loaded[i].at[:, cols], sems.at[i, g])
            for i in (0, 1)
        ]

    copies = short + narrow + [copy for g in range(heads) for copy in wide(g)]
    for copy in copies:
        copy.start()
    for copy in short:
        copy.wait()
    subs = bias_ref.shape[0] // rows - 1
    here, context = lax.axis_index("head"), lax.axis_index(CONTEXT)
    side, sub = here // subs, lax.rem(here, subs)
    span = spans[2 * context + side]
    first = (span * subs + sub) * rows
    flag[0] = first
    flag[1] = side
    flag[2] = sub
    flag[3] = (span == context).astype(jnp.int32)
    flag[4] = lax.rem(context, 2)
    flag[5] = (context == contexts - 1).astype(jnp.int32)
    q_pos = first + lax.broadcasted_iota(jnp.int32, (1, rows), 1)
    at = jnp.int32(0)
    start = jnp.zeros((1, rows), jnp.int32)

    def later(index, carry):
        at, start = carry
        return at + docs[index], jnp.where(at <= q_pos, at, start)

    _, start = lax.fori_loop(0, docs.shape[0], later, (at, start))
    window = bias_ref.shape[0]
    k_pos = first + rows - window + lax.broadcasted_iota(jnp.int32, (window, rows), 0)
    bias = jnp.where((k_pos >= start) & (k_pos <= q_pos), 0.0, MASKED)
    bias_ref[...] = bias
    for copy in narrow:
        copy.wait()

    def step(g, _):
        for copy in wide(g):
            copy.wait()
        row_sums(g, g, q_ref, do_ref, k_ref, v_ref, bias_ref[window - rows :, :], stat_ref)
        return 0

    lax.fori_loop(0, count, step, 0)
    for g in range(count, heads):
        for copy in wide(g):
            copy.wait()


def sums_kernel(start, count, q_ref, do_ref, k_ref, v_ref, bias_ref, stat_ref):
    last = bias_ref.shape[0] - q_ref.shape[0]

    def step(at, _):
        row_sums(start + at, at, q_ref, do_ref, k_ref, v_ref, bias_ref[last:, :], stat_ref)
        return 0

    lax.fori_loop(0, count, step, 0)


def earlier_kernel(start, count, near, q_ref, do_ref, bias_ref, first_k, first_v, *refs):
    near_refs, (stat_ref, *refs) = refs[:near], refs[near:]
    ent_ref, row_ref, p_ref, ds_ref = refs[:4]
    dk_refs, dv_refs = refs[4 : 5 + near], refs[5 + near :]
    rows = q_ref.shape[0]
    width = first_k.shape[1] // WIDTH
    window = (near + 1) * rows

    def head(at, _):
        g = start + at
        k_rows = jnp.concatenate(
            [first_k[:, lanes(at)], *[ref[:, lanes(at)] for ref in near_refs]], axis=0
        )
        v_rows = jnp.concatenate(
            [first_v[:, lanes(at)], *[ref[:, lanes(at + width)] for ref in near_refs]], axis=0
        )
        q_all, do_all = group_rows(q_ref, g), group_rows(do_ref, g)
        s = dot(k_rows, q_all, NT) + tiled(bias_ref[:window, :])
        dp = dot(v_rows, do_all, NT)
        own_top, own_total = stat_ref[at, 0:1, :], stat_ref[at, 1:2, :]
        top = jnp.maximum(jnp.max(s, axis=0, keepdims=True), own_top)
        t = (s - top) * (SCALE * LOG2E)
        e = jnp.exp2(t)
        shift = (own_top - top) * (SCALE * LOG2E)
        ratio = jnp.exp2(shift)
        total = own_total * ratio + jnp.sum(e, axis=0, keepdims=True)
        inv = 1.0 / total
        spread = (stat_ref[at, 2:3, :] + shift * own_total) * ratio
        spread = spread + jnp.sum(e * t, axis=0, keepdims=True)
        entropy = jnp.log(total) - spread * inv * math.log(2.0)
        for h in range(GROUP):
            ent_ref[at, h : h + 1, :] = entropy[:, h * rows : (h + 1) * rows]
        delta = stat_ref[at, 3:4, :] * ratio + jnp.sum(e * dp, axis=0, keepdims=True)
        delta = delta * inv
        row_ref[at, 0:1, :] = top * (SCALE * LOG2E) + jnp.log2(total)
        row_ref[at, 1:2, :] = delta
        p = e * inv
        pb = p.astype(jnp.bfloat16)
        ds = (p * (dp - delta)).astype(jnp.bfloat16)
        p_ref[at] = pb
        ds_ref[at] = ds
        dv = dot(pb, do_all, NN)
        dk = dot(ds, q_all, NN) * SCALE
        for unit in range(near + 1):
            part = slice(unit * rows, (unit + 1) * rows)
            dk_refs[unit][:, lanes(at)] = dk[part].astype(jnp.bfloat16)
            dv_refs[unit][:, lanes(at)] = dv[part].astype(jnp.bfloat16)

        return 0

    lax.fori_loop(0, count, head, 0, unroll=UNROLL)


def rest_kernel(start, skip, per, near, q_ref, do_ref, bias_ref, first_k, first_v, *refs):
    near_refs, (own_k, own_v), refs = refs[:near], refs[near : near + 2], refs[near + 2 :]
    row_ref, p_ref, ds_ref, att_ref, dq_ref, dk_ref, dv_ref = refs
    rows = q_ref.shape[0]
    width = first_k.shape[1] // WIDTH
    last = bias_ref.shape[0] - rows
    for step in range(per):
        index = pl.program_id(0) * per + step
        at, g = skip + index, start + skip + index
        own_keys, own_values = own_k[:, lanes(g)], own_v[:, lanes(g)]
        k_rows = jnp.concatenate(
            [first_k[:, lanes(at)], *[ref[:, lanes(at)] for ref in near_refs], own_keys], axis=0
        )
        v_rows = jnp.concatenate(
            [first_v[:, lanes(at)], *[ref[:, lanes(at + width)] for ref in near_refs], own_values],
            axis=0,
        )
        q_all, do_all = group_rows(q_ref, g), group_rows(do_ref, g)
        s = dot(own_keys, q_all, NT) + tiled(bias_ref[last:, :])
        dp = dot(own_values, do_all, NT)
        p = jnp.exp2(s * (SCALE * LOG2E) - row_ref[at, 0:1, :])
        pb = p.astype(jnp.bfloat16)
        ds = (p * (dp - row_ref[at, 1:2, :])).astype(jnp.bfloat16)
        dv_ref[:, lanes(index)] = dot(pb, do_all, NN)
        dk_ref[:, lanes(index)] = dot(ds, q_all, NN) * SCALE
        p_all = jnp.concatenate([p_ref[at], pb], axis=0)
        ds_all = jnp.concatenate([ds_ref[at], ds], axis=0)
        out = dot(v_rows.T, p_all, NN).T.astype(jnp.bfloat16)
        dq = (dot(k_rows.T, ds_all, NN) * SCALE).T.astype(jnp.bfloat16)
        for h in range(GROUP):
            spot = slice(h * rows, (h + 1) * rows)
            att_ref[:, lanes(step * GROUP + h)] = out[spot, :]
            dq_ref[:, lanes(step * GROUP + h)] = dq[spot, :]


def whole(count, space=pltpu.VMEM):
    return [pl.BlockSpec(memory_space=space)] * count


def near_by(value):
    return pltpu.with_memory_space_constraint(value, pltpu.VMEM)


def in_scalars(value):
    return pltpu.with_memory_space_constraint(value, pltpu.SMEM)


def small(kernel, flags, inputs, outs, behind=(), price=None):
    def body(*refs):
        kernel(*refs[: 1 + len(inputs)], *refs[1 + len(inputs) + len(behind) :])

    return pl.pallas_call(
        body,
        in_specs=whole(1, pltpu.SMEM) + whole(len(inputs)) + whole(len(behind), pl.ANY),
        out_specs=whole(len(outs)),
        out_shape=[pltpu.VMEM(shape, dtype) for shape, dtype in outs],
        compiler_params=pltpu.CompilerParams(vmem_limit_bytes=VMEM_SMALL),
        cost_estimate=price,
    )(in_scalars(flags), *[near_by(value) for value in inputs], *behind)


def cost(count, rows, products):
    return pl.CostEstimate(
        flops=4 * products * count * rows * GROUP * rows * WIDTH,
        bytes_accessed=1,
        transcendentals=0,
    )


def large(kernel, inputs, outs, price, behind=()):
    def body(*refs):
        kernel(*refs[: len(inputs)], *refs[len(inputs) + len(behind) :])

    return pl.pallas_call(
        body,
        in_specs=whole(len(inputs)) + whole(len(behind), pl.ANY),
        out_specs=whole(len(outs)),
        out_shape=[pltpu.VMEM(shape, dtype) for shape, dtype in outs],
        compiler_params=pltpu.CompilerParams(vmem_limit_bytes=VMEM_LARGE),
        cost_estimate=price,
    )(*[near_by(value) for value in inputs], *behind)


def far(value):
    return pltpu.with_memory_space_constraint(value, pltpu.HBM)


def first_step(contexts, subs, count, arrays, spans, docs, behind):
    rows = arrays[0].shape[0]
    heads = arrays[2].shape[1] // WIDTH

    def kernel(*refs):
        first_kernel(contexts, count, *refs[:6], *refs[7:])

    results = pl.pallas_call(
        kernel,
        in_specs=whole(7, pl.ANY),
        out_specs=whole(4) + whole(1, pltpu.SMEM) + whole(2),
        out_shape=[pltpu.VMEM(array.shape, array.dtype) for array in arrays]
        + [
            pltpu.SMEM((6,), jnp.int32),
            pltpu.VMEM(((subs + 1) * rows, rows), jnp.float32),
            pltpu.VMEM((count, 8, GROUP * rows), jnp.float32),
        ],
        scratch_shapes=[
            pltpu.SemaphoreType.DMA((4, heads)),
            pltpu.SMEM(spans.shape, jnp.int32),
            pltpu.SMEM(docs.shape, jnp.int32),
        ],
        compiler_params=pltpu.CompilerParams(vmem_limit_bytes=VMEM_LARGE),
        cost_estimate=cost(count, rows, 3),
    )(*[far(array) for array in (*arrays, spans, docs)], behind)
    return results[4], results[:2], results[2:4], results[5], results[6]


def more_sums(wide, own, bias, start, count, behind=()):
    rows = wide[0].shape[0]
    kernel = functools.partial(sums_kernel, start, count)
    outs = [((count, 8, GROUP * rows), jnp.float32)]
    return large(kernel, [*wide, *own, bias], outs, cost(count, rows, 2), behind)[0]


def earlier_terms(queries, dout, bias, before, near, stats, start, behind=()):
    rows = queries.shape[0]
    units = len(near) + 1
    count = before[0].shape[1] // WIDTH
    wide = (count, units * rows, GROUP * rows)
    outs = [
        ((count, GROUP, rows), jnp.float32),
        ((count, 8, GROUP * rows), jnp.float32),
        (wide, jnp.bfloat16),
        (wide, jnp.bfloat16),
    ] + [((rows, count * WIDTH), jnp.bfloat16)] * (2 * units)
    kernel = functools.partial(earlier_kernel, start, count, len(near))
    inputs = [queries, dout, bias, *before, *near, stats]
    results = large(kernel, inputs, outs, cost(count, rows, 4 * units), behind)
    return results[0], results[1:4], results[4 : 4 + units], results[4 + units :]


def the_rest(queries, dout, bias, before, near, own, kept, start, spots, earlier, behind=()):
    rows = queries.shape[0]
    skip, count, per = spots
    block = pl.BlockSpec((rows, per * GROUP * WIDTH), lambda g: (0, (start + skip) // per + g))
    inputs = [near_by(v) for v in (queries, dout, bias, *before, *near, *own, *kept)]
    extra = [*earlier, *behind]

    def kernel(*refs):
        refs = refs[: len(inputs)] + refs[len(inputs) + len(extra) :]
        rest_kernel(start, skip, per, len(near), *refs)

    wide = jax.ShapeDtypeStruct(queries.shape, jnp.bfloat16)
    results = pl.pallas_call(
        kernel,
        grid=(count // per,),
        in_specs=whole(len(inputs)) + whole(len(extra), pl.ANY),
        out_specs=[block, block] + whole(2),
        out_shape=[wide, wide] + [pltpu.VMEM((rows, count * WIDTH), jnp.float32)] * 2,
        input_output_aliases={len(inputs): 0, len(inputs) + 1: 1} if earlier else {},
        compiler_params=pltpu.CompilerParams(vmem_limit_bytes=VMEM_LARGE),
        cost_estimate=cost(count, rows, 5),
    )(*inputs, *extra)
    return results[:2], results[2:]


def route(flag, first, second, one, two):
    @pl.when(flag != 0)
    def _():
        one[...] = first[...]
        two[...] = second[...]

    @pl.when(flag == 0)
    def _():
        one[...] = second[...]
        two[...] = first[...]


def body(queries, keys, values, dout, doc_lengths, span_order):
    rows = queries.shape[0]
    size = lax.axis_size("head")
    subs = size // 2
    contexts = lax.axis_size(CONTEXT)
    width = keys.shape[1] // CHUNKS
    half = ((rows, width), jnp.bfloat16)

    def across(value):
        return lax.ppermute(value, "head", [(j, (j + subs) % size) for j in range(size)])

    def around(value, steps):
        pairs = [(j, j // subs * subs + (j + steps) % subs) for j in range(size)]
        return lax.ppermute(value, "head", pairs)

    def edges(value, start):
        pairs = [(c, c + 1) for c in range(start, contexts - 1, 2)]
        return lax.ppermute(value, CONTEXT, pairs + [(b, a) for a, b in pairs])

    def columns(chunk):
        return slice(chunk * width, (chunk + 1) * width)

    def pick_in(keys, values, give, sem):
        for flag, source in ((0, values), (1, keys)):

            @pl.when(lax.axis_index("head") // subs == flag)
            def _(source=source):
                copy = pltpu.make_async_copy(source.at[:, columns(0)], give, sem)
                copy.start()
                copy.wait()

    first_give = pl.pallas_call(
        pick_in,
        in_specs=whole(2, pl.ANY),
        out_specs=whole(1)[0],
        out_shape=pltpu.VMEM(*half),
        scratch_shapes=[pltpu.SemaphoreType.DMA],
        compiler_params=pltpu.CompilerParams(vmem_limit_bytes=VMEM_SMALL),
    )(far(keys), far(values))

    def later_give(own, chunk, behind):
        def kernel(flag, key, value, give):
            for which, source in ((0, value), (1, key)):

                @pl.when(flag[1] == which)
                def _(source=source):
                    give[...] = source[:, columns(chunk)]

        return small(kernel, flags, own, [half], behind)[0]

    def out_of_step(flag, backward):
        return (flag[3] + flag[4] + (1 if backward else 0)) % 2

    def edge_part(own, got, backward, odd, cols=slice(None), behind=(), price=None):
        def kernel(flag, *refs):
            own, (got, out) = refs[:-2], refs[-2:]
            keeps = out_of_step(flag, backward) != odd
            for which, keep in enumerate(own):

                @pl.when(keeps & ((flag[1] == which) | (len(own) == 1)))
                def _(keep=keep):
                    out[...] = keep[:, cols]

            @pl.when(jnp.logical_not(keeps))
            def _():
                out[...] = got[:rows, :]

        return small(kernel, flags, [*own, got], [half], behind, price)[0]

    def edge_done(own, got, even, odd, backward, cols=slice(None), behind=()):
        def kernel(flag, *refs):
            own, (got, even, odd, mine, theirs) = refs[:-5], refs[-5:]
            takes_odd = (flag[3] + flag[4]) % 2
            if backward:
                takes_odd = 1 - takes_odd

            @pl.when(flag[5] == 0)
            def _():
                route(takes_odd, odd, even, mine, theirs)

            kept = (flag[3] + (1 if backward else 0)) % 2
            for which, keep in enumerate(own):

                @pl.when((flag[5] != 0) & (kept != 0) & ((flag[1] == which) | (len(own) == 1)))
                def _(keep=keep):
                    route(takes_odd, keep.at[:, cols], even, mine, theirs)

            @pl.when((flag[5] != 0) & (kept == 0))
            def _():
                route(takes_odd, got.at[:rows], even, mine, theirs)

        return small(kernel, flags, [*own, got, even, odd], [half, half], behind)

    def window_parts(own, mine, other, cols, behind=()):
        def kernel(flag, own_key, own_value, mine, other, key, value, *sent):
            route(flag[1], other, mine, key, value)
            for index, out in enumerate(sent):
                inside = flag[2] + (subs - 1 - index) < subs

                @pl.when(inside)
                def _():
                    out[:, :width] = own_key[:, cols]
                    out[:, width:] = own_value[:, cols]

                @pl.when(jnp.logical_not(inside))
                def _():
                    out[:, :width] = key[...]
                    out[:, width:] = value[...]

        both = ((rows, 2 * width), jnp.bfloat16)
        outs = small(kernel, flags, [*own, mine, other], [half, half] + [both] * (subs - 1), behind)
        return outs[:2], [around(out, subs - 1 - i) for i, out in enumerate(outs[2:])]

    per_device = KEY_VALUE_HEADS // size

    def two_parts(out, lo, block):
        block = block.reshape(-1, rows)
        if block.shape[0] < EXTRA:
            fill = jnp.zeros((EXTRA - block.shape[0], rows), jnp.float32)
            block = jnp.concatenate([block, fill], axis=0)
        high = block.astype(jnp.bfloat16)
        out[rows:, lo : lo + rows] = high
        lo += rows
        out[rows:, lo : lo + rows] = (block - high.astype(jnp.float32)).astype(jnp.bfloat16)

    def one_part(ref, lo):
        high, low = ref[rows:, lo : lo + rows], ref[rows:, lo + rows : lo + 2 * rows]
        return high.astype(jnp.float32) + low.astype(jnp.float32)

    def near_terms(dk, dv, entropies=(), behind=()):
        extra = EXTRA if entropies else 0

        def kernel(flag, *refs):
            ents, refs = refs[: len(entropies)], refs[len(entropies) :]
            for index in range(subs - 1):
                out = refs[2 * (subs - 1) + index]
                out[:rows, :width] = refs[index][...]
                out[:rows, width:] = refs[subs - 1 + index][...]
                to = lax.rem(flag[2] + index + 1, subs)
                for which, ent in enumerate(ents):
                    two_parts(out, 2 * which * rows, ent[pl.ds(to * per_device, per_device)])

        both = ((rows + extra, 2 * width), jnp.bfloat16)
        outs = small(kernel, flags, [*entropies, *dk[1:], *dv[1:]], [both] * (subs - 1), behind)
        return [around(out, index + 1 - subs) for index, out in enumerate(outs)], outs

    def collect(dk, dv, arrived, entropies=(), behind=()):
        extra = EXTRA if entropies else 0

        def kernel(flag, dk, dv, *refs):
            ents, refs = refs[: len(entropies)], refs[len(entropies) :]
            got = refs[: subs - 1]
            keep, give, own_key, own_value = refs[subs - 1 : subs + 3]
            for which, term, own in ((0, dk, own_key), (1, dv, own_value)):
                before = term[...].astype(jnp.float32)
                mine = jnp.zeros_like(before)
                for index, ref in enumerate(got):
                    part = ref[:rows, which * width : (which + 1) * width].astype(jnp.float32)
                    within = flag[2] + (subs - 1 - index) < subs
                    mine = mine + jnp.where(within, part, 0.0)
                    before = before + jnp.where(within, 0.0, part)
                own[...] = mine
                before = before.astype(jnp.bfloat16)

                @pl.when(flag[1] == which)
                def _():
                    keep[...] = before

                @pl.when(flag[1] != which)
                def _():
                    give[:rows, :] = before

            for which, ent in enumerate(ents):
                block = ent[pl.ds(flag[2] * per_device, per_device)]
                blocks = [block.reshape(-1, rows)]
                blocks += [one_part(ref, 2 * which * rows)[: blocks[0].shape[0]] for ref in got]

                @pl.when(flag[1] == which)
                def _(blocks=blocks):
                    for index, block in enumerate(blocks):
                        refs[subs + 3][index] = block

                @pl.when(flag[1] != which)
                def _(blocks=blocks):
                    for index, block in enumerate(blocks):
                        two_parts(give, 2 * index * rows, block)

        full = ((rows, width), jnp.float32)
        outs = [half, ((rows + extra, width), jnp.bfloat16), full, full]
        if entropies:
            outs.append(((subs, per_device * GROUP, rows), jnp.float32))
        return small(kernel, flags, [dk[0], dv[0], *entropies, *arrived], outs, behind)

    def finish(chunks, entropies, got):
        local, plans = [entropies, got], []
        for chunk, (own_key, own_value, pieces, mine, other) in enumerate(chunks):
            spot = 0
            for dk, dv in pieces:
                cols = slice(spot, spot + dk.shape[1])
                plans.append((len(local), cols, slice(cols.start + chunk * width, cols.stop + chunk * width)))
                local += [own_key, own_value, mine, other, dk, dv]
                spot = cols.stop
        count = per_device * GROUP

        def kernel(flag, *refs):
            ent, got = refs[:2]
            out_key, out_value, out_ent = refs[-3:]
            is_key = flag[1] == 0
            for at, cols, to in plans:
                own_key, own_value, mine, other, dk, dv = refs[at : at + 6]
                here = mine[:, cols].astype(jnp.float32)
                there = other[:, cols].astype(jnp.float32)
                for out, own, term, back in (
                    (out_key, own_key, dk, jnp.where(is_key, here, there)),
                    (out_value, own_value, dv, jnp.where(is_key, there, here)),
                ):
                    out[:, to] = (own[:, cols] + term[...] + back).astype(jnp.bfloat16)
            for index in range(subs):
                steps = 0 if index == 0 else subs - index
                source = lax.rem(flag[2] + steps, subs)
                for way, block in ((flag[1], ent[index]), (1 - flag[1], one_part(got, 2 * index * rows))):
                    for spot in range(size):

                        @pl.when(way * subs + source == spot)
                        def _(spot=spot, block=block):
                            out_ent[:, spot * rows : (spot + 1) * rows] = block[:count]

        return pl.pallas_call(
            kernel,
            grid=(1,),
            in_specs=whole(1, pltpu.SMEM) + whole(len(local)),
            out_specs=[pl.BlockSpec(keys.shape, lambda g: (0, 0))] * 2
            + [pl.BlockSpec((count, size * rows), lambda g: (0, 0))],
            out_shape=[jax.ShapeDtypeStruct(keys.shape, jnp.bfloat16)] * 2
            + [jax.ShapeDtypeStruct((count, size * rows), jnp.float32)],
            compiler_params=pltpu.CompilerParams(vmem_limit_bytes=VMEM_SMALL),
        )(in_scalars(flags), *[near_by(v) for v in local])

    def taken(value, behind=(), price=None):
        def kernel(flag, value, out):
            out[...] = value[...]

        return small(kernel, flags, [value], [half], behind, price)[0]

    per_chunk = KEY_VALUE_HEADS // CHUNKS
    got = [across(first_give)]
    flags, wide_near, own, bias, stats = first_step(
        contexts, subs, per_chunk, (queries, dout, keys, values), span_order, doc_lengths, first_give
    )
    got.append(across(later_give(own, 1, got)))
    cols = [columns(chunk) for chunk in range(CHUNKS)]
    in0 = [edge_part(own, got[0], False, odd, cols[0], [stats]) for odd in range(2)]
    edge0 = [edges(part, odd) for odd, part in enumerate(in0)]
    in1 = [edge_part(own, got[1], False, odd, cols[1]) for odd in range(2)]
    edge1 = [edges(part, odd) for odd, part in enumerate(in1)]
    mine0, theirs0 = edge_done(own, got[0], *edge0, False, cols[0])
    other0 = across(theirs0)
    stats = [stats, more_sums(wide_near, own, bias, per_chunk, per_chunk, [theirs0])]
    edge1[1] = taken(taken(edge1[1], [theirs0]), price=cost(4, rows, 10))
    mine1, theirs1 = edge_done(own, got[1], *edge1, False, cols[1], [theirs0])
    other1 = across(theirs1)
    before0, near0 = window_parts(own, mine0, other0, cols[0], [theirs1, stats[1]])
    ent0, kept0, dk0, dv0 = earlier_terms(*wide_near, bias, before0, near0, stats[0], 0)
    before1, near1 = window_parts(own, mine1, other1, cols[1], [ent0])
    wide, pieces = [], []

    def rest(chunk, piece, behind):
        nonlocal wide
        before, near, kept = held[chunk]
        start = chunk * per_chunk
        wide, terms = the_rest(
            *wide_near, bias, before, near, own, kept, start, BEHIND[chunk][piece], wide, behind
        )
        pieces.append(terms)
        return terms[:1]

    held = [(before0, near0, kept0), (before1, near1, None)]
    arrived, sent = near_terms(dk0, dv0)
    done = rest(0, 0, sent[:1])
    keep0, give0, *own0 = collect(dk0, dv0, arrived)
    back0 = across(give0)
    ent1, kept1, dk1, dv1 = earlier_terms(
        *wide_near, bias, before1, near1, stats[1], per_chunk, [give0, *done]
    )
    held[1] = (before1, near1, kept1)
    out0 = edge_part([keep0], back0, True, 0)
    edge0 = [edges(out0, 0)]
    ents = [ent0, ent1]
    arrived, sent = near_terms(dk1, dv1, ents, [out0])
    keep1, give1, *own1, entropies = collect(dk1, dv1, arrived, ents)
    back1 = across(give1)
    edge0.append(edges(edge_part([keep0], back0, True, 1, behind=[give1], price=cost(4, rows, 10)), 1))
    out1 = [edge_part([keep1], back1, True, odd) for odd in range(2)]
    edge1 = [edges(part, odd) for odd, part in enumerate(out1)]
    mine0, theirs0 = edge_done([keep0], back0, *edge0, True, behind=out1[:1])
    other0 = across(theirs0)
    done = rest(0, 1, [theirs0])
    edge1[0] = taken(taken(edge1[0], done), price=cost(4, rows, 10))
    mine1, theirs1 = edge_done([keep1], back1, *edge1, True, behind=done)
    other1 = across(theirs1)
    rest(1, 0, [theirs1])
    grad_key, grad_value, entropy = finish(
        [(*own0, pieces[1::-1], mine0, other0), (*own1, pieces[2:], mine1, other1)], entropies, back1
    )
    return wide[0], entropy.T, wide[1], grad_key, grad_value


def solution(mesh):
    rows = P(("inner", "outer", "head"), None)
    return jax.shard_map(
        body,
        mesh=mesh,
        in_specs=(rows, rows, rows, rows, P(), P()),
        out_specs=(rows, P(("inner", "outer"), "head"), rows, rows, rows),
        check_vma=False,
    )
```

```python
import functools
import math

import jax
import jax.numpy as jnp
from jax import lax
from jax.experimental import pallas as pl
from jax.experimental.pallas import tpu as pltpu
from jax.sharding import PartitionSpec as P

QUERY_HEADS = 64
KEY_VALUE_HEADS = 8
WIDTH = 128
GROUP = QUERY_HEADS // KEY_VALUE_HEADS
SCALE = 1.0 / math.sqrt(WIDTH)
MASKED = -1e30
CONTEXT = ("inner", "outer")
CHUNKS = 2
UNROLL = 4
EXTRA = 16
BEHIND = (((0, 4, 2),), ((0, 4, 2),))
LOG2E = math.log2(math.e)
VMEM_SMALL = 8 * 2**20
VMEM_LARGE = 16 * 2**20
NT = (((1,), (1,)), ((), ()))
NN = (((1,), (0,)), ((), ()))


def dot(left, right, dims):
    return lax.dot_general(left, right, dims, preferred_element_type=jnp.float32)


def lanes(index, width=WIDTH):
    if isinstance(index, int):
        return slice(index * width, (index + 1) * width)
    return pl.ds(pl.multiple_of(index * width, WIDTH), width)


def group_rows(ref, g):
    return jnp.concatenate([ref[:, lanes(g * GROUP + h)] for h in range(GROUP)], axis=0)


def tiled(bias):
    return jnp.concatenate([bias] * GROUP, axis=1)


def row_sums(g, at, q_ref, do_ref, k_ref, v_ref, bias, stat_ref):
    s = dot(k_ref[:, lanes(g)], group_rows(q_ref, g), NT) + tiled(bias)
    dp = dot(v_ref[:, lanes(g)], group_rows(do_ref, g), NT)
    top = jnp.max(s, axis=0, keepdims=True)
    t = (s - top) * (SCALE * LOG2E)
    e = jnp.exp2(t)
    stat_ref[at, 0:1, :] = top
    stat_ref[at, 1:2, :] = jnp.sum(e, axis=0, keepdims=True)
    stat_ref[at, 2:3, :] = jnp.sum(e * t, axis=0, keepdims=True)
    stat_ref[at, 3:4, :] = jnp.sum(e * dp, axis=0, keepdims=True)


def first_kernel(contexts, count, *refs):
    sources, refs = refs[:4], refs[4:]
    spans_far, docs_far, refs = refs[0], refs[1], refs[2:]
    loaded, (flag, bias_ref, stat_ref, sems, spans, docs) = refs[:4], refs[4:]
    q_ref, do_ref, k_ref, v_ref = loaded
    rows = q_ref.shape[0]
    heads = k_ref.shape[1] // WIDTH
    short = [
        pltpu.make_async_copy(spans_far, spans, sems.at[2, 1]),
        pltpu.make_async_copy(docs_far, docs, sems.at[3, 1]),
    ]
    narrow = [pltpu.make_async_copy(sources[i], loaded[i], sems.at[i, 0]) for i in (2, 3)]

    def wide(g):
        cols = lanes(g, GROUP * WIDTH)
        return [
            pltpu.make_async_copy(sources[i].at[:, cols], loaded[i].at[:, cols], sems.at[i, g])
            for i in (0, 1)
        ]

    copies = short + narrow + [copy for g in range(heads) for copy in wide(g)]
    for copy in copies:
        copy.start()
    for copy in short:
        copy.wait()
    subs = bias_ref.shape[0] // rows - 1
    here, context = lax.axis_index("head"), lax.axis_index(CONTEXT)
    side, sub = here // subs, lax.rem(here, subs)
    span = spans[2 * context + side]
    first = (span * subs + sub) * rows
    flag[0] = first
    flag[1] = side
    flag[2] = sub
    flag[3] = (span == context).astype(jnp.int32)
    flag[4] = lax.rem(context, 2)
    flag[5] = (context == contexts - 1).astype(jnp.int32)
    q_pos = first + lax.broadcasted_iota(jnp.int32, (1, rows), 1)
    at = jnp.int32(0)
    start = jnp.zeros((1, rows), jnp.int32)

    def later(index, carry):
        at, start = carry
        return at + docs[index], jnp.where(at <= q_pos, at, start)

    _, start = lax.fori_loop(0, docs.shape[0], later, (at, start))
    window = bias_ref.shape[0]
    k_pos = first + rows - window + lax.broadcasted_iota(jnp.int32, (window, rows), 0)
    bias = jnp.where((k_pos >= start) & (k_pos <= q_pos), 0.0, MASKED)
    bias_ref[...] = bias
    for copy in narrow:
        copy.wait()

    def step(g, _):
        for copy in wide(g):
            copy.wait()
        row_sums(g, g, q_ref, do_ref, k_ref, v_ref, bias_ref[window - rows :, :], stat_ref)
        return 0

    lax.fori_loop(0, count, step, 0)
    for g in range(count, heads):
        for copy in wide(g):
            copy.wait()


def sums_kernel(start, count, q_ref, do_ref, k_ref, v_ref, bias_ref, stat_ref):
    last = bias_ref.shape[0] - q_ref.shape[0]

    def step(at, _):
        row_sums(start + at, at, q_ref, do_ref, k_ref, v_ref, bias_ref[last:, :], stat_ref)
        return 0

    lax.fori_loop(0, count, step, 0)


def earlier_kernel(start, count, near, q_ref, do_ref, bias_ref, first_k, first_v, *refs):
    near_refs, (stat_ref, *refs) = refs[:near], refs[near:]
    ent_ref, row_ref, p_ref, ds_ref = refs[:4]
    dk_refs, dv_refs = refs[4 : 5 + near], refs[5 + near :]
    rows = q_ref.shape[0]
    width = first_k.shape[1] // WIDTH
    window = (near + 1) * rows

    def head(at, _):
        g = start + at
        k_rows = jnp.concatenate(
            [first_k[:, lanes(at)], *[ref[:, lanes(at)] for ref in near_refs]], axis=0
        )
        v_rows = jnp.concatenate(
            [first_v[:, lanes(at)], *[ref[:, lanes(at + width)] for ref in near_refs]], axis=0
        )
        q_all, do_all = group_rows(q_ref, g), group_rows(do_ref, g)
        s = dot(k_rows, q_all, NT) + tiled(bias_ref[:window, :])
        dp = dot(v_rows, do_all, NT)
        own_top, own_total = stat_ref[at, 0:1, :], stat_ref[at, 1:2, :]
        top = jnp.maximum(jnp.max(s, axis=0, keepdims=True), own_top)
        t = (s - top) * (SCALE * LOG2E)
        e = jnp.exp2(t)
        shift = (own_top - top) * (SCALE * LOG2E)
        ratio = jnp.exp2(shift)
        total = own_total * ratio + jnp.sum(e, axis=0, keepdims=True)
        inv = 1.0 / total
        spread = (stat_ref[at, 2:3, :] + shift * own_total) * ratio
        spread = spread + jnp.sum(e * t, axis=0, keepdims=True)
        entropy = jnp.log(total) - spread * inv * math.log(2.0)
        for h in range(GROUP):
            ent_ref[at, h : h + 1, :] = entropy[:, h * rows : (h + 1) * rows]
        delta = stat_ref[at, 3:4, :] * ratio + jnp.sum(e * dp, axis=0, keepdims=True)
        delta = delta * inv
        row_ref[at, 0:1, :] = top * (SCALE * LOG2E) + jnp.log2(total)
        row_ref[at, 1:2, :] = delta
        p = e * inv
        pb = p.astype(jnp.bfloat16)
        ds = (p * (dp - delta)).astype(jnp.bfloat16)
        p_ref[at] = pb
        ds_ref[at] = ds
        dv = dot(pb, do_all, NN)
        dk = dot(ds, q_all, NN) * SCALE
        for unit in range(near + 1):
            part = slice(unit * rows, (unit + 1) * rows)
            dk_refs[unit][:, lanes(at)] = dk[part].astype(jnp.bfloat16)
            dv_refs[unit][:, lanes(at)] = dv[part].astype(jnp.bfloat16)

        return 0

    lax.fori_loop(0, count, head, 0, unroll=UNROLL)


def rest_kernel(start, skip, per, near, q_ref, do_ref, bias_ref, first_k, first_v, *refs):
    near_refs, (own_k, own_v), refs = refs[:near], refs[near : near + 2], refs[near + 2 :]
    row_ref, p_ref, ds_ref, att_ref, dq_ref, dk_ref, dv_ref = refs
    rows = q_ref.shape[0]
    width = first_k.shape[1] // WIDTH
    last = bias_ref.shape[0] - rows
    for step in range(per):
        index = pl.program_id(0) * per + step
        at, g = skip + index, start + skip + index
        own_keys, own_values = own_k[:, lanes(g)], own_v[:, lanes(g)]
        k_rows = jnp.concatenate(
            [first_k[:, lanes(at)], *[ref[:, lanes(at)] for ref in near_refs], own_keys], axis=0
        )
        v_rows = jnp.concatenate(
            [first_v[:, lanes(at)], *[ref[:, lanes(at + width)] for ref in near_refs], own_values],
            axis=0,
        )
        q_all, do_all = group_rows(q_ref, g), group_rows(do_ref, g)
        s = dot(own_keys, q_all, NT) + tiled(bias_ref[last:, :])
        dp = dot(own_values, do_all, NT)
        p = jnp.exp2(s * (SCALE * LOG2E) - row_ref[at, 0:1, :])
        pb = p.astype(jnp.bfloat16)
        ds = (p * (dp - row_ref[at, 1:2, :])).astype(jnp.bfloat16)
        dv_ref[:, lanes(index)] = dot(pb, do_all, NN)
        dk_ref[:, lanes(index)] = dot(ds, q_all, NN) * SCALE
        p_all = jnp.concatenate([p_ref[at], pb], axis=0)
        ds_all = jnp.concatenate([ds_ref[at], ds], axis=0)
        out = dot(v_rows.T, p_all, NN).T.astype(jnp.bfloat16)
        dq = (dot(k_rows.T, ds_all, NN) * SCALE).T.astype(jnp.bfloat16)
        for h in range(GROUP):
            spot = slice(h * rows, (h + 1) * rows)
            att_ref[:, lanes(step * GROUP + h)] = out[spot, :]
            dq_ref[:, lanes(step * GROUP + h)] = dq[spot, :]


def whole(count, space=pltpu.VMEM):
    return [pl.BlockSpec(memory_space=space)] * count


def near_by(value):
    return pltpu.with_memory_space_constraint(value, pltpu.VMEM)


def in_scalars(value):
    return pltpu.with_memory_space_constraint(value, pltpu.SMEM)


def small(kernel, flags, inputs, outs, behind=(), price=None):
    def body(*refs):
        kernel(*refs[: 1 + len(inputs)], *refs[1 + len(inputs) + len(behind) :])

    return pl.pallas_call(
        body,
        in_specs=whole(1, pltpu.SMEM) + whole(len(inputs)) + whole(len(behind), pl.ANY),
        out_specs=whole(len(outs)),
        out_shape=[pltpu.VMEM(shape, dtype) for shape, dtype in outs],
        compiler_params=pltpu.CompilerParams(vmem_limit_bytes=VMEM_SMALL),
        cost_estimate=price,
    )(in_scalars(flags), *[near_by(value) for value in inputs], *behind)


def cost(count, rows, products):
    return pl.CostEstimate(
        flops=4 * products * count * rows * GROUP * rows * WIDTH,
        bytes_accessed=1,
        transcendentals=0,
    )


def large(kernel, inputs, outs, price, behind=()):
    def body(*refs):
        kernel(*refs[: len(inputs)], *refs[len(inputs) + len(behind) :])

    return pl.pallas_call(
        body,
        in_specs=whole(len(inputs)) + whole(len(behind), pl.ANY),
        out_specs=whole(len(outs)),
        out_shape=[pltpu.VMEM(shape, dtype) for shape, dtype in outs],
        compiler_params=pltpu.CompilerParams(vmem_limit_bytes=VMEM_LARGE),
        cost_estimate=price,
    )(*[near_by(value) for value in inputs], *behind)


def far(value):
    return pltpu.with_memory_space_constraint(value, pltpu.HBM)


def first_step(contexts, subs, count, arrays, spans, docs, behind):
    rows = arrays[0].shape[0]
    heads = arrays[2].shape[1] // WIDTH

    def kernel(*refs):
        first_kernel(contexts, count, *refs[:6], *refs[7:])

    results = pl.pallas_call(
        kernel,
        in_specs=whole(7, pl.ANY),
        out_specs=whole(4) + whole(1, pltpu.SMEM) + whole(2),
        out_shape=[pltpu.VMEM(array.shape, array.dtype) for array in arrays]
        + [
            pltpu.SMEM((6,), jnp.int32),
            pltpu.VMEM(((subs + 1) * rows, rows), jnp.float32),
            pltpu.VMEM((count, 8, GROUP * rows), jnp.float32),
        ],
        scratch_shapes=[
            pltpu.SemaphoreType.DMA((4, heads)),
            pltpu.SMEM(spans.shape, jnp.int32),
            pltpu.SMEM(docs.shape, jnp.int32),
        ],
        compiler_params=pltpu.CompilerParams(vmem_limit_bytes=VMEM_LARGE),
        cost_estimate=cost(count, rows, 3),
    )(*[far(array) for array in (*arrays, spans, docs)], behind)
    return results[4], results[:2], results[2:4], results[5], results[6]


def more_sums(wide, own, bias, start, count, behind=()):
    rows = wide[0].shape[0]
    kernel = functools.partial(sums_kernel, start, count)
    outs = [((count, 8, GROUP * rows), jnp.float32)]
    return large(kernel, [*wide, *own, bias], outs, cost(count, rows, 2), behind)[0]


def earlier_terms(queries, dout, bias, before, near, stats, start, behind=()):
    rows = queries.shape[0]
    units = len(near) + 1
    count = before[0].shape[1] // WIDTH
    wide = (count, units * rows, GROUP * rows)
    outs = [
        ((count, GROUP, rows), jnp.float32),
        ((count, 8, GROUP * rows), jnp.float32),
        (wide, jnp.bfloat16),
        (wide, jnp.bfloat16),
    ] + [((rows, count * WIDTH), jnp.bfloat16)] * (2 * units)
    kernel = functools.partial(earlier_kernel, start, count, len(near))
    inputs = [queries, dout, bias, *before, *near, stats]
    results = large(kernel, inputs, outs, cost(count, rows, 4 * units), behind)
    return results[0], results[1:4], results[4 : 4 + units], results[4 + units :]


def the_rest(queries, dout, bias, before, near, own, kept, start, spots, earlier, behind=()):
    rows = queries.shape[0]
    skip, count, per = spots
    block = pl.BlockSpec((rows, per * GROUP * WIDTH), lambda g: (0, (start + skip) // per + g))
    inputs = [near_by(v) for v in (queries, dout, bias, *before, *near, *own, *kept)]
    extra = [*earlier, *behind]

    def kernel(*refs):
        refs = refs[: len(inputs)] + refs[len(inputs) + len(extra) :]
        rest_kernel(start, skip, per, len(near), *refs)

    wide = jax.ShapeDtypeStruct(queries.shape, jnp.bfloat16)
    results = pl.pallas_call(
        kernel,
        grid=(count // per,),
        in_specs=whole(len(inputs)) + whole(len(extra), pl.ANY),
        out_specs=[block, block] + whole(2),
        out_shape=[wide, wide] + [pltpu.VMEM((rows, count * WIDTH), jnp.float32)] * 2,
        input_output_aliases={len(inputs): 0, len(inputs) + 1: 1} if earlier else {},
        compiler_params=pltpu.CompilerParams(vmem_limit_bytes=VMEM_LARGE),
        cost_estimate=cost(count, rows, 5),
    )(*inputs, *extra)
    return results[:2], results[2:]


def route(flag, first, second, one, two):
    @pl.when(flag != 0)
    def _():
        one[...] = first[...]
        two[...] = second[...]

    @pl.when(flag == 0)
    def _():
        one[...] = second[...]
        two[...] = first[...]


def body(queries, keys, values, dout, doc_lengths, span_order):
    rows = queries.shape[0]
    size = lax.axis_size("head")
    subs = size // 2
    contexts = lax.axis_size(CONTEXT)
    width = keys.shape[1] // CHUNKS
    half = ((rows, width), jnp.bfloat16)

    def across(value):
        return lax.ppermute(value, "head", [(j, (j + subs) % size) for j in range(size)])

    def around(value, steps):
        pairs = [(j, j // subs * subs + (j + steps) % subs) for j in range(size)]
        return lax.ppermute(value, "head", pairs)

    def edges(value, start):
        pairs = [(c, c + 1) for c in range(start, contexts - 1, 2)]
        return lax.ppermute(value, CONTEXT, pairs + [(b, a) for a, b in pairs])

    def columns(chunk):
        return slice(chunk * width, (chunk + 1) * width)

    def pick_in(keys, values, give, sem):
        for flag, source in ((0, values), (1, keys)):

            @pl.when(lax.axis_index("head") // subs == flag)
            def _(source=source):
                copy = pltpu.make_async_copy(source.at[:, columns(0)], give, sem)
                copy.start()
                copy.wait()

    first_give = pl.pallas_call(
        pick_in,
        in_specs=whole(2, pl.ANY),
        out_specs=whole(1)[0],
        out_shape=pltpu.VMEM(*half),
        scratch_shapes=[pltpu.SemaphoreType.DMA],
        compiler_params=pltpu.CompilerParams(vmem_limit_bytes=VMEM_SMALL),
    )(far(keys), far(values))

    def later_give(own, chunk, behind):
        def kernel(flag, key, value, give):
            for which, source in ((0, value), (1, key)):

                @pl.when(flag[1] == which)
                def _(source=source):
                    give[...] = source[:, columns(chunk)]

        return small(kernel, flags, own, [half], behind)[0]

    def out_of_step(flag, backward):
        return (flag[3] + flag[4] + (1 if backward else 0)) % 2

    def edge_part(own, got, backward, odd, cols=slice(None), behind=(), price=None):
        def kernel(flag, *refs):
            own, (got, out) = refs[:-2], refs[-2:]
            keeps = out_of_step(flag, backward) != odd
            for which, keep in enumerate(own):

                @pl.when(keeps & ((flag[1] == which) | (len(own) == 1)))
                def _(keep=keep):
                    out[...] = keep[:, cols]

            @pl.when(jnp.logical_not(keeps))
            def _():
                out[...] = got[:rows, :]

        return small(kernel, flags, [*own, got], [half], behind, price)[0]

    def edge_done(own, got, even, odd, backward, cols=slice(None), behind=()):
        def kernel(flag, *refs):
            own, (got, even, odd, mine, theirs) = refs[:-5], refs[-5:]
            takes_odd = (flag[3] + flag[4]) % 2
            if backward:
                takes_odd = 1 - takes_odd

            @pl.when(flag[5] == 0)
            def _():
                route(takes_odd, odd, even, mine, theirs)

            kept = (flag[3] + (1 if backward else 0)) % 2
            for which, keep in enumerate(own):

                @pl.when((flag[5] != 0) & (kept != 0) & ((flag[1] == which) | (len(own) == 1)))
                def _(keep=keep):
                    route(takes_odd, keep.at[:, cols], even, mine, theirs)

            @pl.when((flag[5] != 0) & (kept == 0))
            def _():
                route(takes_odd, got.at[:rows], even, mine, theirs)

        return small(kernel, flags, [*own, got, even, odd], [half, half], behind)

    def window_parts(own, mine, other, cols, behind=()):
        def kernel(flag, own_key, own_value, mine, other, key, value, *sent):
            route(flag[1], other, mine, key, value)
            for index, out in enumerate(sent):
                inside = flag[2] + (subs - 1 - index) < subs

                @pl.when(inside)
                def _():
                    out[:, :width] = own_key[:, cols]
                    out[:, width:] = own_value[:, cols]

                @pl.when(jnp.logical_not(inside))
                def _():
                    out[:, :width] = key[...]
                    out[:, width:] = value[...]

        both = ((rows, 2 * width), jnp.bfloat16)
        outs = small(kernel, flags, [*own, mine, other], [half, half] + [both] * (subs - 1), behind)
        return outs[:2], [around(out, subs - 1 - i) for i, out in enumerate(outs[2:])]

    per_device = KEY_VALUE_HEADS // size

    def two_parts(out, lo, block):
        block = block.reshape(-1, rows)
        if block.shape[0] < EXTRA:
            fill = jnp.zeros((EXTRA - block.shape[0], rows), jnp.float32)
            block = jnp.concatenate([block, fill], axis=0)
        high = block.astype(jnp.bfloat16)
        out[rows:, lo : lo + rows] = high
        lo += rows
        out[rows:, lo : lo + rows] = (block - high.astype(jnp.float32)).astype(jnp.bfloat16)

    def one_part(ref, lo):
        high, low = ref[rows:, lo : lo + rows], ref[rows:, lo + rows : lo + 2 * rows]
        return high.astype(jnp.float32) + low.astype(jnp.float32)

    def near_terms(dk, dv, entropies=(), behind=()):
        extra = EXTRA if entropies else 0

        def kernel(flag, *refs):
            ents, refs = refs[: len(entropies)], refs[len(entropies) :]
            for index in range(subs - 1):
                out = refs[2 * (subs - 1) + index]
                out[:rows, :width] = refs[index][...]
                out[:rows, width:] = refs[subs - 1 + index][...]
                to = lax.rem(flag[2] + index + 1, subs)
                for which, ent in enumerate(ents):
                    two_parts(out, 2 * which * rows, ent[pl.ds(to * per_device, per_device)])

        both = ((rows + extra, 2 * width), jnp.bfloat16)
        outs = small(kernel, flags, [*entropies, *dk[1:], *dv[1:]], [both] * (subs - 1), behind)
        return [around(out, index + 1 - subs) for index, out in enumerate(outs)], outs

    def collect(dk, dv, arrived, entropies=(), behind=()):
        extra = EXTRA if entropies else 0

        def kernel(flag, dk, dv, *refs):
            ents, refs = refs[: len(entropies)], refs[len(entropies) :]
            got = refs[: subs - 1]
            keep, give, own_key, own_value = refs[subs - 1 : subs + 3]
            for which, term, own in ((0, dk, own_key), (1, dv, own_value)):
                before = term[...].astype(jnp.float32)
                mine = jnp.zeros_like(before)
                for index, ref in enumerate(got):
                    part = ref[:rows, which * width : (which + 1) * width].astype(jnp.float32)
                    within = flag[2] + (subs - 1 - index) < subs
                    mine = mine + jnp.where(within, part, 0.0)
                    before = before + jnp.where(within, 0.0, part)
                own[...] = mine
                before = before.astype(jnp.bfloat16)

                @pl.when(flag[1] == which)
                def _():
                    keep[...] = before

                @pl.when(flag[1] != which)
                def _():
                    give[:rows, :] = before

            for which, ent in enumerate(ents):
                block = ent[pl.ds(flag[2] * per_device, per_device)]
                blocks = [block.reshape(-1, rows)]
                blocks += [one_part(ref, 2 * which * rows)[: blocks[0].shape[0]] for ref in got]

                @pl.when(flag[1] == which)
                def _(blocks=blocks):
                    for index, block in enumerate(blocks):
                        refs[subs + 3][index] = block

                @pl.when(flag[1] != which)
                def _(blocks=blocks):
                    for index, block in enumerate(blocks):
                        two_parts(give, 2 * index * rows, block)

        full = ((rows, width), jnp.float32)
        outs = [half, ((rows + extra, width), jnp.bfloat16), full, full]
        if entropies:
            outs.append(((subs, per_device * GROUP, rows), jnp.float32))
        return small(kernel, flags, [dk[0], dv[0], *entropies, *arrived], outs, behind)

    def finish(chunks, entropies, got):
        local, plans = [entropies, got], []
        for chunk, (own_key, own_value, pieces, mine, other) in enumerate(chunks):
            spot = 0
            for dk, dv in pieces:
                cols = slice(spot, spot + dk.shape[1])
                plans.append((len(local), cols, slice(cols.start + chunk * width, cols.stop + chunk * width)))
                local += [own_key, own_value, mine, other, dk, dv]
                spot = cols.stop
        count = per_device * GROUP

        def kernel(flag, *refs):
            ent, got = refs[:2]
            out_key, out_value, out_ent = refs[-3:]
            is_key = flag[1] == 0
            for at, cols, to in plans:
                own_key, own_value, mine, other, dk, dv = refs[at : at + 6]
                here = mine[:, cols].astype(jnp.float32)
                there = other[:, cols].astype(jnp.float32)
                for out, own, term, back in (
                    (out_key, own_key, dk, jnp.where(is_key, here, there)),
                    (out_value, own_value, dv, jnp.where(is_key, there, here)),
                ):
                    out[:, to] = (own[:, cols] + term[...] + back).astype(jnp.bfloat16)
            for index in range(subs):
                steps = 0 if index == 0 else subs - index
                source = lax.rem(flag[2] + steps, subs)
                for way, block in ((flag[1], ent[index]), (1 - flag[1], one_part(got, 2 * index * rows))):
                    for spot in range(size):

                        @pl.when(way * subs + source == spot)
                        def _(spot=spot, block=block):
                            out_ent[:, spot * rows : (spot + 1) * rows] = block[:count]

        return pl.pallas_call(
            kernel,
            grid=(1,),
            in_specs=whole(1, pltpu.SMEM) + whole(len(local)),
            out_specs=[pl.BlockSpec(keys.shape, lambda g: (0, 0))] * 2
            + [pl.BlockSpec((count, size * rows), lambda g: (0, 0))],
            out_shape=[jax.ShapeDtypeStruct(keys.shape, jnp.bfloat16)] * 2
            + [jax.ShapeDtypeStruct((count, size * rows), jnp.float32)],
            compiler_params=pltpu.CompilerParams(vmem_limit_bytes=VMEM_SMALL),
        )(in_scalars(flags), *[near_by(v) for v in local])

    def taken(value, behind=(), price=None):
        def kernel(flag, value, out):
            out[...] = value[...]

        return small(kernel, flags, [value], [half], behind, price)[0]

    per_chunk = KEY_VALUE_HEADS // CHUNKS
    got = [across(first_give)]
    flags, wide_near, own, bias, stats = first_step(
        contexts, subs, per_chunk, (queries, dout, keys, values), span_order, doc_lengths, first_give
    )
    got.append(across(later_give(own, 1, got)))
    cols = [columns(chunk) for chunk in range(CHUNKS)]
    in0 = [edge_part(own, got[0], False, odd, cols[0], [stats]) for odd in range(2)]
    edge0 = [edges(part, odd) for odd, part in enumerate(in0)]
    in1 = [edge_part(own, got[1], False, odd, cols[1]) for odd in range(2)]
    edge1 = [edges(part, odd) for odd, part in enumerate(in1)]
    mine0, theirs0 = edge_done(own, got[0], *edge0, False, cols[0])
    other0 = across(theirs0)
    stats = [stats, more_sums(wide_near, own, bias, per_chunk, per_chunk, [theirs0])]
    edge1[1] = taken(taken(edge1[1], [theirs0]), price=cost(4, rows, 10))
    mine1, theirs1 = edge_done(own, got[1], *edge1, False, cols[1], [theirs0])
    other1 = across(theirs1)
    before0, near0 = window_parts(own, mine0, other0, cols[0], [theirs1, stats[1]])
    ent0, kept0, dk0, dv0 = earlier_terms(*wide_near, bias, before0, near0, stats[0], 0)
    before1, near1 = window_parts(own, mine1, other1, cols[1], [ent0])
    wide, pieces = [], []

    def rest(chunk, piece, behind):
        nonlocal wide
        before, near, kept = held[chunk]
        start = chunk * per_chunk
        wide, terms = the_rest(
            *wide_near, bias, before, near, own, kept, start, BEHIND[chunk][piece], wide, behind
        )
        pieces.append(terms)
        return terms[:1]

    held = [(before0, near0, kept0), (before1, near1, None)]
    arrived, sent = near_terms(dk0, dv0)
    keep0, give0, *own0 = collect(dk0, dv0, arrived)
    back0 = across(give0)
    ent1, kept1, dk1, dv1 = earlier_terms(
        *wide_near, bias, before1, near1, stats[1], per_chunk, [give0]
    )
    held[1] = (before1, near1, kept1)
    out0 = edge_part([keep0], back0, True, 0)
    edge0 = [edges(out0, 0)]
    ents = [ent0, ent1]
    arrived, sent = near_terms(dk1, dv1, ents, [out0])
    keep1, give1, *own1, entropies = collect(dk1, dv1, arrived, ents)
    back1 = across(give1)
    edge0.append(edges(edge_part([keep0], back0, True, 1, behind=[give1], price=cost(4, rows, 10)), 1))
    out1 = [edge_part([keep1], back1, True, odd) for odd in range(2)]
    edge1 = [edges(part, odd) for odd, part in enumerate(out1)]
    mine0, theirs0 = edge_done([keep0], back0, *edge0, True, behind=out1[:1])
    other0 = across(theirs0)
    done = rest(0, 0, [theirs0])
    edge1[0] = taken(taken(edge1[0], done), price=cost(4, rows, 10))
    mine1, theirs1 = edge_done([keep1], back1, *edge1, True, behind=done)
    other1 = across(theirs1)
    rest(1, 0, [theirs1])
    grad_key, grad_value, entropy = finish(
        [(*own0, pieces[:1], mine0, other0), (*own1, pieces[1:], mine1, other1)], entropies, back1
    )
    return wide[0], entropy.T, wide[1], grad_key, grad_value


def solution(mesh):
    rows = P(("inner", "outer", "head"), None)
    return jax.shard_map(
        body,
        mesh=mesh,
        in_specs=(rows, rows, rows, rows, P(), P()),
        out_specs=(rows, P(("inner", "outer"), "head"), rows, rows, rows),
        check_vma=False,
    )
```

```python
import functools
import math

import jax
import jax.numpy as jnp
from jax import lax
from jax.experimental import pallas as pl
from jax.experimental.pallas import tpu as pltpu
from jax.sharding import PartitionSpec as P

QUERY_HEADS = 64
KEY_VALUE_HEADS = 8
WIDTH = 128
GROUP = QUERY_HEADS // KEY_VALUE_HEADS
SCALE = 1.0 / math.sqrt(WIDTH)
MASKED = -1e30
CONTEXT = ("inner", "outer")
CHUNKS = 2
UNROLL = 4
EXTRA = 16
BEHIND = (((0, 4, 4),), ((0, 4, 2),))
LOG2E = math.log2(math.e)
VMEM_SMALL = 8 * 2**20
VMEM_LARGE = 24 * 2**20
NT = (((1,), (1,)), ((), ()))
NN = (((1,), (0,)), ((), ()))


def dot(left, right, dims):
    return lax.dot_general(left, right, dims, preferred_element_type=jnp.float32)


def lanes(index, width=WIDTH):
    if isinstance(index, int):
        return slice(index * width, (index + 1) * width)
    return pl.ds(pl.multiple_of(index * width, WIDTH), width)


def group_rows(ref, g):
    return jnp.concatenate([ref[:, lanes(g * GROUP + h)] for h in range(GROUP)], axis=0)


def tiled(bias):
    return jnp.concatenate([bias] * GROUP, axis=1)


def row_sums(g, at, q_ref, do_ref, k_ref, v_ref, bias, stat_ref):
    s = dot(k_ref[:, lanes(g)], group_rows(q_ref, g), NT) + tiled(bias)
    dp = dot(v_ref[:, lanes(g)], group_rows(do_ref, g), NT)
    top = jnp.max(s, axis=0, keepdims=True)
    t = (s - top) * (SCALE * LOG2E)
    e = jnp.exp2(t)
    stat_ref[at, 0:1, :] = top
    stat_ref[at, 1:2, :] = jnp.sum(e, axis=0, keepdims=True)
    stat_ref[at, 2:3, :] = jnp.sum(e * t, axis=0, keepdims=True)
    stat_ref[at, 3:4, :] = jnp.sum(e * dp, axis=0, keepdims=True)


def first_kernel(contexts, count, *refs):
    sources, refs = refs[:4], refs[4:]
    spans_far, docs_far, refs = refs[0], refs[1], refs[2:]
    loaded, (flag, bias_ref, stat_ref, sems, spans, docs) = refs[:4], refs[4:]
    q_ref, do_ref, k_ref, v_ref = loaded
    rows = q_ref.shape[0]
    heads = k_ref.shape[1] // WIDTH
    short = [
        pltpu.make_async_copy(spans_far, spans, sems.at[2, 1]),
        pltpu.make_async_copy(docs_far, docs, sems.at[3, 1]),
    ]
    narrow = [pltpu.make_async_copy(sources[i], loaded[i], sems.at[i, 0]) for i in (2, 3)]

    def wide(g):
        cols = lanes(g, GROUP * WIDTH)
        return [
            pltpu.make_async_copy(sources[i].at[:, cols], loaded[i].at[:, cols], sems.at[i, g])
            for i in (0, 1)
        ]

    copies = short + narrow + [copy for g in range(heads) for copy in wide(g)]
    for copy in copies:
        copy.start()
    for copy in short:
        copy.wait()
    subs = bias_ref.shape[0] // rows - 1
    here, context = lax.axis_index("head"), lax.axis_index(CONTEXT)
    side, sub = here // subs, lax.rem(here, subs)
    span = spans[2 * context + side]
    first = (span * subs + sub) * rows
    flag[0] = first
    flag[1] = side
    flag[2] = sub
    flag[3] = (span == context).astype(jnp.int32)
    flag[4] = lax.rem(context, 2)
    flag[5] = (context == contexts - 1).astype(jnp.int32)
    q_pos = first + lax.broadcasted_iota(jnp.int32, (1, rows), 1)
    at = jnp.int32(0)
    start = jnp.zeros((1, rows), jnp.int32)

    def later(index, carry):
        at, start = carry
        return at + docs[index], jnp.where(at <= q_pos, at, start)

    _, start = lax.fori_loop(0, docs.shape[0], later, (at, start))
    window = bias_ref.shape[0]
    k_pos = first + rows - window + lax.broadcasted_iota(jnp.int32, (window, rows), 0)
    bias = jnp.where((k_pos >= start) & (k_pos <= q_pos), 0.0, MASKED)
    bias_ref[...] = bias
    for copy in narrow:
        copy.wait()

    def step(g, _):
        for copy in wide(g):
            copy.wait()
        row_sums(g, g, q_ref, do_ref, k_ref, v_ref, bias_ref[window - rows :, :], stat_ref)
        return 0

    lax.fori_loop(0, count, step, 0, unroll=2)
    for g in range(count, heads):
        for copy in wide(g):
            copy.wait()


def sums_kernel(start, count, q_ref, do_ref, k_ref, v_ref, bias_ref, stat_ref):
    last = bias_ref.shape[0] - q_ref.shape[0]

    def step(at, _):
        row_sums(start + at, at, q_ref, do_ref, k_ref, v_ref, bias_ref[last:, :], stat_ref)
        return 0

    lax.fori_loop(0, count, step, 0, unroll=2)


def earlier_kernel(start, count, near, q_ref, do_ref, bias_ref, first_k, first_v, *refs):
    near_refs, (stat_ref, *refs) = refs[:near], refs[near:]
    ent_ref, row_ref, p_ref, ds_ref = refs[:4]
    dk_refs, dv_refs = refs[4 : 5 + near], refs[5 + near :]
    rows = q_ref.shape[0]
    width = first_k.shape[1] // WIDTH
    window = (near + 1) * rows

    def head(at, _):
        g = start + at
        k_rows = jnp.concatenate(
            [first_k[:, lanes(at)], *[ref[:, lanes(at)] for ref in near_refs]], axis=0
        )
        v_rows = jnp.concatenate(
            [first_v[:, lanes(at)], *[ref[:, lanes(at + width)] for ref in near_refs]], axis=0
        )
        q_all, do_all = group_rows(q_ref, g), group_rows(do_ref, g)
        s = dot(k_rows, q_all, NT) + tiled(bias_ref[:window, :])
        dp = dot(v_rows, do_all, NT)
        own_top, own_total = stat_ref[at, 0:1, :], stat_ref[at, 1:2, :]
        top = jnp.maximum(jnp.max(s, axis=0, keepdims=True), own_top)
        t = (s - top) * (SCALE * LOG2E)
        e = jnp.exp2(t)
        shift = (own_top - top) * (SCALE * LOG2E)
        ratio = jnp.exp2(shift)
        total = own_total * ratio + jnp.sum(e, axis=0, keepdims=True)
        inv = 1.0 / total
        spread = (stat_ref[at, 2:3, :] + shift * own_total) * ratio
        spread = spread + jnp.sum(e * t, axis=0, keepdims=True)
        entropy = jnp.log(total) - spread * inv * math.log(2.0)
        for h in range(GROUP):
            ent_ref[at, h : h + 1, :] = entropy[:, h * rows : (h + 1) * rows]
        delta = stat_ref[at, 3:4, :] * ratio + jnp.sum(e * dp, axis=0, keepdims=True)
        delta = delta * inv
        row_ref[at, 0:1, :] = top * (SCALE * LOG2E) + jnp.log2(total)
        row_ref[at, 1:2, :] = delta
        p = e * inv
        pb = p.astype(jnp.bfloat16)
        ds = (p * (dp - delta)).astype(jnp.bfloat16)
        p_ref[at] = pb
        ds_ref[at] = ds
        dv = dot(pb, do_all, NN)
        dk = dot(ds, q_all, NN) * SCALE
        for unit in range(near + 1):
            part = slice(unit * rows, (unit + 1) * rows)
            dk_refs[unit][:, lanes(at)] = dk[part].astype(jnp.bfloat16)
            dv_refs[unit][:, lanes(at)] = dv[part].astype(jnp.bfloat16)

        return 0

    lax.fori_loop(0, count, head, 0, unroll=UNROLL)


def rest_kernel(start, skip, per, near, q_ref, do_ref, bias_ref, first_k, first_v, *refs):
    near_refs, (own_k, own_v), refs = refs[:near], refs[near : near + 2], refs[near + 2 :]
    row_ref, p_ref, ds_ref, att_ref, dq_ref, dk_ref, dv_ref = refs
    rows = q_ref.shape[0]
    width = first_k.shape[1] // WIDTH
    last = bias_ref.shape[0] - rows
    for step in range(per):
        index = pl.program_id(0) * per + step
        at, g = skip + index, start + skip + index
        own_keys, own_values = own_k[:, lanes(g)], own_v[:, lanes(g)]
        k_rows = jnp.concatenate(
            [first_k[:, lanes(at)], *[ref[:, lanes(at)] for ref in near_refs], own_keys], axis=0
        )
        v_rows = jnp.concatenate(
            [first_v[:, lanes(at)], *[ref[:, lanes(at + width)] for ref in near_refs], own_values],
            axis=0,
        )
        q_all, do_all = group_rows(q_ref, g), group_rows(do_ref, g)
        s = dot(own_keys, q_all, NT) + tiled(bias_ref[last:, :])
        dp = dot(own_values, do_all, NT)
        p = jnp.exp2(s * (SCALE * LOG2E) - row_ref[at, 0:1, :])
        pb = p.astype(jnp.bfloat16)
        ds = (p * (dp - row_ref[at, 1:2, :])).astype(jnp.bfloat16)
        dv_ref[:, lanes(index)] = dot(pb, do_all, NN)
        dk_ref[:, lanes(index)] = dot(ds, q_all, NN) * SCALE
        p_all = jnp.concatenate([p_ref[at], pb], axis=0)
        ds_all = jnp.concatenate([ds_ref[at], ds], axis=0)
        out = dot(v_rows.T, p_all, NN).T.astype(jnp.bfloat16)
        dq = (dot(k_rows.T, ds_all, NN) * SCALE).T.astype(jnp.bfloat16)
        for h in range(GROUP):
            spot = slice(h * rows, (h + 1) * rows)
            att_ref[:, lanes(step * GROUP + h)] = out[spot, :]
            dq_ref[:, lanes(step * GROUP + h)] = dq[spot, :]


def whole(count, space=pltpu.VMEM):
    return [pl.BlockSpec(memory_space=space)] * count


def near_by(value):
    return pltpu.with_memory_space_constraint(value, pltpu.VMEM)


def in_scalars(value):
    return pltpu.with_memory_space_constraint(value, pltpu.SMEM)


def small(kernel, flags, inputs, outs, behind=(), price=None):
    def body(*refs):
        kernel(*refs[: 1 + len(inputs)], *refs[1 + len(inputs) + len(behind) :])

    return pl.pallas_call(
        body,
        in_specs=whole(1, pltpu.SMEM) + whole(len(inputs)) + whole(len(behind), pl.ANY),
        out_specs=whole(len(outs)),
        out_shape=[pltpu.VMEM(shape, dtype) for shape, dtype in outs],
        compiler_params=pltpu.CompilerParams(vmem_limit_bytes=VMEM_SMALL),
        cost_estimate=price,
    )(in_scalars(flags), *[near_by(value) for value in inputs], *behind)


def cost(count, rows, products):
    return pl.CostEstimate(
        flops=4 * products * count * rows * GROUP * rows * WIDTH,
        bytes_accessed=1,
        transcendentals=0,
    )


def large(kernel, inputs, outs, price, behind=()):
    def body(*refs):
        kernel(*refs[: len(inputs)], *refs[len(inputs) + len(behind) :])

    return pl.pallas_call(
        body,
        in_specs=whole(len(inputs)) + whole(len(behind), pl.ANY),
        out_specs=whole(len(outs)),
        out_shape=[pltpu.VMEM(shape, dtype) for shape, dtype in outs],
        compiler_params=pltpu.CompilerParams(vmem_limit_bytes=VMEM_LARGE),
        cost_estimate=price,
    )(*[near_by(value) for value in inputs], *behind)


def far(value):
    return pltpu.with_memory_space_constraint(value, pltpu.HBM)


def first_step(contexts, subs, count, arrays, spans, docs, behind):
    rows = arrays[0].shape[0]
    heads = arrays[2].shape[1] // WIDTH

    def kernel(*refs):
        first_kernel(contexts, count, *refs[:6], *refs[7:])

    results = pl.pallas_call(
        kernel,
        in_specs=whole(7, pl.ANY),
        out_specs=whole(4) + whole(1, pltpu.SMEM) + whole(2),
        out_shape=[pltpu.VMEM(array.shape, array.dtype) for array in arrays]
        + [
            pltpu.SMEM((6,), jnp.int32),
            pltpu.VMEM(((subs + 1) * rows, rows), jnp.float32),
            pltpu.VMEM((count, 8, GROUP * rows), jnp.float32),
        ],
        scratch_shapes=[
            pltpu.SemaphoreType.DMA((4, heads)),
            pltpu.SMEM(spans.shape, jnp.int32),
            pltpu.SMEM(docs.shape, jnp.int32),
        ],
        compiler_params=pltpu.CompilerParams(vmem_limit_bytes=VMEM_LARGE),
        cost_estimate=cost(count, rows, 3),
    )(*[far(array) for array in (*arrays, spans, docs)], behind)
    return results[4], results[:2], results[2:4], results[5], results[6]


def more_sums(wide, own, bias, start, count, behind=()):
    rows = wide[0].shape[0]
    kernel = functools.partial(sums_kernel, start, count)
    outs = [((count, 8, GROUP * rows), jnp.float32)]
    return large(kernel, [*wide, *own, bias], outs, cost(count, rows, 2), behind)[0]


def earlier_terms(queries, dout, bias, before, near, stats, start, behind=()):
    rows = queries.shape[0]
    units = len(near) + 1
    count = before[0].shape[1] // WIDTH
    wide = (count, units * rows, GROUP * rows)
    outs = [
        ((count, GROUP, rows), jnp.float32),
        ((count, 8, GROUP * rows), jnp.float32),
        (wide, jnp.bfloat16),
        (wide, jnp.bfloat16),
    ] + [((rows, count * WIDTH), jnp.bfloat16)] * (2 * units)
    kernel = functools.partial(earlier_kernel, start, count, len(near))
    inputs = [queries, dout, bias, *before, *near, stats]
    results = large(kernel, inputs, outs, cost(count, rows, 4 * units), behind)
    return results[0], results[1:4], results[4 : 4 + units], results[4 + units :]


def the_rest(queries, dout, bias, before, near, own, kept, start, spots, earlier, behind=()):
    rows = queries.shape[0]
    skip, count, per = spots
    block = pl.BlockSpec((rows, per * GROUP * WIDTH), lambda g: (0, (start + skip) // per + g))
    inputs = [near_by(v) for v in (queries, dout, bias, *before, *near, *own, *kept)]
    extra = [*earlier, *behind]

    def kernel(*refs):
        refs = refs[: len(inputs)] + refs[len(inputs) + len(extra) :]
        rest_kernel(start, skip, per, len(near), *refs)

    wide = jax.ShapeDtypeStruct(queries.shape, jnp.bfloat16)
    results = pl.pallas_call(
        kernel,
        grid=(count // per,),
        in_specs=whole(len(inputs)) + whole(len(extra), pl.ANY),
        out_specs=[block, block] + whole(2),
        out_shape=[wide, wide] + [pltpu.VMEM((rows, count * WIDTH), jnp.float32)] * 2,
        input_output_aliases={len(inputs): 0, len(inputs) + 1: 1} if earlier else {},
        compiler_params=pltpu.CompilerParams(vmem_limit_bytes=VMEM_LARGE),
        cost_estimate=cost(count, rows, 5),
    )(*inputs, *extra)
    return results[:2], results[2:]


def route(flag, first, second, one, two):
    @pl.when(flag != 0)
    def _():
        one[...] = first[...]
        two[...] = second[...]

    @pl.when(flag == 0)
    def _():
        one[...] = second[...]
        two[...] = first[...]


def body(queries, keys, values, dout, doc_lengths, span_order):
    rows = queries.shape[0]
    size = lax.axis_size("head")
    subs = size // 2
    contexts = lax.axis_size(CONTEXT)
    width = keys.shape[1] // CHUNKS
    half = ((rows, width), jnp.bfloat16)

    def across(value):
        return lax.ppermute(value, "head", [(j, (j + subs) % size) for j in range(size)])

    def around(value, steps):
        pairs = [(j, j // subs * subs + (j + steps) % subs) for j in range(size)]
        return lax.ppermute(value, "head", pairs)

    def edges(value, start):
        pairs = [(c, c + 1) for c in range(start, contexts - 1, 2)]
        return lax.ppermute(value, CONTEXT, pairs + [(b, a) for a, b in pairs])

    def columns(chunk):
        return slice(chunk * width, (chunk + 1) * width)

    def pick_in(keys, values, give, sem):
        for flag, source in ((0, values), (1, keys)):

            @pl.when(lax.axis_index("head") // subs == flag)
            def _(source=source):
                copy = pltpu.make_async_copy(source.at[:, columns(0)], give, sem)
                copy.start()
                copy.wait()

    first_give = pl.pallas_call(
        pick_in,
        in_specs=whole(2, pl.ANY),
        out_specs=whole(1)[0],
        out_shape=pltpu.VMEM(*half),
        scratch_shapes=[pltpu.SemaphoreType.DMA],
        compiler_params=pltpu.CompilerParams(vmem_limit_bytes=VMEM_SMALL),
    )(far(keys), far(values))

    def later_give(own, chunk, behind):
        def kernel(flag, key, value, give):
            for which, source in ((0, value), (1, key)):

                @pl.when(flag[1] == which)
                def _(source=source):
                    give[...] = source[:, columns(chunk)]

        return small(kernel, flags, own, [half], behind)[0]

    def out_of_step(flag, backward):
        return (flag[3] + flag[4] + (1 if backward else 0)) % 2

    def edge_part(own, got, backward, odd, cols=slice(None), behind=(), price=None):
        def kernel(flag, *refs):
            own, (got, out) = refs[:-2], refs[-2:]
            keeps = out_of_step(flag, backward) != odd
            for which, keep in enumerate(own):

                @pl.when(keeps & ((flag[1] == which) | (len(own) == 1)))
                def _(keep=keep):
                    out[...] = keep[:, cols]

            @pl.when(jnp.logical_not(keeps))
            def _():
                out[...] = got[:rows, :]

        return small(kernel, flags, [*own, got], [half], behind, price)[0]

    def edge_done(own, got, even, odd, backward, cols=slice(None), behind=()):
        def kernel(flag, *refs):
            own, (got, even, odd, mine, theirs) = refs[:-5], refs[-5:]
            takes_odd = (flag[3] + flag[4]) % 2
            if backward:
                takes_odd = 1 - takes_odd

            @pl.when(flag[5] == 0)
            def _():
                route(takes_odd, odd, even, mine, theirs)

            kept = (flag[3] + (1 if backward else 0)) % 2
            for which, keep in enumerate(own):

                @pl.when((flag[5] != 0) & (kept != 0) & ((flag[1] == which) | (len(own) == 1)))
                def _(keep=keep):
                    route(takes_odd, keep.at[:, cols], even, mine, theirs)

            @pl.when((flag[5] != 0) & (kept == 0))
            def _():
                route(takes_odd, got.at[:rows], even, mine, theirs)

        return small(kernel, flags, [*own, got, even, odd], [half, half], behind)

    def window_parts(own, mine, other, cols, behind=()):
        def kernel(flag, own_key, own_value, mine, other, key, value, *sent):
            route(flag[1], other, mine, key, value)
            for index, out in enumerate(sent):
                inside = flag[2] + (subs - 1 - index) < subs

                @pl.when(inside)
                def _():
                    out[:, :width] = own_key[:, cols]
                    out[:, width:] = own_value[:, cols]

                @pl.when(jnp.logical_not(inside))
                def _():
                    out[:, :width] = key[...]
                    out[:, width:] = value[...]

        both = ((rows, 2 * width), jnp.bfloat16)
        outs = small(kernel, flags, [*own, mine, other], [half, half] + [both] * (subs - 1), behind)
        return outs[:2], [around(out, subs - 1 - i) for i, out in enumerate(outs[2:])]

    per_device = KEY_VALUE_HEADS // size

    def two_parts(out, lo, block):
        block = block.reshape(-1, rows)
        if block.shape[0] < EXTRA:
            fill = jnp.zeros((EXTRA - block.shape[0], rows), jnp.float32)
            block = jnp.concatenate([block, fill], axis=0)
        high = block.astype(jnp.bfloat16)
        out[rows:, lo : lo + rows] = high
        lo += rows
        out[rows:, lo : lo + rows] = (block - high.astype(jnp.float32)).astype(jnp.bfloat16)

    def one_part(ref, lo):
        high, low = ref[rows:, lo : lo + rows], ref[rows:, lo + rows : lo + 2 * rows]
        return high.astype(jnp.float32) + low.astype(jnp.float32)

    def near_terms(dk, dv, entropies=(), behind=()):
        extra = EXTRA if entropies else 0

        def kernel(flag, *refs):
            ents, refs = refs[: len(entropies)], refs[len(entropies) :]
            for index in range(subs - 1):
                out = refs[2 * (subs - 1) + index]
                out[:rows, :width] = refs[index][...]
                out[:rows, width:] = refs[subs - 1 + index][...]
                to = lax.rem(flag[2] + index + 1, subs)
                for which, ent in enumerate(ents):
                    two_parts(out, 2 * which * rows, ent[pl.ds(to * per_device, per_device)])

        both = ((rows + extra, 2 * width), jnp.bfloat16)
        outs = small(kernel, flags, [*entropies, *dk[1:], *dv[1:]], [both] * (subs - 1), behind)
        return [around(out, index + 1 - subs) for index, out in enumerate(outs)], outs

    def collect(dk, dv, arrived, entropies=(), behind=()):
        extra = EXTRA if entropies else 0

        def kernel(flag, dk, dv, *refs):
            ents, refs = refs[: len(entropies)], refs[len(entropies) :]
            got = refs[: subs - 1]
            keep, give, own_key, own_value = refs[subs - 1 : subs + 3]
            for which, term, own in ((0, dk, own_key), (1, dv, own_value)):
                before = term[...].astype(jnp.float32)
                mine = jnp.zeros_like(before)
                for index, ref in enumerate(got):
                    part = ref[:rows, which * width : (which + 1) * width].astype(jnp.float32)
                    within = flag[2] + (subs - 1 - index) < subs
                    mine = mine + jnp.where(within, part, 0.0)
                    before = before + jnp.where(within, 0.0, part)
                own[...] = mine
                before = before.astype(jnp.bfloat16)

                @pl.when(flag[1] == which)
                def _():
                    keep[...] = before

                @pl.when(flag[1] != which)
                def _():
                    give[:rows, :] = before

            for which, ent in enumerate(ents):
                block = ent[pl.ds(flag[2] * per_device, per_device)]
                blocks = [block.reshape(-1, rows)]
                blocks += [one_part(ref, 2 * which * rows)[: blocks[0].shape[0]] for ref in got]

                @pl.when(flag[1] == which)
                def _(blocks=blocks):
                    for index, block in enumerate(blocks):
                        refs[subs + 3][index] = block

                @pl.when(flag[1] != which)
                def _(blocks=blocks):
                    for index, block in enumerate(blocks):
                        two_parts(give, 2 * index * rows, block)

        full = ((rows, width), jnp.float32)
        outs = [half, ((rows + extra, width), jnp.bfloat16), full, full]
        if entropies:
            outs.append(((subs, per_device * GROUP, rows), jnp.float32))
        return small(kernel, flags, [dk[0], dv[0], *entropies, *arrived], outs, behind)

    def finish(chunks, entropies, got):
        local, plans = [entropies, got], []
        for chunk, (own_key, own_value, pieces, mine, other) in enumerate(chunks):
            spot = 0
            for dk, dv in pieces:
                cols = slice(spot, spot + dk.shape[1])
                plans.append((len(local), cols, slice(cols.start + chunk * width, cols.stop + chunk * width)))
                local += [own_key, own_value, mine, other, dk, dv]
                spot = cols.stop
        count = per_device * GROUP

        def kernel(flag, *refs):
            ent, got = refs[:2]
            out_key, out_value, out_ent = refs[-3:]
            is_key = flag[1] == 0
            for at, cols, to in plans:
                own_key, own_value, mine, other, dk, dv = refs[at : at + 6]
                here = mine[:, cols].astype(jnp.float32)
                there = other[:, cols].astype(jnp.float32)
                for out, own, term, back in (
                    (out_key, own_key, dk, jnp.where(is_key, here, there)),
                    (out_value, own_value, dv, jnp.where(is_key, there, here)),
                ):
                    out[:, to] = (own[:, cols] + term[...] + back).astype(jnp.bfloat16)
            for index in range(subs):
                steps = 0 if index == 0 else subs - index
                source = lax.rem(flag[2] + steps, subs)
                for way, block in ((flag[1], ent[index]), (1 - flag[1], one_part(got, 2 * index * rows))):
                    for spot in range(size):

                        @pl.when(way * subs + source == spot)
                        def _(spot=spot, block=block):
                            out_ent[:, spot * rows : (spot + 1) * rows] = block[:count]

        return pl.pallas_call(
            kernel,
            grid=(1,),
            in_specs=whole(1, pltpu.SMEM) + whole(len(local)),
            out_specs=[pl.BlockSpec(keys.shape, lambda g: (0, 0))] * 2
            + [pl.BlockSpec((count, size * rows), lambda g: (0, 0))],
            out_shape=[jax.ShapeDtypeStruct(keys.shape, jnp.bfloat16)] * 2
            + [jax.ShapeDtypeStruct((count, size * rows), jnp.float32)],
            compiler_params=pltpu.CompilerParams(vmem_limit_bytes=VMEM_SMALL),
        )(in_scalars(flags), *[near_by(v) for v in local])

    def taken(value, behind=(), price=None):
        def kernel(flag, value, out):
            out[...] = value[...]

        return small(kernel, flags, [value], [half], behind, price)[0]

    per_chunk = KEY_VALUE_HEADS // CHUNKS
    got = [across(first_give)]
    flags, wide_near, own, bias, stats = first_step(
        contexts, subs, per_chunk, (queries, dout, keys, values), span_order, doc_lengths, first_give
    )
    got.append(across(later_give(own, 1, got)))
    cols = [columns(chunk) for chunk in range(CHUNKS)]
    in0 = [edge_part(own, got[0], False, odd, cols[0], [stats]) for odd in range(2)]
    edge0 = [edges(part, odd) for odd, part in enumerate(in0)]
    in1 = [edge_part(own, got[1], False, odd, cols[1]) for odd in range(2)]
    edge1 = [edges(part, odd) for odd, part in enumerate(in1)]
    mine0, theirs0 = edge_done(own, got[0], *edge0, False, cols[0])
    other0 = across(theirs0)
    stats = [stats, more_sums(wide_near, own, bias, per_chunk, per_chunk, [theirs0])]
    edge1[1] = taken(taken(edge1[1], [theirs0]), price=cost(4, rows, 10))
    mine1, theirs1 = edge_done(own, got[1], *edge1, False, cols[1], [theirs0])
    other1 = across(theirs1)
    before0, near0 = window_parts(own, mine0, other0, cols[0], [theirs1, stats[1]])
    ent0, kept0, dk0, dv0 = earlier_terms(*wide_near, bias, before0, near0, stats[0], 0)
    before1, near1 = window_parts(own, mine1, other1, cols[1], [ent0])
    wide, pieces = [], []

    def rest(chunk, piece, behind):
        nonlocal wide
        before, near, kept = held[chunk]
        start = chunk * per_chunk
        wide, terms = the_rest(
            *wide_near, bias, before, near, own, kept, start, BEHIND[chunk][piece], wide, behind
        )
        pieces.append(terms)
        return terms[:1]

    held = [(before0, near0, kept0), (before1, near1, None)]
    arrived, sent = near_terms(dk0, dv0)
    keep0, give0, *own0 = collect(dk0, dv0, arrived)
    back0 = across(give0)
    ent1, kept1, dk1, dv1 = earlier_terms(
        *wide_near, bias, before1, near1, stats[1], per_chunk, [give0]
    )
    held[1] = (before1, near1, kept1)
    out0 = edge_part([keep0], back0, True, 0)
    edge0 = [edges(out0, 0)]
    ents = [ent0, ent1]
    arrived, sent = near_terms(dk1, dv1, ents, [out0])
    keep1, give1, *own1, entropies = collect(dk1, dv1, arrived, ents)
    back1 = across(give1)
    edge0.append(edges(edge_part([keep0], back0, True, 1, behind=[give1], price=cost(4, rows, 10)), 1))
    out1 = [edge_part([keep1], back1, True, odd) for odd in range(2)]
    edge1 = [edges(part, odd) for odd, part in enumerate(out1)]
    mine0, theirs0 = edge_done([keep0], back0, *edge0, True, behind=out1[:1])
    other0 = across(theirs0)
    done = rest(0, 0, [theirs0])
    edge1[0] = taken(taken(edge1[0], done), price=cost(4, rows, 10))
    mine1, theirs1 = edge_done([keep1], back1, *edge1, True, behind=done)
    other1 = across(theirs1)
    rest(1, 0, [theirs1])
    grad_key, grad_value, entropy = finish(
        [(*own0, pieces[:1], mine0, other0), (*own1, pieces[1:], mine1, other1)], entropies, back1
    )
    return wide[0], entropy.T, wide[1], grad_key, grad_value


def solution(mesh):
    rows = P(("inner", "outer", "head"), None)
    return jax.shard_map(
        body,
        mesh=mesh,
        in_specs=(rows, rows, rows, rows, P(), P()),
        out_specs=(rows, P(("inner", "outer"), "head"), rows, rows, rows),
        check_vma=False,
    )
```
